128 devices in a mesh: slab: 32 (over y, z, core), cross: 4 (over x).
Axes of the slice: x: 4, y: 4, z: 4, core: 2. Of those that a mesh axis runs over, the one named last changes fastest.
Arguments:
- pressure_drive: float32 [3, 256, 256, 512], P(None, 'slab', 'cross'), may hold values from -23 to 23
- throat_radius: float32 [3, 256, 256, 512], P(None, 'slab', 'cross'), may hold values from 0.5 to 1.5
- wet_flag: int32 [3, 256, 256, 512], P(None, 'slab', 'cross'), may hold values 0 or 1
- cap_pressure: float32 [256, 256, 512], P('slab', 'cross'), may hold values from 1 to 3
- storage: float32 [256, 256, 512], P('slab', 'cross'), may hold values from 0.05 to 0.5
Outputs:
- solution: float32 [3, 256, 256, 512], P(None, 'slab', 'cross')
- residual: float32 [3, 256, 256, 512], P(None, 'slab', 'cross')
The draws below stay inside these ranges and needn't reach their ends.
All inputs are finite; a program needn't handle non-finite values. No bound on the sum of `wet_flag` on one device may be relied on, other than what follows from the above.
Results may differ from the reference program's by a relative error of at most 0.0003.
Values sent between devices are 32-bit elements; how exact they have to be, the bound alone decides.
A program may use at most 128 MiB of HBM per device.

```python
import math
import jax
import jax.numpy as jnp
from jax import lax

NC = 512
RHS = 3
ITERS = 3
NA = 256
NB = 256


def draw_pressure_drive(key, part):
    key = jax.random.fold_in(key, 7)
    key_values = jax.random.fold_in(key, 1)
    key_scale = jax.random.fold_in(key, 2)
    column = jnp.exp(jax.random.uniform(key_scale, (RHS, NA, NB, 1), jnp.float32, -1.0, 1.0) * (0.5 * math.log(10.0)))
    slope_scale = 0.5 + jnp.arange(NA, dtype=jnp.float32) / (NA - 1.0)
    values = jnp.clip(jax.random.normal(key_values, (RHS, NA, NB, NC), jnp.float32), -5.0, 5.0)
    return values * column * slope_scale[None, :, None, None]


def with_ends(entries, stream_key, low, largest):
    dims = entries.shape
    place = [jax.random.randint(jax.random.fold_in(stream_key, axis), (), 0, dims[axis]) for axis in range(len(dims))]
    entries = entries.at[tuple(place)].set(low)
    longest = dims.index(max(dims))
    place[longest] = (place[longest] + 1) % dims[longest]
    return entries.at[tuple(place)].set(largest)


def level_of(own_key, dims, shards, smallest, largest):
    gain = 1.0
    for position, blocks in shards:
        steps = jax.random.uniform(jax.random.fold_in(jax.random.fold_in(own_key, 6), position), (blocks,), jnp.float32, smallest / len(shards), largest / len(shards))
        gain = gain * jnp.repeat(jnp.exp(steps), dims[position] // blocks).reshape((-1,) + (1,) * (len(dims) - 1 - position))
    return gain


def setup_inputs(seed: int = 0) -> dict:
    streams_of = jax.random.split(jax.random.key(seed), 6)
    pressure_drive = draw_pressure_drive(jax.random.fold_in(streams_of[5], 71), 0)
    throat_radius = jnp.clip(jnp.exp(math.log(1.5) - 1.0986123 * jax.random.uniform(streams_of[1], (3, NA, NB, NC), jnp.float32) ** level_of(streams_of[1], (3, NA, NB, NC), ((1, 32), (2, 4)), -0.2, 0.2)), 0.5, 1.5)
    wet_flag = with_ends((jax.random.randint(streams_of[2], (3, NA, NB, NC), 0, 2) < 1).astype(jnp.int32), jax.random.fold_in(streams_of[2], 1), 0, 1)
    cap_pressure = jnp.clip(jnp.exp(math.log(3.0) - 1.0986123 * jax.random.uniform(streams_of[3], (NA, NB, NC), jnp.float32) ** level_of(streams_of[3], (NA, NB, NC), ((0, 32), (1, 4)), -0.2, 0.2)), 1.0, 3.0)
    storage = jnp.clip(jnp.exp(math.log(0.5) - 2.3025851 * jax.random.uniform(streams_of[4], (NA, NB, NC), jnp.float32) ** level_of(streams_of[4], (NA, NB, NC), ((0, 32), (1, 4)), -0.2, 0.2)), 0.05, 0.5)
    return dict(pressure_drive=pressure_drive, throat_radius=throat_radius, wet_flag=wet_flag, cap_pressure=cap_pressure, storage=storage)


def conductances(throat_radius, wet_flag, cap_pressure):
    squared = throat_radius * throat_radius
    film_term = 0.4 * squared / (cap_pressure * cap_pressure)[None]
    conduct = jnp.where(wet_flag == 1, squared * squared, film_term)
    along_slab = conduct[0].at[-1, :, :].set(0.0)
    along_cross = conduct[1].at[:, -1, :].set(0.0)
    along_depth = conduct[2].at[:, :, -1].set(0.0)
    return along_slab, along_cross, along_depth


def operate(vector, along_slab, along_cross, along_depth, storage):
    padded = jnp.pad(vector, 1)
    below_slab = jnp.pad(along_slab, ((1, 0), (0, 0), (0, 0)))[:-1]
    below_cross = jnp.pad(along_cross, ((0, 0), (1, 0), (0, 0)))[:, :-1]
    below_depth = jnp.pad(along_depth, ((0, 0), (0, 0), (1, 0)))[:, :, :-1]
    result = storage * vector
    result = result + along_slab * (vector - padded[2:, 1:-1, 1:-1])
    result = result + below_slab * (vector - padded[:-2, 1:-1, 1:-1])
    result = result + along_cross * (vector - padded[1:-1, 2:, 1:-1])
    result = result + below_cross * (vector - padded[1:-1, :-2, 1:-1])
    result = result + along_depth * (vector - padded[1:-1, 1:-1, 2:])
    result = result + below_depth * (vector - padded[1:-1, 1:-1, :-2])
    return result


def reference(pressure_drive, throat_radius, wet_flag, cap_pressure, storage):
    along_slab, along_cross, along_depth = conductances(throat_radius, wet_flag, cap_pressure)

    def solve_one(source):
        solution = jnp.zeros_like(source)
        residual = source
        direction = source
        norm_now = jnp.sum(residual * residual)
        for iteration in range(ITERS):
            applied = operate(direction, along_slab, along_cross, along_depth, storage)
            step_size = norm_now / jnp.sum(direction * applied)
            solution = solution + step_size * direction
            residual = residual - step_size * applied
            norm_next = jnp.sum(residual * residual)
            direction = residual + (norm_next / norm_now) * direction
            norm_now = norm_next
        return solution, residual

    solution, residual = lax.map(solve_one, pressure_drive)
    return solution, residual
```

```python
import functools

import jax
import jax.numpy as jnp
from jax import lax
from jax.experimental import pallas as pl
from jax.experimental.pallas import tpu as pltpu
from jax.sharding import PartitionSpec as P

ITERS = 3
RHS = 3
F32 = jnp.float32
MESH = pl.DeviceIdType.MESH
SLABS, CROSSES = 32, 4
LA, LB, NC = 8, 64, 512
TILES = LB // 8
ERROR_GAIN_MAX = 2500.0
CANCEL_MAX = 300.0


def shifted(value, axis, steps):
    count = lax.axis_size(axis)
    leading, last = (max(0, -steps), min(count, count - steps))
    return lax.ppermute(value, axis, [(source, source + steps) for source in range(leading, last)])


def with_halo(cells, sides, width):
    for axis, dim in sides:
        count = lax.axis_size(axis)
        ends = count - 1
        head = lax.slice_in_dim(cells, 0, width, axis=dim)
        tail = lax.slice_in_dim(cells, cells.shape[dim] - width, cells.shape[dim], axis=dim)
        cells = jnp.concatenate(
            [
                lax.ppermute(tail, axis, [(i, (i + 1) % count) for i in range(ends)]),
                cells,
                lax.ppermute(head, axis, [((i + 1) % count, i) for i in range(ends)]),
            ],
            axis=dim,
        )
    return cells


def totals(values):
    return jnp.sum(values, axis=(1, 2, 3))


def widen(scalars):
    return scalars[:, None, None, None]


def squares(residual):
    return lax.psum(totals(residual * residual), ("slab", "cross"))


def depth_terms(vector, along_depth, lower_depth):
    upper_values = jnp.pad(vector[..., 1:], ((0, 0), (0, 0), (0, 0), (0, 1)))
    lower_values = jnp.pad(vector[..., :-1], ((0, 0), (0, 0), (0, 0), (1, 0)))
    return along_depth * (vector - upper_values) + lower_depth * (vector - lower_values)


def plain_iteration(pressure_drive, throat_radius, wet_flag, cap_pressure, storage):
    squared = throat_radius * throat_radius
    film_term = 0.4 * squared / (cap_pressure * cap_pressure)[None]
    conduct = jnp.where(wet_flag == 1, squared * squared, film_term)
    extent = conduct.shape[1:]
    layer_slab = lax.broadcasted_iota(jnp.int32, extent, 0)
    layer_cross = lax.broadcasted_iota(jnp.int32, extent, 1)
    layer_depth = lax.broadcasted_iota(jnp.int32, extent, 2)
    edge_slab = (layer_slab == extent[0] - 1) & (
        lax.axis_index("slab") == lax.axis_size("slab") - 1
    )
    edge_cross = (layer_cross == extent[1] - 1) & (
        lax.axis_index("cross") == lax.axis_size("cross") - 1
    )
    along_slab = jnp.where(edge_slab, 0.0, conduct[0])
    along_cross = jnp.where(edge_cross, 0.0, conduct[1])
    along_depth = jnp.where(layer_depth == extent[2] - 1, 0.0, conduct[2])
    lower_depth = jnp.pad(along_depth[:, :, :-1], ((0, 0), (0, 0), (1, 0)))
    rim_slab = shifted(along_slab[-1:], "slab", 1)
    rim_cross = shifted(along_cross[:, -1:], "cross", 1)
    lower_slab = jnp.concatenate([rim_slab, along_slab[:-1]], 0)
    lower_cross = jnp.concatenate([rim_cross, along_cross[:, :-1]], 1)
    solution = jnp.zeros_like(pressure_drive)
    residual = pressure_drive
    direction = pressure_drive
    norm_now = squares(residual)
    for iteration in range(ITERS):
        padded = with_halo(direction, (("slab", 1), ("cross", 2)), 1)
        result = storage * direction
        result = result + along_slab * (direction - padded[:, 2:, 1:-1])
        result = result + lower_slab * (direction - padded[:, :-2, 1:-1])
        result = result + along_cross * (direction - padded[:, 1:-1, 2:])
        result = result + lower_cross * (direction - padded[:, 1:-1, :-2])
        applied = result + depth_terms(direction, along_depth, lower_depth)
        step_size = norm_now / lax.psum(totals(direction * applied), ("slab", "cross"))
        solution = solution + widen(step_size) * direction
        residual = residual - widen(step_size) * applied
        if iteration + 1 < ITERS:
            norm_next = squares(residual)
            direction = residual + widen(norm_next / norm_now) * direction
            norm_now = norm_next
    return (solution, residual)


def scalars_of(m):
    def parts(c0, c1, c2, first):
        return (
            c0 * c0 * m[first],
            2.0 * c0 * c1 * m[first + 1],
            c1 * c1 * m[first + 2],
            2.0 * c0 * c2 * m[first + 2],
            2.0 * c1 * c2 * m[first + 3],
            c2 * c2 * m[first + 4],
        )

    def total(terms):
        return (terms[0] + terms[1]) + (terms[2] + terms[3]) + (terms[4] + terms[5])

    def bulk(terms):
        return total([jnp.abs(term) for term in terms])

    rr0 = m[0]
    step0 = m[0] / m[1]
    image0 = step0 * step0 * m[2]
    rr1 = image0 - rr0
    turn0 = rr1 / rr0
    p0, p1 = 1.0 + turn0, -step0

    def pair(first):
        return p0 * p0 * m[first], 2.0 * p0 * p1 * m[first + 1], p1 * p1 * m[first + 2]

    energy1 = pair(1)
    curve1 = energy1[0] + energy1[1] + energy1[2]
    step1 = rr1 / curve1
    image1 = pair(2)
    rr2 = step1 * step1 * (image1[0] + image1[1] + image1[2]) - rr1
    turn1 = rr2 / rr1
    r1, r2 = -step0 - step1 * p0, -step1 * p1
    q0, q1, q2 = 1.0 + turn1 * p0, r1 + turn1 * p1, r2
    energy2 = parts(q0, q1, q2, 1)
    curve2 = total(energy2)
    step2 = rr2 / curve2
    x0 = step0 + step1 * p0 + step2 * q0
    x1 = step1 * p1 + step2 * q1
    x2 = step2 * q2
    d1, d2, d3 = r1 - step2 * q0, r2 - step2 * q1, -step2 * q2

    image2 = parts(q0, q1, q2, 2)
    rr3 = step2 * step2 * total(image2) - rr2
    gain1 = (image0 + rr0) / rr1
    gain2 = (energy1[0] + jnp.abs(energy1[1]) + energy1[2]) / curve1
    gain3 = (step1 * step1 * (image1[0] + jnp.abs(image1[1]) + image1[2]) + rr1) / rr2
    gain4 = bulk(energy2) / curve2
    gain5 = (step2 * step2 * bulk(image2) + rr2) / rr3
    gain = (
        (gain1 + gain2) * jnp.sqrt(rr0 / rr3)
        + gain3 * jnp.sqrt(rr1 / rr3)
        + gain4 * jnp.sqrt(rr2 / rr3)
        + gain5
    )
    cancel = (
        jnp.sqrt(m[0])
        + jnp.abs(d1) * jnp.sqrt(m[2])
        + jnp.abs(d2) * jnp.sqrt(m[4])
        + jnp.abs(d3) * jnp.sqrt(m[6])
    ) / jnp.sqrt(rr3)
    sound = (
        (rr1 > 0.0)
        & (curve1 > 0.0)
        & (rr2 > 0.0)
        & (curve2 > 0.0)
        & (rr3 > 0.0)
        & (gain < ERROR_GAIN_MAX)
        & (cancel < CANCEL_MAX)
    )
    return (x0, x1, x2, d1, d2, d3), sound


def fold(value):
    return (value[:, 0:128] + value[:, 128:256]) + (value[:, 256:384] + value[:, 384:512])


def powers_kernel(
    b_hbm, rad_hbm, wet_hbm, cap_hbm, sto_hbm,
    v0, v1, v2, v3, coef_ref, sound_ref,
    cond, wet, cap, sto, cs_low, cc_out, cc_low,
    halo_low, halo_up, edge_low, edge_up, rim_low, rim_up,
    flux, moments, sent1, sent2, got1, got2,
    load_sem, halo_send, halo_recv, cond_send, cond_recv, sum_send, sum_recv,
):
    s, c = lax.axis_index("slab"), lax.axis_index("cross")
    up, down = lax.rem(s + 1, SLABS), lax.rem(s + SLABS - 1, SLABS)
    right, left = lax.rem(c + 1, CROSSES), lax.rem(c + CROSSES - 1, CROSSES)
    row_y, in_row = s // 8, lax.rem(s, 8)
    group1 = [(row_y * 8 + lax.rem(in_row + i, 8), c) for i in range(1, 8)]
    group2 = [
        (lax.rem(row_y + i, 4) * 8 + in_row, lax.rem(c + j, 4))
        for i in range(4)
        for j in range(4)
        if i or j
    ]
    barrier = pltpu.get_barrier_semaphore()
    greeted = [(up, c), (down, c), (s, right), (s, left)] + group1 + group2
    for peer in greeted:
        pl.semaphore_signal(barrier, inc=1, device_id=peer, device_id_type=MESH)

    loads = [
        pltpu.make_async_copy(rad_hbm, cond, load_sem.at[0]),
        pltpu.make_async_copy(wet_hbm, wet, load_sem.at[1]),
        pltpu.make_async_copy(cap_hbm, cap, load_sem.at[2]),
        pltpu.make_async_copy(b_hbm, v0, load_sem.at[3]),
        pltpu.make_async_copy(sto_hbm, sto, load_sem.at[4]),
    ]
    for load in loads:
        load.start()
    for load in loads[:3]:
        load.wait()

    row = lax.broadcasted_iota(jnp.int32, (8, NC), 0)
    lane = lax.broadcasted_iota(jnp.int32, (8, NC), 1)
    first_row, last_row, last_lane = row == 0, row == 7, lane == NC - 1

    def conduct(a, carry):
        ends_slab = (s == SLABS - 1) & (a == LA - 1)
        for j in range(TILES):
            at = pl.ds(8 * j, 8)
            pressure = cap[a, at, :]
            film = 0.4 / (pressure * pressure)
            for k in range(3):
                radius = cond[k, a, at, :]
                squared = radius * radius
                value = squared * jnp.where(wet[k, a, at, :] == 1, squared, film)
                if k == 0:
                    value = jnp.where(ends_slab, 0.0, value)
                if k == 1 and j == TILES - 1:
                    value = jnp.where(last_row & (c == CROSSES - 1), 0.0, value)
                    cc_out[a] = value[7:8, :]
                if k == 2:
                    value = jnp.where(last_lane, 0.0, value)
                cond[k, a, at, :] = value
        return carry

    lax.fori_loop(0, LA, conduct, 0)

    loads[3].wait()
    for q in range(RHS):
        for a in range(LA):
            edge_low[0, q, a] = v0[q, a, 0:1, :]
            edge_up[0, q, a] = v0[q, a, LB - 1 : LB, :]
    loads[4].wait()
    moments[...] = jnp.zeros_like(moments)
    pl.semaphore_wait(barrier, len(greeted))

    vectors = (v0, v1, v2, v3)

    def halo_copies(k, q):
        v = vectors[k]
        return (
            pltpu.make_async_remote_copy(
                src_ref=v.at[q, 0], dst_ref=halo_up.at[k, q], send_sem=halo_send.at[k, q, 0],
                recv_sem=halo_recv.at[k, q, 0], device_id=(down, c), device_id_type=MESH),
            pltpu.make_async_remote_copy(
                src_ref=v.at[q, LA - 1], dst_ref=halo_low.at[k, q], send_sem=halo_send.at[k, q, 1],
                recv_sem=halo_recv.at[k, q, 1], device_id=(up, c), device_id_type=MESH),
            pltpu.make_async_remote_copy(
                src_ref=edge_low.at[k, q], dst_ref=rim_up.at[k, q], send_sem=halo_send.at[k, q, 2],
                recv_sem=halo_recv.at[k, q, 2], device_id=(s, left), device_id_type=MESH),
            pltpu.make_async_remote_copy(
                src_ref=edge_up.at[k, q], dst_ref=rim_low.at[k, q], send_sem=halo_send.at[k, q, 3],
                recv_sem=halo_recv.at[k, q, 3], device_id=(s, right), device_id_type=MESH),
        )

    cond_copies = (
        pltpu.make_async_remote_copy(
            src_ref=cond.at[0, LA - 1], dst_ref=cs_low, send_sem=cond_send.at[0],
            recv_sem=cond_recv.at[0], device_id=(up, c), device_id_type=MESH),
        pltpu.make_async_remote_copy(
            src_ref=cc_out, dst_ref=cc_low, send_sem=cond_send.at[1],
            recv_sem=cond_recv.at[1], device_id=(s, right), device_id_type=MESH),
    )
    for q in range(RHS):
        for copy in halo_copies(0, q):
            copy.start()
        if q == 0:
            for copy in cond_copies:
                copy.start()
    for copy in cond_copies:
        copy.wait_recv()

    def spread(line):
        return jnp.broadcast_to(line, (8, NC))

    for k in range(ITERS):
        v, w = vectors[k], vectors[k + 1]

        def layer(q, a, above, carry):
            dots = carry
            here = v[q, a, 0:8, :]
            here_up = pltpu.roll(here, 7, 0)
            passed = spread(cc_low[a]) * (here - spread(rim_low[k, q, a]))
            for j in range(TILES):
                at = pl.ds(8 * j, 8)
                if j + 1 < TILES:
                    after = v[q, a, 8 * j + 8 : 8 * j + 16, :]
                    after_up = pltpu.roll(after, 7, 0)
                else:
                    after = None
                    after_up = spread(rim_up[k, q, a])
                flux_cross = cond[1, a, at, :] * (jnp.where(last_row, after_up, here_up) - here)
                arrived = pltpu.roll(flux_cross, 1, 0)
                flux_depth = cond[2, a, at, :] * (pltpu.roll(here, NC - 1, 1) - here)
                flux_slab = cond[0, a, at, :] * (above(at) - here)
                image = sto[a, at, :] * here
                image = image - flux_slab + flux[at, :]
                image = image - flux_cross + jnp.where(first_row, passed, arrived)
                image = image - flux_depth + pltpu.roll(flux_depth, 1, 1)
                flux[at, :] = flux_slab
                w[q, a, at, :] = image
                if k + 1 < ITERS:
                    if j == 0:
                        edge_low[k + 1, q, a] = image[0:1, :]
                    if j == TILES - 1:
                        edge_up[k + 1, q, a] = image[7:8, :]
                dots = (dots[0] + fold(here * image), dots[1] + fold(image * image)) + (
                    (dots[2] + fold(here * here),) if k == 0 else ()
                )
                passed, here, here_up = arrived, after, after_up
            return dots

        def apply(q, unused):
            for copy in halo_copies(k, q):
                copy.wait_recv()
            for j in range(TILES):
                at = pl.ds(8 * j, 8)
                flux[at, :] = cs_low[at, :] * (v[q, 0, at, :] - halo_low[k, q, at, :])
            dots = (jnp.zeros((8, 128), F32),) * (3 if k == 0 else 2)
            dots = lax.fori_loop(
                0, LA - 1,
                lambda a, carry: layer(q, a, lambda at: v[q, a + 1, at, :], carry),
                dots)
            dots = layer(q, LA - 1, lambda at: halo_up[k, q, at, :], dots)
            if k + 1 < ITERS:
                for copy in halo_copies(k + 1, q):
                    copy.start()
            places = (2 * k + 1, 2 * k + 2, 0)
            for place, dot in zip(places, dots):
                moments[q, place : place + 1, :] = jnp.sum(dot, axis=0, keepdims=True)
            return unused

        lax.fori_loop(0, RHS, apply, 0)

    rows = lax.broadcasted_iota(jnp.int32, (8, 128), 0)
    lanes = lax.broadcasted_iota(jnp.int32, (8, 128), 1)
    packed = jnp.zeros((8, 128), F32)
    for q in range(RHS):
        lane_sum = jnp.sum(moments[q], axis=1, keepdims=True)
        packed = packed + jnp.where(lanes == rows + 8 * q, lane_sum, 0.0)
    own = jnp.sum(packed, axis=0, keepdims=True)

    for sent, got, group, place, index in (
        (sent1, got1, group1, in_row, 0),
        (sent2, got2, group2, row_y * 4 + c, 1),
    ):
        sent[...] = own
        for peer in group:
            pltpu.make_async_remote_copy(
                src_ref=sent, dst_ref=got.at[place], send_sem=sum_send.at[index],
                recv_sem=sum_recv.at[index], device_id=peer, device_id_type=MESH).start()
        got[place] = own
        others = got.at[pl.ds(0, len(group))]
        pltpu.make_async_copy(others, others, sum_recv.at[index]).wait()
        terms = [got[i] for i in range(len(group) + 1)]
        while len(terms) > 1:
            terms = [terms[i] + terms[i + 1] for i in range(0, len(terms), 2)]
        own = terms[0]

    summed = jnp.broadcast_to(own, (8, 128))
    used = (lanes % 8 == 0) & (lanes < 8 * RHS)
    stand_in = (1.0, 1.0, 2.0, 6.0, 24.0, 120.0, 720.0)
    m = [
        jnp.where(used, pltpu.roll(summed, (128 - j) % 128, 1) if j else summed, stand_in[j])
        for j in range(7)
    ]
    coefs, sound = scalars_of(m)
    for i, coef in enumerate(coefs):
        coef_ref[i : i + 1, :] = coef[0:1, :]
    coef_ref[6:8, :] = jnp.zeros((2, 128), F32)
    sound_ref[...] = jnp.min(jnp.where(sound, 1, 0), axis=1, keepdims=True)[0:1, :]

    for copy in cond_copies:
        copy.wait_send()

    def finish(q, unused):
        for k in range(ITERS):
            for copy in halo_copies(k, q):
                copy.wait_send()
        return unused

    lax.fori_loop(0, RHS, finish, 0)
    for got, group, index in ((got1, group1, 0), (got2, group2, 1)):
        others = got.at[pl.ds(0, len(group))]
        pltpu.make_async_copy(others, others, sum_send.at[index]).wait()


def combine_kernel(coef, v0, v1, v2, v3, x_hbm, r_hbm, x, r, sem):
    copies = []
    for q in range(RHS):
        x0, x1, x2, d1, d2, d3 = (coef[i, 8 * q] for i in range(6))

        def layer(a, carry):
            for j in range(TILES):
                at = pl.ds(8 * j, 8)
                t0, t1, t2, t3 = (v[q, a, at, :] for v in (v0, v1, v2, v3))
                x[q, a, at, :] = x0 * t0 + x1 * t1 + x2 * t2
                r[q, a, at, :] = t0 + d1 * t1 + d2 * t2 + d3 * t3
            return carry

        lax.fori_loop(0, LA, layer, 0)
        for index, (source, target) in enumerate(((x, x_hbm), (r, r_hbm))):
            copy = pltpu.make_async_copy(source.at[q], target.at[q], sem.at[q, index])
            copy.start()
            copies.append(copy)
    for copy in copies:
        copy.wait()


def per_device(pressure_drive, throat_radius, wet_flag, cap_pressure, storage):
    field = (RHS, LA, LB, NC)
    vmem = functools.partial(pltpu.VMEM, dtype=F32)
    in_vmem = pl.BlockSpec(memory_space=pltpu.VMEM)
    anywhere = pl.BlockSpec(memory_space=pl.ANY)
    *vectors, coefs, sound = pl.pallas_call(
        powers_kernel,
        out_shape=[pltpu.VMEM(field, F32)] * 4
        + [jax.ShapeDtypeStruct((8, 128), F32), jax.ShapeDtypeStruct((1, 1), jnp.int32)],
        in_specs=[anywhere] * 5,
        out_specs=[in_vmem] * 6,
        scratch_shapes=[
            vmem(field),
            pltpu.VMEM(field, jnp.int32),
            vmem((LA, LB, NC)),
            vmem((LA, LB, NC)),
            vmem((LB, NC)),
            vmem((LA, 1, NC)),
            vmem((LA, 1, NC)),
            vmem((ITERS, RHS, LB, NC)),
            vmem((ITERS, RHS, LB, NC)),
            vmem((ITERS, RHS, LA, 1, NC)),
            vmem((ITERS, RHS, LA, 1, NC)),
            vmem((ITERS, RHS, LA, 1, NC)),
            vmem((ITERS, RHS, LA, 1, NC)),
            vmem((LB, NC)),
            vmem((RHS, 8, 128)),
            vmem((1, 128)),
            vmem((1, 128)),
            vmem((8, 1, 128)),
            vmem((16, 1, 128)),
            pltpu.SemaphoreType.DMA((5,)),
            pltpu.SemaphoreType.DMA((ITERS, RHS, 4)),
            pltpu.SemaphoreType.DMA((ITERS, RHS, 4)),
            pltpu.SemaphoreType.DMA((2,)),
            pltpu.SemaphoreType.DMA((2,)),
            pltpu.SemaphoreType.DMA((2,)),
            pltpu.SemaphoreType.DMA((2,)),
        ],
        compiler_params=pltpu.CompilerParams(
            collective_id=0, has_side_effects=True, vmem_limit_bytes=34 << 20
        ),
        name="powers",
    )(pressure_drive, throat_radius, wet_flag, cap_pressure, storage)
    fast = pl.pallas_call(
        combine_kernel,
        out_shape=[jax.ShapeDtypeStruct(field, F32)] * 2,
        in_specs=[pl.BlockSpec(memory_space=pltpu.SMEM)] + [in_vmem] * 4,
        out_specs=[anywhere] * 2,
        scratch_shapes=[vmem(field), vmem(field), pltpu.SemaphoreType.DMA((RHS, 2))],
        compiler_params=pltpu.CompilerParams(vmem_limit_bytes=24 << 20),
        name="combine",
    )(coefs, *vectors)
    return lax.cond(
        sound[0, 0] == 1,
        lambda: tuple(fast),
        lambda: plain_iteration(pressure_drive, throat_radius, wet_flag, cap_pressure, storage),
    )


def solution(mesh):
    in_specs = (
        P(None, "slab", "cross", None),
        P(None, "slab", "cross", None),
        P(None, "slab", "cross", None),
        P("slab", "cross", None),
        P("slab", "cross", None),
    )
    out_specs = (P(None, "slab", "cross", None), P(None, "slab", "cross", None))
    return jax.shard_map(
        per_device, mesh=mesh, in_specs=in_specs, out_specs=out_specs, check_vma=False
    )
```

```python
import functools

import jax
import jax.numpy as jnp
from jax import lax
from jax.experimental import pallas as pl
from jax.experimental.pallas import tpu as pltpu
from jax.sharding import PartitionSpec as P

ITERS = 3
RHS = 3
F32 = jnp.float32
MESH = pl.DeviceIdType.MESH
SLABS, CROSSES = 32, 4
LA, LB, NC = 8, 64, 512
TILES = LB // 8
CHUNKS = LA // 2
ERROR_GAIN_MAX = 2500.0
CANCEL_MAX = 300.0


def shifted(value, axis, steps):
    count = lax.axis_size(axis)
    leading, last = (max(0, -steps), min(count, count - steps))
    return lax.ppermute(value, axis, [(source, source + steps) for source in range(leading, last)])


def with_halo(cells, sides, width):
    for axis, dim in sides:
        count = lax.axis_size(axis)
        ends = count - 1
        head = lax.slice_in_dim(cells, 0, width, axis=dim)
        tail = lax.slice_in_dim(cells, cells.shape[dim] - width, cells.shape[dim], axis=dim)
        cells = jnp.concatenate(
            [
                lax.ppermute(tail, axis, [(i, (i + 1) % count) for i in range(ends)]),
                cells,
                lax.ppermute(head, axis, [((i + 1) % count, i) for i in range(ends)]),
            ],
            axis=dim,
        )
    return cells


def totals(values):
    return jnp.sum(values, axis=(1, 2, 3))


def widen(scalars):
    return scalars[:, None, None, None]


def squares(residual):
    return lax.psum(totals(residual * residual), ("slab", "cross"))


def depth_terms(vector, along_depth, lower_depth):
    upper_values = jnp.pad(vector[..., 1:], ((0, 0), (0, 0), (0, 0), (0, 1)))
    lower_values = jnp.pad(vector[..., :-1], ((0, 0), (0, 0), (0, 0), (1, 0)))
    return along_depth * (vector - upper_values) + lower_depth * (vector - lower_values)


def plain_iteration(pressure_drive, throat_radius, wet_flag, cap_pressure, storage):
    squared = throat_radius * throat_radius
    film_term = 0.4 * squared / (cap_pressure * cap_pressure)[None]
    conduct = jnp.where(wet_flag == 1, squared * squared, film_term)
    extent = conduct.shape[1:]
    layer_slab = lax.broadcasted_iota(jnp.int32, extent, 0)
    layer_cross = lax.broadcasted_iota(jnp.int32, extent, 1)
    layer_depth = lax.broadcasted_iota(jnp.int32, extent, 2)
    edge_slab = (layer_slab == extent[0] - 1) & (
        lax.axis_index("slab") == lax.axis_size("slab") - 1
    )
    edge_cross = (layer_cross == extent[1] - 1) & (
        lax.axis_index("cross") == lax.axis_size("cross") - 1
    )
    along_slab = jnp.where(edge_slab, 0.0, conduct[0])
    along_cross = jnp.where(edge_cross, 0.0, conduct[1])
    along_depth = jnp.where(layer_depth == extent[2] - 1, 0.0, conduct[2])
    lower_depth = jnp.pad(along_depth[:, :, :-1], ((0, 0), (0, 0), (1, 0)))
    rim_slab = shifted(along_slab[-1:], "slab", 1)
    rim_cross = shifted(along_cross[:, -1:], "cross", 1)
    lower_slab = jnp.concatenate([rim_slab, along_slab[:-1]], 0)
    lower_cross = jnp.concatenate([rim_cross, along_cross[:, :-1]], 1)
    solution = jnp.zeros_like(pressure_drive)
    residual = pressure_drive
    direction = pressure_drive
    norm_now = squares(residual)
    for iteration in range(ITERS):
        padded = with_halo(direction, (("slab", 1), ("cross", 2)), 1)
        result = storage * direction
        result = result + along_slab * (direction - padded[:, 2:, 1:-1])
        result = result + lower_slab * (direction - padded[:, :-2, 1:-1])
        result = result + along_cross * (direction - padded[:, 1:-1, 2:])
        result = result + lower_cross * (direction - padded[:, 1:-1, :-2])
        applied = result + depth_terms(direction, along_depth, lower_depth)
        step_size = norm_now / lax.psum(totals(direction * applied), ("slab", "cross"))
        solution = solution + widen(step_size) * direction
        residual = residual - widen(step_size) * applied
        if iteration + 1 < ITERS:
            norm_next = squares(residual)
            direction = residual + widen(norm_next / norm_now) * direction
            norm_now = norm_next
    return (solution, residual)


def scalars_of(m):
    def parts(c0, c1, c2, first):
        return (
            c0 * c0 * m[first],
            2.0 * c0 * c1 * m[first + 1],
            c1 * c1 * m[first + 2],
            2.0 * c0 * c2 * m[first + 2],
            2.0 * c1 * c2 * m[first + 3],
            c2 * c2 * m[first + 4],
        )

    def total(terms):
        return (terms[0] + terms[1]) + (terms[2] + terms[3]) + (terms[4] + terms[5])

    def bulk(terms):
        return total([jnp.abs(term) for term in terms])

    rr0 = m[0]
    step0 = m[0] / m[1]
    image0 = step0 * step0 * m[2]
    rr1 = image0 - rr0
    turn0 = rr1 / rr0
    p0, p1 = 1.0 + turn0, -step0

    def pair(first):
        return p0 * p0 * m[first], 2.0 * p0 * p1 * m[first + 1], p1 * p1 * m[first + 2]

    energy1 = pair(1)
    curve1 = energy1[0] + energy1[1] + energy1[2]
    step1 = rr1 / curve1
    image1 = pair(2)
    rr2 = step1 * step1 * (image1[0] + image1[1] + image1[2]) - rr1
    turn1 = rr2 / rr1
    r1, r2 = -step0 - step1 * p0, -step1 * p1
    q0, q1, q2 = 1.0 + turn1 * p0, r1 + turn1 * p1, r2
    energy2 = parts(q0, q1, q2, 1)
    curve2 = total(energy2)
    step2 = rr2 / curve2
    x0 = step0 + step1 * p0 + step2 * q0
    x1 = step1 * p1 + step2 * q1
    x2 = step2 * q2
    d1, d2, d3 = r1 - step2 * q0, r2 - step2 * q1, -step2 * q2

    image2 = parts(q0, q1, q2, 2)
    rr3 = step2 * step2 * total(image2) - rr2
    gain1 = (image0 + rr0) / rr1
    gain2 = (energy1[0] + jnp.abs(energy1[1]) + energy1[2]) / curve1
    gain3 = (step1 * step1 * (image1[0] + jnp.abs(image1[1]) + image1[2]) + rr1) / rr2
    gain4 = bulk(energy2) / curve2
    gain5 = (step2 * step2 * bulk(image2) + rr2) / rr3
    gain = (
        (gain1 + gain2) * jnp.sqrt(rr0 / rr3)
        + gain3 * jnp.sqrt(rr1 / rr3)
        + gain4 * jnp.sqrt(rr2 / rr3)
        + gain5
    )
    cancel = (
        jnp.sqrt(m[0])
        + jnp.abs(d1) * jnp.sqrt(m[2])
        + jnp.abs(d2) * jnp.sqrt(m[4])
        + jnp.abs(d3) * jnp.sqrt(m[6])
    ) / jnp.sqrt(rr3)
    sound = (
        (rr1 > 0.0)
        & (curve1 > 0.0)
        & (rr2 > 0.0)
        & (curve2 > 0.0)
        & (rr3 > 0.0)
        & (gain < ERROR_GAIN_MAX)
        & (cancel < CANCEL_MAX)
    )
    return (x0, x1, x2, d1, d2, d3), sound


def fold(value):
    return (value[:, 0:128] + value[:, 128:256]) + (value[:, 256:384] + value[:, 384:512])


def powers_kernel(
    b_hbm, rad_hbm, wet_hbm, cap_hbm, sto_hbm,
    v0, v1, v2, v3, coef_ref, sound_ref,
    cond, wet, cap, sto, cs_low, cc_out, cc_low,
    halo_low, halo_up, edge_low, edge_up, rim_low, rim_up,
    flux, dots_ref, sent1, sent2, got1, got2,
    load_sem, chunk_sem, halo_send, halo_recv, cond_send, cond_recv, sum_send, sum_recv,
):
    s, c = lax.axis_index("slab"), lax.axis_index("cross")
    up, down = lax.rem(s + 1, SLABS), lax.rem(s + SLABS - 1, SLABS)
    right, left = lax.rem(c + 1, CROSSES), lax.rem(c + CROSSES - 1, CROSSES)
    row_y, in_row = s // 8, lax.rem(s, 8)
    group1 = [(row_y * 8 + lax.rem(in_row + i, 8), c) for i in range(1, 8)]
    group2 = [
        (lax.rem(row_y + i, 4) * 8 + in_row, lax.rem(c + j, 4))
        for i in range(4)
        for j in range(4)
        if i or j
    ]
    barrier = pltpu.get_barrier_semaphore()
    greeted = [(up, c), (down, c), (s, right), (s, left)] + group1 + group2
    for peer in greeted:
        pl.semaphore_signal(barrier, inc=1, device_id=peer, device_id_type=MESH)

    def chunk_copies(i):
        layers = pl.ds(LA - 2 - 2 * i, 2)
        return (
            pltpu.make_async_copy(rad_hbm.at[:, layers], cond.at[:, layers], chunk_sem.at[i, 0]),
            pltpu.make_async_copy(wet_hbm.at[:, layers], wet.at[:, layers], chunk_sem.at[i, 1]),
            pltpu.make_async_copy(cap_hbm.at[layers], cap.at[layers], chunk_sem.at[i, 2]),
        )

    load_b = pltpu.make_async_copy(b_hbm, v0, load_sem.at[0])
    load_sto = pltpu.make_async_copy(sto_hbm, sto, load_sem.at[1])
    for i in range(CHUNKS):
        for copy in chunk_copies(i):
            copy.start()
        if i == 0:
            load_b.start()
    load_sto.start()

    vectors = (v0, v1, v2, v3)

    def send(src, dst, k, q, place, device):
        return pltpu.make_async_remote_copy(
            src_ref=src, dst_ref=dst, send_sem=halo_send.at[k, q, place],
            recv_sem=halo_recv.at[k, q, place], device_id=device, device_id_type=MESH)

    def to_down(k, q):
        src = b_hbm if k == 0 else vectors[k]
        return send(src.at[q, 0], halo_up.at[k, q], k, q, 0, (down, c))

    def to_up(k, q):
        src = b_hbm if k == 0 else vectors[k]
        return send(src.at[q, LA - 1], halo_low.at[k, q], k, q, 1, (up, c))

    def to_left(k, q):
        return send(edge_low.at[k, q], rim_up.at[k, q], k, q, 2, (s, left))

    def to_right(k, q):
        return send(edge_up.at[k, q], rim_low.at[k, q], k, q, 3, (s, right))

    send_cs = pltpu.make_async_remote_copy(
        src_ref=cond.at[0, LA - 1], dst_ref=cs_low, send_sem=cond_send.at[0],
        recv_sem=cond_recv.at[0], device_id=(up, c), device_id_type=MESH)
    send_cc = pltpu.make_async_remote_copy(
        src_ref=cc_out, dst_ref=cc_low, send_sem=cond_send.at[1],
        recv_sem=cond_recv.at[1], device_id=(s, right), device_id_type=MESH)

    pl.semaphore_wait(barrier, len(greeted))
    to_up(0, 0).start()
    for q in range(RHS):
        to_down(0, q).start()

    row = lax.broadcasted_iota(jnp.int32, (8, NC), 0)
    lane = lax.broadcasted_iota(jnp.int32, (8, NC), 1)
    first_row, last_row, last_lane = row == 0, row == 7, lane == NC - 1

    def conduct(a):
        ends_slab = (s == SLABS - 1) & (a == LA - 1)
        for j in range(TILES):
            at = pl.ds(8 * j, 8)
            pressure = cap[a, at, :]
            film = 0.4 / (pressure * pressure)
            for k in range(3):
                radius = cond[k, a, at, :]
                squared = radius * radius
                value = squared * jnp.where(wet[k, a, at, :] == 1, squared, film)
                if k == 0:
                    value = jnp.where(ends_slab, 0.0, value)
                if k == 1 and j == TILES - 1:
                    value = jnp.where(last_row & (c == CROSSES - 1), 0.0, value)
                    cc_out[a] = value[7:8, :]
                if k == 2:
                    value = jnp.where(last_lane, 0.0, value)
                cond[k, a, at, :] = value

    for copy in chunk_copies(0):
        copy.wait()
    conduct(LA - 1)
    send_cs.start()
    for q in range(1, RHS):
        to_up(0, q).start()
    load_b.wait()

    def pack(a, carry):
        for q in range(RHS):
            edge_low[0, q, a] = v0[q, a, 0:1, :]
            edge_up[0, q, a] = v0[q, a, LB - 1 : LB, :]
        return carry

    lax.fori_loop(0, LA, pack, 0)
    for q in range(RHS):
        to_left(0, q).start()
        to_right(0, q).start()
    conduct(LA - 2)

    def chunk(i, carry):
        for copy in chunk_copies(i):
            copy.wait()
        conduct(LA - 1 - 2 * i)
        conduct(LA - 2 - 2 * i)
        return carry

    lax.fori_loop(1, CHUNKS, chunk, 0)
    send_cc.start()
    load_sto.wait()
    dots_ref[...] = jnp.zeros_like(dots_ref)

    def stages(k):
        v, w = vectors[k], vectors[k + 1]
        places = (2 * k + 1, 2 * k + 2) + ((0,) if k == 0 else ())

        def layer(q, a, below, above, keep, dots):
            here = v[q, a, 0:8, :]
            here_up = pltpu.roll(here, 7, 0)
            passed = jnp.zeros((8, NC), F32)
            for j in range(TILES):
                at = pl.ds(8 * j, 8)
                if j + 1 < TILES:
                    after = v[q, a, 8 * j + 8 : 8 * j + 16, :]
                    after_up = pltpu.roll(after, 7, 0)
                else:
                    after = after_up = here
                flux_cross = cond[1, a, at, :] * (jnp.where(last_row, after_up, here_up) - here)
                arrived = pltpu.roll(flux_cross, 1, 0)
                flux_depth = cond[2, a, at, :] * (pltpu.roll(here, NC - 1, 1) - here)
                flux_slab = cond[0, a, at, :] * (above(at) - here)
                image = sto[a, at, :] * here
                image = image - flux_slab + below(at, here)
                image = image - flux_cross + jnp.where(first_row, passed, arrived)
                image = image - flux_depth + pltpu.roll(flux_depth, 1, 1)
                if keep:
                    flux[at, :] = flux_slab
                w[q, a, at, :] = image
                dots = (dots[0] + fold(here * image), dots[1] + fold(image * image)) + (
                    (dots[2] + fold(here * here),) if k == 0 else ()
                )
                passed, here, here_up = arrived, after, after_up
            return dots

        def interior(q, unused):
            for j in range(TILES):
                at = pl.ds(8 * j, 8)
                flux[at, :] = cond[0, 0, at, :] * (v[q, 1, at, :] - v[q, 0, at, :])
            dots = (jnp.zeros((8, 128), F32),) * len(places)
            dots = lax.fori_loop(
                1, LA - 1,
                lambda a, carry: layer(
                    q, a, lambda at, here: flux[at, :], lambda at: v[q, a + 1, at, :], True, carry),
                dots)
            for place, dot in zip(places, dots):
                dots_ref[q, place] = dot
            return unused

        def rim(q, a, dots):
            low, high = edge_low[k, q, a], edge_up[k, q, a]
            enters = cc_low[a] * (low - rim_low[k, q, a])
            leaves = cc_out[a] * (rim_up[k, q, a] - high)
            first, last = w[q, a, 0:1, :], w[q, a, LB - 1 : LB, :]
            new_first, new_last = first + enters, last - leaves
            w[q, a, 0:1, :] = new_first
            w[q, a, LB - 1 : LB, :] = new_last
            if k + 1 < ITERS:
                edge_low[k + 1, q, a] = new_first
                edge_up[k + 1, q, a] = new_last
            return (
                dots[0] + fold(low * enters - high * leaves),
                dots[1] + fold(enters * (first + new_first) - leaves * (last + new_last)),
            )

        def border(q, unused):
            to_down(k, q).wait_recv()
            to_left(k, q).wait_recv()
            to_right(k, q).wait_recv()
            if k == 0:
                @pl.when(q == 0)
                def _():
                    send_cc.wait_recv()
            dots = (jnp.zeros((8, 128), F32),) * len(places)
            line = (jnp.zeros((1, 128), F32),) * 2
            dots = layer(
                q, LA - 1,
                lambda at, here: cond[0, LA - 2, at, :] * (here - v[q, LA - 2, at, :]),
                lambda at: halo_up[k, q, at, :], False, dots)
            line = rim(q, LA - 1, line)
            if k + 1 < ITERS:
                to_up(k + 1, q).start()
            to_up(k, q).wait_recv()
            if k == 0:
                @pl.when(q == 0)
                def _():
                    send_cs.wait_recv()
            dots = layer(
                q, 0,
                lambda at, here: cs_low[at, :] * (here - halo_low[k, q, at, :]),
                lambda at: v[q, 1, at, :], False, dots)
            line = rim(q, 0, line)
            if k + 1 < ITERS:
                to_down(k + 1, q).start()
            line = lax.fori_loop(1, LA - 1, lambda a, carry: rim(q, a, carry), line)
            if k + 1 < ITERS:
                to_left(k + 1, q).start()
                to_right(k + 1, q).start()
            for i, (place, dot) in enumerate(zip(places, dots)):
                dots_ref[q, place] = dots_ref[q, place] + dot
                if i < 2:
                    dots_ref[q, place, 0:1, :] = dots_ref[q, place, 0:1, :] + line[i]
            return unused

        return interior, border

    interior, border = stages(0)
    lax.fori_loop(0, RHS, interior, 0)
    for k in range(1, ITERS):
        next_interior, next_border = stages(k)

        def both(q, unused, border=border, interior=next_interior):
            border(q, unused)
            return interior(q, unused)

        lax.fori_loop(0, RHS, both, 0)
        border = next_border
    lax.fori_loop(0, RHS, border, 0)

    rows = lax.broadcasted_iota(jnp.int32, (8, 128), 0)
    lanes = lax.broadcasted_iota(jnp.int32, (8, 128), 1)
    packed = jnp.zeros((8, 128), F32)
    for q in range(RHS):
        moments = jnp.concatenate(
            [jnp.sum(dots_ref[q, j], axis=0, keepdims=True) for j in range(8)], axis=0)
        lane_sum = jnp.sum(moments, axis=1, keepdims=True)
        packed = packed + jnp.where(lanes == rows + 8 * q, lane_sum, 0.0)
    own = jnp.sum(packed, axis=0, keepdims=True)

    for sent, got, group, place, index in (
        (sent1, got1, group1, in_row, 0),
        (sent2, got2, group2, row_y * 4 + c, 1),
    ):
        sent[...] = own
        for peer in group:
            pltpu.make_async_remote_copy(
                src_ref=sent, dst_ref=got.at[place], send_sem=sum_send.at[index],
                recv_sem=sum_recv.at[index], device_id=peer, device_id_type=MESH).start()
        got[place] = own
        others = got.at[pl.ds(0, len(group))]
        pltpu.make_async_copy(others, others, sum_recv.at[index]).wait()
        terms = [got[i] for i in range(len(group) + 1)]
        while len(terms) > 1:
            terms = [terms[i] + terms[i + 1] for i in range(0, len(terms), 2)]
        own = terms[0]

    summed = jnp.broadcast_to(own, (8, 128))
    used = (lanes % 8 == 0) & (lanes < 8 * RHS)
    stand_in = (1.0, 1.0, 2.0, 6.0, 24.0, 120.0, 720.0)
    m = [
        jnp.where(used, pltpu.roll(summed, (128 - j) % 128, 1) if j else summed, stand_in[j])
        for j in range(7)
    ]
    coefs, sound = scalars_of(m)
    for i, coef in enumerate(coefs):
        coef_ref[i : i + 1, :] = coef[0:1, :]
    coef_ref[6:8, :] = jnp.zeros((2, 128), F32)
    sound_ref[...] = jnp.min(jnp.where(sound, 1, 0), axis=1, keepdims=True)[0:1, :]

    send_cs.wait_send()
    send_cc.wait_send()

    def finish(q, unused):
        for k in range(ITERS):
            for copy in (to_down(k, q), to_up(k, q), to_left(k, q), to_right(k, q)):
                copy.wait_send()
        return unused

    lax.fori_loop(0, RHS, finish, 0)
    for got, group, index in ((got1, group1, 0), (got2, group2, 1)):
        others = got.at[pl.ds(0, len(group))]
        pltpu.make_async_copy(others, others, sum_send.at[index]).wait()


def combine_kernel(coef, v0, v1, v2, v3, x_hbm, r_hbm, x, r, sem):
    half = LA // 2
    copies = []
    for q in range(RHS):
        x0, x1, x2, d1, d2, d3 = (coef[i, 8 * q] for i in range(6))

        def layer(a, carry):
            for j in range(TILES):
                at = pl.ds(8 * j, 8)
                t0, t1, t2, t3 = (v[q, a, at, :] for v in (v0, v1, v2, v3))
                x[q, a, at, :] = x0 * t0 + x1 * t1 + x2 * t2
                r[q, a, at, :] = t0 + d1 * t1 + d2 * t2 + d3 * t3
            return carry

        for h in range(2):
            lax.fori_loop(h * half, (h + 1) * half, layer, 0)
            part = pl.ds(h * half, half)
            for index, (source, target) in enumerate(((x, x_hbm), (r, r_hbm))):
                copy = pltpu.make_async_copy(
                    source.at[q, part], target.at[q, part], sem.at[q, h, index])
                copy.start()
                copies.append(copy)
    for copy in copies:
        copy.wait()


def per_device(pressure_drive, throat_radius, wet_flag, cap_pressure, storage):
    field = (RHS, LA, LB, NC)
    vmem = functools.partial(pltpu.VMEM, dtype=F32)
    in_vmem = pl.BlockSpec(memory_space=pltpu.VMEM)
    anywhere = pl.BlockSpec(memory_space=pl.ANY)
    *vectors, coefs, sound = pl.pallas_call(
        powers_kernel,
        out_shape=[pltpu.VMEM(field, F32)] * 4
        + [jax.ShapeDtypeStruct((8, 128), F32), jax.ShapeDtypeStruct((1, 1), jnp.int32)],
        in_specs=[anywhere] * 5,
        out_specs=[in_vmem] * 6,
        scratch_shapes=[
            vmem(field),
            pltpu.VMEM(field, jnp.int32),
            vmem((LA, LB, NC)),
            vmem((LA, LB, NC)),
            vmem((LB, NC)),
            vmem((LA, 1, NC)),
            vmem((LA, 1, NC)),
            vmem((ITERS, RHS, LB, NC)),
            vmem((ITERS, RHS, LB, NC)),
            vmem((ITERS, RHS, LA, 1, NC)),
            vmem((ITERS, RHS, LA, 1, NC)),
            vmem((ITERS, RHS, LA, 1, NC)),
            vmem((ITERS, RHS, LA, 1, NC)),
            vmem((LB, NC)),
            vmem((RHS, 8, 8, 128)),
            vmem((1, 128)),
            vmem((1, 128)),
            vmem((8, 1, 128)),
            vmem((16, 1, 128)),
            pltpu.SemaphoreType.DMA((2,)),
            pltpu.SemaphoreType.DMA((CHUNKS, 3)),
            pltpu.SemaphoreType.DMA((ITERS, RHS, 4)),
            pltpu.SemaphoreType.DMA((ITERS, RHS, 4)),
            pltpu.SemaphoreType.DMA((2,)),
            pltpu.SemaphoreType.DMA((2,)),
            pltpu.SemaphoreType.DMA((2,)),
            pltpu.SemaphoreType.DMA((2,)),
        ],
        compiler_params=pltpu.CompilerParams(
            collective_id=0, has_side_effects=True, vmem_limit_bytes=34 << 20
        ),
        name="powers",
    )(pressure_drive, throat_radius, wet_flag, cap_pressure, storage)
    fast = pl.pallas_call(
        combine_kernel,
        out_shape=[jax.ShapeDtypeStruct(field, F32)] * 2,
        in_specs=[pl.BlockSpec(memory_space=pltpu.SMEM)] + [in_vmem] * 4,
        out_specs=[anywhere] * 2,
        scratch_shapes=[vmem(field), vmem(field), pltpu.SemaphoreType.DMA((RHS, 2, 2))],
        compiler_params=pltpu.CompilerParams(vmem_limit_bytes=24 << 20),
        name="combine",
    )(coefs, *vectors)
    return lax.cond(
        sound[0, 0] == 1,
        lambda: tuple(fast),
        lambda: plain_iteration(pressure_drive, throat_radius, wet_flag, cap_pressure, storage),
    )


def solution(mesh):
    in_specs = (
        P(None, "slab", "cross", None),
        P(None, "slab", "cross", None),
        P(None, "slab", "cross", None),
        P("slab", "cross", None),
        P("slab", "cross", None),
    )
    out_specs = (P(None, "slab", "cross", None), P(None, "slab", "cross", None))
    return jax.shard_map(
        per_device, mesh=mesh, in_specs=in_specs, out_specs=out_specs, check_vma=False
    )
```

```python
import functools

import jax
import jax.numpy as jnp
from jax import lax
from jax.experimental import pallas as pl
from jax.experimental.pallas import tpu as pltpu
from jax.sharding import PartitionSpec as P

ITERS = 3
RHS = 3
F32 = jnp.float32
MESH = pl.DeviceIdType.MESH
SLABS, CROSSES = 32, 4
LA, LB, NC = 8, 64, 512
TILES = LB // 8
CHUNKS = LA // 2
CHIP_OFFSETS = sorted(
    [(y, z, x) for y in range(4) for z in range(4) for x in range(4) if x or y or z],
    key=lambda offset: -sum(min(step, 4 - step) for step in offset),
)
ERROR_GAIN_MAX = 3000.0
CANCEL_MAX = 150.0
MOMENTS = 6
PAIRS = [(i, j) for i in range(4) for j in range(i, 4)]
LANES = MOMENTS + len(PAIRS)


def shifted(value, axis, steps):
    count = lax.axis_size(axis)
    leading, last = (max(0, -steps), min(count, count - steps))
    return lax.ppermute(value, axis, [(source, source + steps) for source in range(leading, last)])


def with_halo(cells, sides, width):
    for axis, dim in sides:
        count = lax.axis_size(axis)
        ends = count - 1
        head = lax.slice_in_dim(cells, 0, width, axis=dim)
        tail = lax.slice_in_dim(cells, cells.shape[dim] - width, cells.shape[dim], axis=dim)
        cells = jnp.concatenate(
            [
                lax.ppermute(tail, axis, [(i, (i + 1) % count) for i in range(ends)]),
                cells,
                lax.ppermute(head, axis, [((i + 1) % count, i) for i in range(ends)]),
            ],
            axis=dim,
        )
    return cells


def totals(values):
    return jnp.sum(values, axis=(1, 2, 3))


def widen(scalars):
    return scalars[:, None, None, None]


def squares(residual):
    return lax.psum(totals(residual * residual), ("slab", "cross"))


def depth_terms(vector, along_depth, lower_depth):
    upper_values = jnp.pad(vector[..., 1:], ((0, 0), (0, 0), (0, 0), (0, 1)))
    lower_values = jnp.pad(vector[..., :-1], ((0, 0), (0, 0), (0, 0), (1, 0)))
    return along_depth * (vector - upper_values) + lower_depth * (vector - lower_values)


def plain_iteration(pressure_drive, throat_radius, wet_flag, cap_pressure, storage):
    squared = throat_radius * throat_radius
    film_term = 0.4 * squared / (cap_pressure * cap_pressure)[None]
    conduct = jnp.where(wet_flag == 1, squared * squared, film_term)
    extent = conduct.shape[1:]
    layer_slab = lax.broadcasted_iota(jnp.int32, extent, 0)
    layer_cross = lax.broadcasted_iota(jnp.int32, extent, 1)
    layer_depth = lax.broadcasted_iota(jnp.int32, extent, 2)
    edge_slab = (layer_slab == extent[0] - 1) & (
        lax.axis_index("slab") == lax.axis_size("slab") - 1
    )
    edge_cross = (layer_cross == extent[1] - 1) & (
        lax.axis_index("cross") == lax.axis_size("cross") - 1
    )
    along_slab = jnp.where(edge_slab, 0.0, conduct[0])
    along_cross = jnp.where(edge_cross, 0.0, conduct[1])
    along_depth = jnp.where(layer_depth == extent[2] - 1, 0.0, conduct[2])
    lower_depth = jnp.pad(along_depth[:, :, :-1], ((0, 0), (0, 0), (1, 0)))
    rim_slab = shifted(along_slab[-1:], "slab", 1)
    rim_cross = shifted(along_cross[:, -1:], "cross", 1)
    lower_slab = jnp.concatenate([rim_slab, along_slab[:-1]], 0)
    lower_cross = jnp.concatenate([rim_cross, along_cross[:, :-1]], 1)
    solution = jnp.zeros_like(pressure_drive)
    residual = pressure_drive
    direction = pressure_drive
    norm_now = squares(residual)
    for iteration in range(ITERS):
        padded = with_halo(direction, (("slab", 1), ("cross", 2)), 1)
        result = storage * direction
        result = result + along_slab * (direction - padded[:, 2:, 1:-1])
        result = result + lower_slab * (direction - padded[:, :-2, 1:-1])
        result = result + along_cross * (direction - padded[:, 1:-1, 2:])
        result = result + lower_cross * (direction - padded[:, 1:-1, :-2])
        applied = result + depth_terms(direction, along_depth, lower_depth)
        step_size = norm_now / lax.psum(totals(direction * applied), ("slab", "cross"))
        solution = solution + widen(step_size) * direction
        residual = residual - widen(step_size) * applied
        if iteration + 1 < ITERS:
            norm_next = squares(residual)
            direction = residual + widen(norm_next / norm_now) * direction
            norm_now = norm_next
    return (solution, residual)


def scalars_of(m, sample):
    def parts(c0, c1, c2, first):
        return (
            c0 * c0 * m[first],
            2.0 * c0 * c1 * m[first + 1],
            c1 * c1 * m[first + 2],
            2.0 * c0 * c2 * m[first + 2],
            2.0 * c1 * c2 * m[first + 3],
            c2 * c2 * m[first + 4],
        )

    def total(terms):
        return (terms[0] + terms[1]) + (terms[2] + terms[3]) + (terms[4] + terms[5])

    rr0 = m[0]
    step0 = m[0] / m[1]
    image0 = step0 * step0 * m[2]
    rr1 = image0 - rr0
    turn0 = rr1 / rr0
    p0, p1 = 1.0 + turn0, -step0

    def pair(first):
        return p0 * p0 * m[first], 2.0 * p0 * p1 * m[first + 1], p1 * p1 * m[first + 2]

    energy1 = pair(1)
    curve1 = energy1[0] + energy1[1] + energy1[2]
    step1 = rr1 / curve1
    image1 = pair(2)
    rr2 = step1 * step1 * (image1[0] + image1[1] + image1[2]) - rr1
    turn1 = rr2 / rr1
    r1, r2 = -step0 - step1 * p0, -step1 * p1
    q0, q1, q2 = 1.0 + turn1 * p0, r1 + turn1 * p1, r2
    energy2 = parts(q0, q1, q2, 1)
    curve2 = total(energy2)
    step2 = rr2 / curve2
    x0 = step0 + step1 * p0 + step2 * q0
    x1 = step1 * p1 + step2 * q1
    x2 = step2 * q2
    d1, d2, d3 = r1 - step2 * q0, r2 - step2 * q1, -step2 * q2

    d = (1.0, d1, d2, d3)
    rr3 = 0.0
    for products, (i, j) in zip(sample, PAIRS):
        rr3 = rr3 + (1.0 if i == j else 2.0) * d[i] * d[j] * products
    gain1 = (image0 + rr0) / rr1
    gain2 = (energy1[0] + jnp.abs(energy1[1]) + energy1[2]) / curve1
    gain3 = (step1 * step1 * (image1[0] + jnp.abs(image1[1]) + image1[2]) + rr1) / rr2
    gain4 = total([jnp.abs(term) for term in energy2]) / curve2
    gain = (
        (gain1 + gain2) * jnp.sqrt(rr0 / rr3)
        + gain3 * jnp.sqrt(rr1 / rr3)
        + gain4 * jnp.sqrt((rr2 + rr3) / rr3)
    )
    cancel = (
        jnp.sqrt(m[0]) + jnp.abs(d1) * jnp.sqrt(m[2]) + jnp.abs(d2) * jnp.sqrt(m[4])
    ) / jnp.sqrt(rr3)
    sound = (
        (rr1 > 0.0)
        & (curve1 > 0.0)
        & (rr2 > 0.0)
        & (curve2 > 0.0)
        & (rr3 > 0.0)
        & (gain < ERROR_GAIN_MAX)
        & (cancel < CANCEL_MAX)
    )
    return (x0, x1, x2, d1, d2, d3), sound


def fold(value):
    return (value[:, 0:128] + value[:, 128:256]) + (value[:, 256:384] + value[:, 384:512])


def powers_kernel(
    b_hbm, rad_hbm, wet_hbm, cap_hbm, sto_hbm,
    v0, v1, v2, v3, coef_ref, sound_ref,
    cond, wet, cap, sto, cs_low, cc_out, cc_low,
    halo_low, halo_up, edge_low, edge_up, rims,
    flux, dots_ref, early_sum, token, met, sent, got, pair_sent, pair_got,
    load_sem, chunk_sem, halo_send, halo_recv, cond_send, cond_recv, meet_send, meet_recv,
    sum_send, sum_recv,
):
    s, c = lax.axis_index("slab"), lax.axis_index("cross")
    has_up, has_down = s < SLABS - 1, s > 0
    has_right, has_left = c < CROSSES - 1, c > 0
    up, down = jnp.where(has_up, s + 1, s - 1), jnp.where(has_down, s - 1, s + 1)
    right, left = jnp.where(has_right, c + 1, c - 1), jnp.where(has_left, c - 1, c + 1)
    row_y = s // 8
    col_z, core = lax.rem(s // 2, 4), lax.rem(s, 2)
    along_z = [(row_y * 8 + lax.rem(col_z + i, 4) * 2 + core, c) for i in range(1, 4)]
    along_y = [(lax.rem(row_y + i, 4) * 8 + lax.rem(s, 8), c) for i in range(1, 4)]
    along_x = [(s, lax.rem(c + i, 4)) for i in range(1, 4)]
    barrier = pltpu.get_barrier_semaphore()
    greeted = along_x + along_z + along_y
    for peer in greeted:
        pl.semaphore_signal(barrier, inc=1, device_id=peer, device_id_type=MESH)
    for there, peer in ((has_up, up), (has_down, down)):
        @pl.when(there)
        def _(peer=peer):
            pl.semaphore_signal(barrier, inc=1, device_id=(peer, c), device_id_type=MESH)

    def chunk_copies(i):
        layers = pl.ds(LA - 2 - 2 * i, 2)
        return (
            pltpu.make_async_copy(rad_hbm.at[:, layers], cond.at[:, layers], chunk_sem.at[i, 0]),
            pltpu.make_async_copy(wet_hbm.at[:, layers], wet.at[:, layers], chunk_sem.at[i, 1]),
            pltpu.make_async_copy(cap_hbm.at[layers], cap.at[layers], chunk_sem.at[i, 2]),
        )

    load_b = pltpu.make_async_copy(b_hbm, v0, load_sem.at[0])
    load_sto = pltpu.make_async_copy(sto_hbm, sto, load_sem.at[1])
    for i in range(CHUNKS):
        for copy in chunk_copies(i):
            copy.start()
        if i == 0:
            load_b.start()
    load_sto.start()

    vectors = (v0, v1, v2, v3)

    def send(src, dst, direction, arrival, device):
        return pltpu.make_async_remote_copy(
            src_ref=src, dst_ref=dst, send_sem=halo_send.at[direction], recv_sem=arrival,
            device_id=device, device_id_type=MESH)

    def to_down(k, q):
        src = b_hbm if k == 0 else vectors[k]
        return send(src.at[q, 0], halo_up.at[k, q], 0, halo_recv.at[k, q, 0], (down, c))

    def to_up(k, q):
        src = b_hbm if k == 0 else vectors[k]
        return send(src.at[q, LA - 1], halo_low.at[k, q], 1, halo_recv.at[k, q, 1], (up, c))

    def to_sides(k, q):
        arrival = halo_recv.at[k, q, 2]

        @pl.when(has_left)
        def _():
            send(edge_low.at[k, q], rims.at[k, q, 1], 2, arrival, (s, left)).start()

        @pl.when(has_right)
        def _():
            send(edge_up.at[k, q], rims.at[k, q, 0], 3, arrival, (s, right)).start()

    def wait_sides(k, q):
        arrival = halo_recv.at[k, q, 2]

        @pl.when(has_left & has_right)
        def _():
            wait_for(rims.at[k, q], arrival)

        @pl.when(jnp.logical_not(has_left & has_right))
        def _():
            wait_for(rims.at[k, q, 0], arrival)

    def wait_for(whole, sem):
        pltpu.make_async_copy(whole, whole, sem).wait()

    send_cs = pltpu.make_async_remote_copy(
        src_ref=cond.at[0, LA - 1], dst_ref=cs_low, send_sem=cond_send.at[0],
        recv_sem=cond_recv.at[0], device_id=(up, c), device_id_type=MESH)
    send_cc = pltpu.make_async_remote_copy(
        src_ref=cc_out, dst_ref=cc_low, send_sem=cond_send.at[1],
        recv_sem=cond_recv.at[1], device_id=(s, right), device_id_type=MESH)

    pl.semaphore_wait(barrier, len(greeted) + jnp.where(has_up & has_down, 2, 1))

    def start_up(copies):
        @pl.when(has_up)
        def _():
            for copy in copies():
                copy.start()

    def start_down(copies):
        @pl.when(has_down)
        def _():
            for copy in copies():
                copy.start()

    start_up(lambda: [to_up(0, 0)])
    start_down(lambda: [to_down(0, q) for q in range(RHS)])

    @pl.when(s == 0)
    def _():
        halo_low[...] = jnp.zeros_like(halo_low)
        cs_low[...] = jnp.zeros_like(cs_low)

    @pl.when(s == SLABS - 1)
    def _():
        halo_up[...] = jnp.zeros_like(halo_up)

    @pl.when(c == 0)
    def _():
        rims[:, :, 0] = jnp.zeros((ITERS, RHS, LA, 1, NC), F32)
        cc_low[...] = jnp.zeros_like(cc_low)

    @pl.when(c == CROSSES - 1)
    def _():
        rims[:, :, 1] = jnp.zeros((ITERS, RHS, LA, 1, NC), F32)

    row = lax.broadcasted_iota(jnp.int32, (8, NC), 0)
    lane = lax.broadcasted_iota(jnp.int32, (8, NC), 1)
    first_row, last_row, last_lane = row == 0, row == 7, lane == NC - 1

    def conduct(a):
        ends_slab = (s == SLABS - 1) & (a == LA - 1)
        for j in range(TILES):
            at = pl.ds(8 * j, 8)
            pressure = cap[a, at, :]
            film = 0.4 / (pressure * pressure)
            for k in range(3):
                radius = cond[k, a, at, :]
                squared = radius * radius
                value = squared * jnp.where(wet[k, a, at, :] == 1, squared, film)
                if k == 0:
                    value = jnp.where(ends_slab, 0.0, value)
                if k == 1 and j == TILES - 1:
                    value = jnp.where(last_row & (c == CROSSES - 1), 0.0, value)
                    cc_out[a] = value[7:8, :]
                if k == 2:
                    value = jnp.where(last_lane, 0.0, value)
                cond[k, a, at, :] = value

    for copy in chunk_copies(0):
        copy.wait()
    conduct(LA - 1)
    start_up(lambda: [send_cs] + [to_up(0, q) for q in range(1, RHS)])
    token[...] = jnp.zeros_like(token)
    load_b.wait()

    def pack(a, carry):
        for q in range(RHS):
            edge_low[0, q, a] = v0[q, a, 0:1, :]
            edge_up[0, q, a] = v0[q, a, LB - 1 : LB, :]
        return carry

    lax.fori_loop(0, LA, pack, 0)
    for q in range(RHS):
        to_sides(0, q)
    conduct(LA - 2)

    def chunk(i, carry):
        for copy in chunk_copies(i):
            copy.wait()
        conduct(LA - 1 - 2 * i)
        conduct(LA - 2 - 2 * i)
        return carry

    lax.fori_loop(1, CHUNKS, chunk, 0)

    @pl.when(has_right)
    def _():
        send_cc.start()

    load_sto.wait()
    dots_ref[...] = jnp.zeros_like(dots_ref)

    def stages(k):
        v, w = vectors[k], vectors[k + 1]
        last = k + 1 == ITERS
        places = ((1, 2, 0), (3, 4), (5,))[k]

        def layer(q, a, below, above, keep, dots, faces=False):
            here = v[q, a, 0:8, :]
            here_up = pltpu.roll(here, 7, 0)
            passed = jnp.zeros((8, NC), F32)
            for j in range(TILES):
                at = pl.ds(8 * j, 8)
                if j + 1 < TILES:
                    after = v[q, a, 8 * j + 8 : 8 * j + 16, :]
                    after_up = pltpu.roll(after, 7, 0)
                else:
                    after = after_up = here
                flux_cross = cond[1, a, at, :] * (jnp.where(last_row, after_up, here_up) - here)
                arrived = pltpu.roll(flux_cross, 1, 0)
                flux_depth = cond[2, a, at, :] * (pltpu.roll(here, NC - 1, 1) - here)
                higher = above(at)
                flux_slab = cond[0, a, at, :] * (higher - here)
                image = sto[a, at, :] * here
                image = image - flux_slab
                if below is not None:
                    image = image + below(at, here)
                image = image - flux_cross + jnp.where(first_row, passed, arrived)
                image = image - flux_depth + pltpu.roll(flux_depth, 1, 1)
                if keep:
                    flux[at, :] = flux_slab
                w[q, a, at, :] = image
                products = [here * image]
                if faces:
                    products[0] = products[0] + higher * flux_slab
                if k + 1 < ITERS:
                    products.append(image * image)
                if k == 0:
                    products.append(here * here)
                dots = tuple(dot + fold(product) for dot, product in zip(dots, products))
                passed, here, here_up = arrived, after, after_up
            return dots

        def interior(q, unused):
            dots = (jnp.zeros((8, 128), F32),) * len(places)
            if last:
                dots = layer(q, 0, None, lambda at: v[q, 1, at, :], True, dots)
            else:
                for j in range(TILES):
                    at = pl.ds(8 * j, 8)
                    flux[at, :] = cond[0, 0, at, :] * (v[q, 1, at, :] - v[q, 0, at, :])
            dots = lax.fori_loop(
                1, LA - 1,
                lambda a, carry: layer(
                    q, a, lambda at, here: flux[at, :], lambda at: v[q, a + 1, at, :], True, carry),
                dots)
            for place, dot in zip(places, dots):
                dots_ref[q, place] = dot
            return unused

        def rim_first(q, a, line):
            low = edge_low[k, q, a]
            enters = cc_low[a] * (low - rims[k, q, 0, a])
            old = w[q, a, 0:1, :]
            new = old + enters
            w[q, a, 0:1, :] = new
            if last:
                return (line[0] + fold(low * enters),)
            edge_low[k + 1, q, a] = new
            return line[0] + fold(low * enters), line[1] + fold(enters * (old + new))

        def rim_last(q, a, line):
            high = edge_up[k, q, a]
            leaves = cc_out[a] * (rims[k, q, 1, a] - high)
            old = w[q, a, LB - 1 : LB, :]
            new = old - leaves
            w[q, a, LB - 1 : LB, :] = new
            if last:
                return (line[0] - fold(high * leaves),)
            edge_up[k + 1, q, a] = new
            return line[0] - fold(high * leaves), line[1] - fold(leaves * (old + new))

        def below_top(q):
            return lambda at, here: cond[0, LA - 2, at, :] * (here - v[q, LA - 2, at, :])

        def below_bottom(q):
            return lambda at, here: cs_low[at, :] * (here - halo_low[k, q, at, :])

        def only_first(q, there, wait):
            if k == 0:
                @pl.when((q == 0) & there)
                def _():
                    wait()

        def both_rims(q, a, line):
            return rim_last(q, a, rim_first(q, a, line))

        def no_dots():
            return (
                (jnp.zeros((8, 128), F32),) * len(places),
                (jnp.zeros((1, 128), F32),) * min(2, len(places)),
            )

        def add_dots(q, dots, line):
            for i, (place, dot) in enumerate(zip(places, dots)):
                dots_ref[q, place] = dots_ref[q, place] + dot
                if i < len(line):
                    dots_ref[q, place, 0:1, :] = dots_ref[q, place, 0:1, :] + line[i]

        def top(q):
            dots, line = no_dots()
            @pl.when(has_up)
            def _():
                to_down(k, q).wait_recv()

            dots = layer(
                q, LA - 1, below_top(q), lambda at: halo_up[k, q, at, :], False, dots, last)
            line = both_rims(q, LA - 1, line)
            if not last:
                start_up(lambda: [to_up(k + 1, q)])
            add_dots(q, dots, line)

        def bottom(q):
            dots, line = no_dots()

            @pl.when(has_down)
            def _():
                to_up(k, q).wait_recv()

            only_first(q, has_down, lambda: send_cs.wait_recv())
            dots = layer(q, 0, below_bottom(q), lambda at: v[q, 1, at, :], False, dots)
            line = both_rims(q, 0, line)
            start_down(lambda: [to_down(k + 1, q)])
            add_dots(q, dots, line)

        def inner_rims(q, low):
            line = lax.fori_loop(
                low, LA - 1, lambda a, carry: both_rims(q, a, carry), no_dots()[1])
            add_dots(q, no_dots()[0], line)

        def border(q, unused):
            wait_sides(k, q)
            only_first(q, has_left, lambda: send_cc.wait_recv())
            if last:
                inner_rims(q, 0)
                top(q)
                return unused

            @pl.when(core == 0)
            def _():
                bottom(q)
                top(q)

            @pl.when(core == 1)
            def _():
                top(q)
                bottom(q)

            inner_rims(q, 1)
            to_sides(k + 1, q)
            return unused

        return interior, border

    def step(index, group):
        for i, peer in enumerate(group):
            pltpu.make_async_remote_copy(
                src_ref=token, dst_ref=met.at[index, i], send_sem=meet_send.at[index],
                recv_sem=meet_recv.at[index], device_id=peer, device_id_type=MESH).start()

    step(0, along_z)
    interior, border = stages(0)
    lax.fori_loop(0, RHS, interior, 0)
    wait_for(met.at[0], meet_recv.at[0])
    step(1, along_y)
    for k in range(1, ITERS):
        next_interior, next_border = stages(k)

        def both(q, unused, border=border, interior=next_interior):
            border(q, unused)
            return interior(q, unused)

        lax.fori_loop(0, RHS, both, 0)
        border = next_border
        if k == 1:
            wait_for(met.at[1], meet_recv.at[1])
            step(2, along_x)
        else:
            wait_for(met.at[2], meet_recv.at[2])

    def sample_products(q, unused):
        def line(a, sums):
            for j in range(1, TILES - 1):
                at = pl.ds(8 * j, 8)
                t = [vector[q, a, at, :] for vector in vectors]
                sums = tuple(
                    total + fold(t[i] * t[l]) for total, (i, l) in zip(sums, PAIRS))
            return sums

        sums = lax.fori_loop(2, LA - 2, line, (jnp.zeros((8, 128), F32),) * len(PAIRS))
        for place, total in enumerate(sums):
            dots_ref[q, MOMENTS + place] = total
        return unused

    lax.fori_loop(0, RHS, sample_products, 0)

    rows = lax.broadcasted_iota(jnp.int32, (8, 128), 0)
    lanes = lax.broadcasted_iota(jnp.int32, (8, 128), 1)

    def lane_sums(tiles, target):
        stacked = jnp.concatenate(
            [jnp.sum(tile, axis=0, keepdims=True) for tile in tiles], axis=0)
        spread = jnp.broadcast_to(jnp.sum(stacked, axis=1, keepdims=True), (8, 128))
        return jnp.where(lanes == target, spread, 0.0)

    early = jnp.zeros((8, 128), F32)
    for q in range(RHS):
        tiles = [dots_ref[q, j] for j in range(LANES) if j != MOMENTS - 1]
        tiles.append(jnp.zeros((8, 128), F32))
        early = early + lane_sums(tiles[:8], LANES * q + rows + jnp.where(rows >= 5, 1, 0))
        early = early + lane_sums(tiles[8:], LANES * q + rows + 9)
    early_sum[...] = early

    lax.fori_loop(0, RHS, border, 0)

    late = [dots_ref[min(q, RHS - 1), MOMENTS - 1] for q in range(8)]
    packed = early_sum[...] + jnp.where(
        rows < RHS, lane_sums(late, LANES * rows + MOMENTS - 1), 0.0)
    own = jnp.sum(packed, axis=0, keepdims=True)

    chip = (row_y * 4 + col_z) * 4 + c
    sent[...] = own
    for dy, dz, dx in CHIP_OFFSETS:
        slab = lax.rem(row_y + dy, 4) * 8 + lax.rem(col_z + dz, 4) * 2 + core
        pltpu.make_async_remote_copy(
            src_ref=sent, dst_ref=got.at[chip], send_sem=sum_send.at[0],
            recv_sem=sum_recv.at[0], device_id=(slab, lax.rem(c + dx, 4)),
            device_id_type=MESH).start()
    got[chip] = own

    def complete(q, unused):
        @pl.when(has_down)
        def _():
            to_up(ITERS - 1, q).wait_recv()

        for j in range(TILES):
            at = pl.ds(8 * j, 8)
            v3[q, 0, at, :] = v3[q, 0, at, :] + cs_low[at, :] * (
                v2[q, 0, at, :] - halo_low[ITERS - 1, q, at, :])
        return unused

    lax.fori_loop(0, RHS, complete, 0)

    @pl.when(has_down)
    def _():
        wait_for(halo_up, halo_send.at[0])

    @pl.when(has_up)
    def _():
        wait_for(halo_low, halo_send.at[1])
        send_cs.wait_send()

    @pl.when(has_left)
    def _():
        wait_for(edge_low, halo_send.at[2])

    @pl.when(has_right)
    def _():
        wait_for(edge_up, halo_send.at[3])
        send_cc.wait_send()

    for index in range(3):
        wait_for(met.at[index], meet_send.at[index])

    others = got.at[pl.ds(0, len(CHIP_OFFSETS))]
    wait_for(others, sum_recv.at[0])
    terms = [got[i] for i in range(len(CHIP_OFFSETS) + 1)]
    while len(terms) > 1:
        terms = [terms[i] + terms[i + 1] for i in range(0, len(terms), 2)]
    pair_sent[...] = terms[0]
    pair = pltpu.make_async_remote_copy(
        src_ref=pair_sent, dst_ref=pair_got, send_sem=sum_send.at[1], recv_sem=sum_recv.at[1],
        device_id=(s + 1 - 2 * core, c), device_id_type=MESH)
    pair.start()
    wait_for(others, sum_send.at[0])
    pair.wait_recv()
    own = terms[0] + pair_got[...]

    summed = jnp.broadcast_to(own, (8, 128))
    used = (lanes % LANES == 0) & (lanes < LANES * RHS)
    stand_in = (1.0, 1.0, 2.0, 6.0, 24.0, 120.0) + (1.0,) * len(PAIRS)
    m = [
        jnp.where(used, pltpu.roll(summed, 128 - j, 1) if j else summed, stand_in[j])
        for j in range(LANES)
    ]
    coefs, sound = scalars_of(m[:MOMENTS], m[MOMENTS:])
    sound = sound | ~used
    for i, coef in enumerate(coefs):
        coef_ref[i : i + 1, :] = coef[0:1, :]
    coef_ref[6:8, :] = jnp.zeros((2, 128), F32)
    sound_ref[...] = jnp.min(jnp.where(sound, 1, 0), axis=1, keepdims=True)[0:1, :]

    pair.wait_send()


def combine_kernel(coef, v0, v1, v2, v3, x_hbm, r_hbm, x, r, sem):
    part = 2
    copies = []
    for q in range(RHS):
        x0, x1, x2, d1, d2, d3 = (coef[i, LANES * q] for i in range(6))

        def layer(a, carry):
            for j in range(TILES):
                at = pl.ds(8 * j, 8)
                t0, t1, t2, t3 = (v[q, a, at, :] for v in (v0, v1, v2, v3))
                x[q, a, at, :] = x0 * t0 + x1 * t1 + x2 * t2
                r[q, a, at, :] = t0 + d1 * t1 + d2 * t2 + d3 * t3
            return carry

        for h in range(LA // part):
            lax.fori_loop(h * part, (h + 1) * part, layer, 0)
            layers = pl.ds(h * part, part)
            for index, (source, target) in enumerate(((x, x_hbm), (r, r_hbm))):
                copy = pltpu.make_async_copy(
                    source.at[q, layers], target.at[q, layers], sem.at[q, h, index])
                copy.start()
                copies.append(copy)
    for copy in copies:
        copy.wait()


def per_device(pressure_drive, throat_radius, wet_flag, cap_pressure, storage):
    field = (RHS, LA, LB, NC)
    vmem = functools.partial(pltpu.VMEM, dtype=F32)
    in_vmem = pl.BlockSpec(memory_space=pltpu.VMEM)
    anywhere = pl.BlockSpec(memory_space=pl.ANY)
    *vectors, coefs, sound = pl.pallas_call(
        powers_kernel,
        out_shape=[pltpu.VMEM(field, F32)] * 4
        + [jax.ShapeDtypeStruct((8, 128), F32), jax.ShapeDtypeStruct((1, 1), jnp.int32)],
        in_specs=[anywhere] * 5,
        out_specs=[in_vmem] * 6,
        scratch_shapes=[
            vmem(field),
            pltpu.VMEM(field, jnp.int32),
            vmem((LA, LB, NC)),
            vmem((LA, LB, NC)),
            vmem((LB, NC)),
            vmem((LA, 1, NC)),
            vmem((LA, 1, NC)),
            vmem((ITERS, RHS, LB, NC)),
            vmem((ITERS, RHS, LB, NC)),
            vmem((ITERS, RHS, LA, 1, NC)),
            vmem((ITERS, RHS, LA, 1, NC)),
            vmem((ITERS, RHS, 2, LA, 1, NC)),
            vmem((LB, NC)),
            vmem((RHS, LANES, 8, 128)),
            vmem((8, 128)),
            vmem((1, 128)),
            vmem((3, 3, 1, 128)),
            vmem((1, 128)),
            vmem((64, 1, 128)),
            vmem((1, 128)),
            vmem((1, 128)),
            pltpu.SemaphoreType.DMA((2,)),
            pltpu.SemaphoreType.DMA((CHUNKS, 3)),
            pltpu.SemaphoreType.DMA((4,)),
            pltpu.SemaphoreType.DMA((ITERS, RHS, 3)),
            pltpu.SemaphoreType.DMA((2,)),
            pltpu.SemaphoreType.DMA((2,)),
            pltpu.SemaphoreType.DMA((3,)),
            pltpu.SemaphoreType.DMA((3,)),
            pltpu.SemaphoreType.DMA((2,)),
            pltpu.SemaphoreType.DMA((2,)),
        ],
        compiler_params=pltpu.CompilerParams(
            collective_id=0, has_side_effects=True, vmem_limit_bytes=34 << 20
        ),
        name="powers",
    )(pressure_drive, throat_radius, wet_flag, cap_pressure, storage)
    fast = pl.pallas_call(
        combine_kernel,
        out_shape=[jax.ShapeDtypeStruct(field, F32)] * 2,
        in_specs=[pl.BlockSpec(memory_space=pltpu.SMEM)] + [in_vmem] * 4,
        out_specs=[anywhere] * 2,
        scratch_shapes=[vmem(field), vmem(field), pltpu.SemaphoreType.DMA((RHS, 4, 2))],
        compiler_params=pltpu.CompilerParams(vmem_limit_bytes=24 << 20),
        name="combine",
    )(coefs, *vectors)
    return lax.cond(
        sound[0, 0] == 1,
        lambda: tuple(fast),
        lambda: plain_iteration(pressure_drive, throat_radius, wet_flag, cap_pressure, storage),
    )


def solution(mesh):
    in_specs = (
        P(None, "slab", "cross", None),
        P(None, "slab", "cross", None),
        P(None, "slab", "cross", None),
        P("slab", "cross", None),
        P("slab", "cross", None),
    )
    out_specs = (P(None, "slab", "cross", None), P(None, "slab", "cross", None))
    return jax.shard_map(
        per_device, mesh=mesh, in_specs=in_specs, out_specs=out_specs, check_vma=False
    )
```

```python
import functools

import jax
import jax.numpy as jnp
from jax import lax
from jax.experimental import pallas as pl
from jax.experimental.pallas import tpu as pltpu
from jax.sharding import PartitionSpec as P

ITERS = 3
RHS = 3
F32 = jnp.float32
MESH = pl.DeviceIdType.MESH
SLABS, CROSSES = 32, 4
LA, LB, NC = 8, 64, 512
TILES = LB // 8
CHUNKS = LA // 2
CHIP_OFFSETS = sorted(
    [(y, z, x) for y in range(4) for z in range(4) for x in range(4) if x or y or z],
    key=lambda offset: -sum(min(step, 4 - step) for step in offset),
)
ERROR_GAIN_MAX = 3000.0
CANCEL_MAX = 150.0
MOMENTS = 6
PAIRS = [(i, j) for i in range(4) for j in range(i, 4)]
LANES = MOMENTS + len(PAIRS)


def shifted(value, axis, steps):
    count = lax.axis_size(axis)
    leading, last = (max(0, -steps), min(count, count - steps))
    return lax.ppermute(value, axis, [(source, source + steps) for source in range(leading, last)])


def with_halo(cells, sides, width):
    for axis, dim in sides:
        count = lax.axis_size(axis)
        ends = count - 1
        head = lax.slice_in_dim(cells, 0, width, axis=dim)
        tail = lax.slice_in_dim(cells, cells.shape[dim] - width, cells.shape[dim], axis=dim)
        cells = jnp.concatenate(
            [
                lax.ppermute(tail, axis, [(i, (i + 1) % count) for i in range(ends)]),
                cells,
                lax.ppermute(head, axis, [((i + 1) % count, i) for i in range(ends)]),
            ],
            axis=dim,
        )
    return cells


def totals(values):
    return jnp.sum(values, axis=(1, 2, 3))


def widen(scalars):
    return scalars[:, None, None, None]


def squares(residual):
    return lax.psum(totals(residual * residual), ("slab", "cross"))


def depth_terms(vector, along_depth, lower_depth):
    upper_values = jnp.pad(vector[..., 1:], ((0, 0), (0, 0), (0, 0), (0, 1)))
    lower_values = jnp.pad(vector[..., :-1], ((0, 0), (0, 0), (0, 0), (1, 0)))
    return along_depth * (vector - upper_values) + lower_depth * (vector - lower_values)


def plain_iteration(pressure_drive, throat_radius, wet_flag, cap_pressure, storage):
    squared = throat_radius * throat_radius
    film_term = 0.4 * squared / (cap_pressure * cap_pressure)[None]
    conduct = jnp.where(wet_flag == 1, squared * squared, film_term)
    extent = conduct.shape[1:]
    layer_slab = lax.broadcasted_iota(jnp.int32, extent, 0)
    layer_cross = lax.broadcasted_iota(jnp.int32, extent, 1)
    layer_depth = lax.broadcasted_iota(jnp.int32, extent, 2)
    edge_slab = (layer_slab == extent[0] - 1) & (
        lax.axis_index("slab") == lax.axis_size("slab") - 1
    )
    edge_cross = (layer_cross == extent[1] - 1) & (
        lax.axis_index("cross") == lax.axis_size("cross") - 1
    )
    along_slab = jnp.where(edge_slab, 0.0, conduct[0])
    along_cross = jnp.where(edge_cross, 0.0, conduct[1])
    along_depth = jnp.where(layer_depth == extent[2] - 1, 0.0, conduct[2])
    lower_depth = jnp.pad(along_depth[:, :, :-1], ((0, 0), (0, 0), (1, 0)))
    rim_slab = shifted(along_slab[-1:], "slab", 1)
    rim_cross = shifted(along_cross[:, -1:], "cross", 1)
    lower_slab = jnp.concatenate([rim_slab, along_slab[:-1]], 0)
    lower_cross = jnp.concatenate([rim_cross, along_cross[:, :-1]], 1)
    solution = jnp.zeros_like(pressure_drive)
    residual = pressure_drive
    direction = pressure_drive
    norm_now = squares(residual)
    for iteration in range(ITERS):
        padded = with_halo(direction, (("slab", 1), ("cross", 2)), 1)
        result = storage * direction
        result = result + along_slab * (direction - padded[:, 2:, 1:-1])
        result = result + lower_slab * (direction - padded[:, :-2, 1:-1])
        result = result + along_cross * (direction - padded[:, 1:-1, 2:])
        result = result + lower_cross * (direction - padded[:, 1:-1, :-2])
        applied = result + depth_terms(direction, along_depth, lower_depth)
        step_size = norm_now / lax.psum(totals(direction * applied), ("slab", "cross"))
        solution = solution + widen(step_size) * direction
        residual = residual - widen(step_size) * applied
        if iteration + 1 < ITERS:
            norm_next = squares(residual)
            direction = residual + widen(norm_next / norm_now) * direction
            norm_now = norm_next
    return (solution, residual)


def scalars_of(m, sample):
    def parts(c0, c1, c2, first):
        return (
            c0 * c0 * m[first],
            2.0 * c0 * c1 * m[first + 1],
            c1 * c1 * m[first + 2],
            2.0 * c0 * c2 * m[first + 2],
            2.0 * c1 * c2 * m[first + 3],
            c2 * c2 * m[first + 4],
        )

    def total(terms):
        return (terms[0] + terms[1]) + (terms[2] + terms[3]) + (terms[4] + terms[5])

    rr0 = m[0]
    step0 = m[0] / m[1]
    image0 = step0 * step0 * m[2]
    rr1 = image0 - rr0
    turn0 = rr1 / rr0
    p0, p1 = 1.0 + turn0, -step0

    def pair(first):
        return p0 * p0 * m[first], 2.0 * p0 * p1 * m[first + 1], p1 * p1 * m[first + 2]

    energy1 = pair(1)
    curve1 = energy1[0] + energy1[1] + energy1[2]
    step1 = rr1 / curve1
    image1 = pair(2)
    rr2 = step1 * step1 * (image1[0] + image1[1] + image1[2]) - rr1
    turn1 = rr2 / rr1
    r1, r2 = -step0 - step1 * p0, -step1 * p1
    q0, q1, q2 = 1.0 + turn1 * p0, r1 + turn1 * p1, r2
    energy2 = parts(q0, q1, q2, 1)
    curve2 = total(energy2)
    step2 = rr2 / curve2
    x0 = step0 + step1 * p0 + step2 * q0
    x1 = step1 * p1 + step2 * q1
    x2 = step2 * q2
    d1, d2, d3 = r1 - step2 * q0, r2 - step2 * q1, -step2 * q2

    d = (1.0, d1, d2, d3)
    rr3 = 0.0
    for products, (i, j) in zip(sample, PAIRS):
        rr3 = rr3 + (1.0 if i == j else 2.0) * d[i] * d[j] * products
    gain1 = (image0 + rr0) / rr1
    gain2 = (energy1[0] + jnp.abs(energy1[1]) + energy1[2]) / curve1
    gain3 = (step1 * step1 * (image1[0] + jnp.abs(image1[1]) + image1[2]) + rr1) / rr2
    gain4 = total([jnp.abs(term) for term in energy2]) / curve2
    gain = (
        (gain1 + gain2) * jnp.sqrt(rr0 / rr3)
        + gain3 * jnp.sqrt(rr1 / rr3)
        + gain4 * jnp.sqrt((rr2 + rr3) / rr3)
    )
    cancel = (
        jnp.sqrt(m[0]) + jnp.abs(d1) * jnp.sqrt(m[2]) + jnp.abs(d2) * jnp.sqrt(m[4])
    ) / jnp.sqrt(rr3)
    sound = (
        (rr1 > 0.0)
        & (curve1 > 0.0)
        & (rr2 > 0.0)
        & (curve2 > 0.0)
        & (rr3 > 0.0)
        & (gain < ERROR_GAIN_MAX)
        & (cancel < CANCEL_MAX)
    )
    return (x0, x1, x2, d1, d2, d3), sound


def fold(value):
    return (value[:, 0:128] + value[:, 128:256]) + (value[:, 256:384] + value[:, 384:512])


def powers_kernel(
    b_hbm, rad_hbm, wet_hbm, cap_hbm, sto_hbm,
    v0, v1, v2, v3, coef_ref, sound_ref,
    cond, wet, cap, sto, cs_low, cc_out, cc_low,
    halo_low, halo_up, edge_low, edge_up, rims,
    flux, dots_ref, early_sum, token, met, sent, got, pair_sent, pair_got,
    load_sem, chunk_sem, halo_send, halo_recv, cond_send, cond_recv, meet_send, meet_recv,
    sum_send, sum_recv,
):
    s, c = lax.axis_index("slab"), lax.axis_index("cross")
    has_up, has_down = s < SLABS - 1, s > 0
    has_right, has_left = c < CROSSES - 1, c > 0
    up, down = jnp.where(has_up, s + 1, s - 1), jnp.where(has_down, s - 1, s + 1)
    right, left = jnp.where(has_right, c + 1, c - 1), jnp.where(has_left, c - 1, c + 1)
    row_y = s // 8
    col_z, core = lax.rem(s // 2, 4), lax.rem(s, 2)
    along_z = [(row_y * 8 + lax.rem(col_z + i, 4) * 2 + core, c) for i in range(1, 4)]
    along_y = [(lax.rem(row_y + i, 4) * 8 + lax.rem(s, 8), c) for i in range(1, 4)]
    along_x = [(s, lax.rem(c + i, 4)) for i in range(1, 4)]
    barrier = pltpu.get_barrier_semaphore()
    greeted = along_x + along_z + along_y
    for peer in greeted:
        pl.semaphore_signal(barrier, inc=1, device_id=peer, device_id_type=MESH)
    for there, peer in ((has_up, up), (has_down, down)):
        @pl.when(there)
        def _(peer=peer):
            pl.semaphore_signal(barrier, inc=1, device_id=(peer, c), device_id_type=MESH)

    def chunk_copies(i):
        layers = pl.ds(LA - 2 - 2 * i, 2)
        return (
            pltpu.make_async_copy(rad_hbm.at[:, layers], cond.at[:, layers], chunk_sem.at[i, 0]),
            pltpu.make_async_copy(wet_hbm.at[:, layers], wet.at[:, layers], chunk_sem.at[i, 1]),
            pltpu.make_async_copy(cap_hbm.at[layers], cap.at[layers], chunk_sem.at[i, 2]),
        )

    load_b = pltpu.make_async_copy(b_hbm, v0, load_sem.at[0])
    load_sto = pltpu.make_async_copy(sto_hbm, sto, load_sem.at[1])
    for i in range(CHUNKS):
        for copy in chunk_copies(i):
            copy.start()
        if i == 0:
            load_b.start()
    load_sto.start()

    vectors = (v0, v1, v2, v3)

    def send(src, dst, direction, arrival, device):
        return pltpu.make_async_remote_copy(
            src_ref=src, dst_ref=dst, send_sem=halo_send.at[direction], recv_sem=arrival,
            device_id=device, device_id_type=MESH)

    def to_down(k, q):
        src = b_hbm if k == 0 else vectors[k]
        return send(src.at[q, 0], halo_up.at[k, q], 0, halo_recv.at[k, q, 0], (down, c))

    def to_up(k, q):
        src = b_hbm if k == 0 else vectors[k]
        return send(src.at[q, LA - 1], halo_low.at[k, q], 1, halo_recv.at[k, q, 1], (up, c))

    def to_sides(k, q):
        arrival = halo_recv.at[k, q, 2]

        @pl.when(has_left)
        def _():
            send(edge_low.at[k, q], rims.at[k, q, 1], 2, arrival, (s, left)).start()

        @pl.when(has_right)
        def _():
            send(edge_up.at[k, q], rims.at[k, q, 0], 3, arrival, (s, right)).start()

    def wait_sides(k, q):
        arrival = halo_recv.at[k, q, 2]

        @pl.when(has_left & has_right)
        def _():
            wait_for(rims.at[k, q], arrival)

        @pl.when(jnp.logical_not(has_left & has_right))
        def _():
            wait_for(rims.at[k, q, 0], arrival)

    def wait_for(whole, sem):
        pltpu.make_async_copy(whole, whole, sem).wait()

    send_cs = pltpu.make_async_remote_copy(
        src_ref=cond.at[0, LA - 1], dst_ref=cs_low, send_sem=cond_send.at[0],
        recv_sem=cond_recv.at[0], device_id=(up, c), device_id_type=MESH)
    send_cc = pltpu.make_async_remote_copy(
        src_ref=cc_out, dst_ref=cc_low, send_sem=cond_send.at[1],
        recv_sem=cond_recv.at[1], device_id=(s, right), device_id_type=MESH)

    pl.semaphore_wait(barrier, len(greeted) + jnp.where(has_up & has_down, 2, 1))

    def start_up(copies):
        @pl.when(has_up)
        def _():
            for copy in copies():
                copy.start()

    def start_down(copies):
        @pl.when(has_down)
        def _():
            for copy in copies():
                copy.start()

    start_up(lambda: [to_up(0, 0)])
    start_down(lambda: [to_down(0, q) for q in range(RHS)])

    @pl.when(s == 0)
    def _():
        halo_low[...] = jnp.zeros_like(halo_low)
        cs_low[...] = jnp.zeros_like(cs_low)

    @pl.when(s == SLABS - 1)
    def _():
        halo_up[...] = jnp.zeros_like(halo_up)

    @pl.when(c == 0)
    def _():
        rims[:, :, 0] = jnp.zeros((ITERS, RHS, LA, 1, NC), F32)
        cc_low[...] = jnp.zeros_like(cc_low)

    @pl.when(c == CROSSES - 1)
    def _():
        rims[:, :, 1] = jnp.zeros((ITERS, RHS, LA, 1, NC), F32)

    row = lax.broadcasted_iota(jnp.int32, (8, NC), 0)
    lane = lax.broadcasted_iota(jnp.int32, (8, NC), 1)
    first_row, last_row, last_lane = row == 0, row == 7, lane == NC - 1

    def conduct(a):
        ends_slab = (s == SLABS - 1) & (a == LA - 1)
        for j in range(TILES):
            at = pl.ds(8 * j, 8)
            pressure = cap[a, at, :]
            film = 0.4 / (pressure * pressure)
            for k in range(3):
                radius = cond[k, a, at, :]
                squared = radius * radius
                value = squared * jnp.where(wet[k, a, at, :] == 1, squared, film)
                if k == 0:
                    value = jnp.where(ends_slab, 0.0, value)
                if k == 1 and j == TILES - 1:
                    value = jnp.where(last_row & (c == CROSSES - 1), 0.0, value)
                    cc_out[a] = value[7:8, :]
                if k == 2:
                    value = jnp.where(last_lane, 0.0, value)
                cond[k, a, at, :] = value

    for copy in chunk_copies(0):
        copy.wait()
    conduct(LA - 1)
    start_up(lambda: [send_cs] + [to_up(0, q) for q in range(1, RHS)])
    token[...] = jnp.zeros_like(token)
    load_b.wait()

    def pack(a, carry):
        for q in range(RHS):
            edge_low[0, q, a] = v0[q, a, 0:1, :]
            edge_up[0, q, a] = v0[q, a, LB - 1 : LB, :]
        return carry

    lax.fori_loop(0, LA, pack, 0)
    for q in range(RHS):
        to_sides(0, q)
    conduct(LA - 2)

    def chunk(i, carry):
        for copy in chunk_copies(i):
            copy.wait()
        conduct(LA - 1 - 2 * i)
        conduct(LA - 2 - 2 * i)
        return carry

    lax.fori_loop(1, CHUNKS, chunk, 0)

    @pl.when(has_right)
    def _():
        send_cc.start()

    load_sto.wait()
    dots_ref[...] = jnp.zeros_like(dots_ref)

    def stages(k):
        v, w = vectors[k], vectors[k + 1]
        last = k + 1 == ITERS
        places = ((1, 2, 0), (3, 4), (5,))[k]

        def layer(q, a, below, above, keep, dots, faces=False):
            here = v[q, a, 0:8, :]
            here_up = pltpu.roll(here, 7, 0)
            passed = jnp.zeros((8, NC), F32)
            for j in range(TILES):
                at = pl.ds(8 * j, 8)
                if j + 1 < TILES:
                    after = v[q, a, 8 * j + 8 : 8 * j + 16, :]
                    after_up = pltpu.roll(after, 7, 0)
                else:
                    after = after_up = here
                flux_cross = cond[1, a, at, :] * (jnp.where(last_row, after_up, here_up) - here)
                arrived = pltpu.roll(flux_cross, 1, 0)
                flux_depth = cond[2, a, at, :] * (pltpu.roll(here, NC - 1, 1) - here)
                higher = above(at)
                flux_slab = cond[0, a, at, :] * (higher - here)
                image = sto[a, at, :] * here
                image = image - flux_slab
                if below is not None:
                    image = image + below(at, here)
                image = image - flux_cross + jnp.where(first_row, passed, arrived)
                image = image - flux_depth + pltpu.roll(flux_depth, 1, 1)
                if keep:
                    flux[at, :] = flux_slab
                w[q, a, at, :] = image
                products = [here * image]
                if faces:
                    products[0] = products[0] + higher * flux_slab
                if k + 1 < ITERS:
                    products.append(image * image)
                if k == 0:
                    products.append(here * here)
                dots = tuple(dot + fold(product) for dot, product in zip(dots, products))
                passed, here, here_up = arrived, after, after_up
            return dots

        def interior(q, unused):
            dots = (jnp.zeros((8, 128), F32),) * len(places)
            if last:
                dots = layer(q, 0, None, lambda at: v[q, 1, at, :], True, dots)
            else:
                for j in range(TILES):
                    at = pl.ds(8 * j, 8)
                    flux[at, :] = cond[0, 0, at, :] * (v[q, 1, at, :] - v[q, 0, at, :])
            dots = lax.fori_loop(
                1, LA - 1,
                lambda a, carry: layer(
                    q, a, lambda at, here: flux[at, :], lambda at: v[q, a + 1, at, :], True, carry),
                dots)
            for place, dot in zip(places, dots):
                dots_ref[q, place] = dot
            return unused

        def rim_first(q, a, line):
            low = edge_low[k, q, a]
            enters = cc_low[a] * (low - rims[k, q, 0, a])
            old = w[q, a, 0:1, :]
            new = old + enters
            w[q, a, 0:1, :] = new
            if last:
                return (line[0] + fold(low * enters),)
            edge_low[k + 1, q, a] = new
            return line[0] + fold(low * enters), line[1] + fold(enters * (old + new))

        def rim_last(q, a, line):
            high = edge_up[k, q, a]
            leaves = cc_out[a] * (rims[k, q, 1, a] - high)
            old = w[q, a, LB - 1 : LB, :]
            new = old - leaves
            w[q, a, LB - 1 : LB, :] = new
            if last:
                return (line[0] - fold(high * leaves),)
            edge_up[k + 1, q, a] = new
            return line[0] - fold(high * leaves), line[1] - fold(leaves * (old + new))

        def below_top(q):
            return lambda at, here: cond[0, LA - 2, at, :] * (here - v[q, LA - 2, at, :])

        def below_bottom(q):
            return lambda at, here: cs_low[at, :] * (here - halo_low[k, q, at, :])

        def only_first(q, there, wait):
            if k == 0:
                @pl.when((q == 0) & there)
                def _():
                    wait()

        def both_rims(q, a, line):
            return rim_last(q, a, rim_first(q, a, line))

        def no_dots():
            return (
                (jnp.zeros((8, 128), F32),) * len(places),
                (jnp.zeros((1, 128), F32),) * min(2, len(places)),
            )

        def add_dots(q, dots, line):
            for i, (place, dot) in enumerate(zip(places, dots)):
                dots_ref[q, place] = dots_ref[q, place] + dot
                if i < len(line):
                    dots_ref[q, place, 0:1, :] = dots_ref[q, place, 0:1, :] + line[i]

        def top(q):
            dots, line = no_dots()
            @pl.when(has_up)
            def _():
                to_down(k, q).wait_recv()

            dots = layer(
                q, LA - 1, below_top(q), lambda at: halo_up[k, q, at, :], False, dots, last)
            line = both_rims(q, LA - 1, line)
            if not last:
                start_up(lambda: [to_up(k + 1, q)])
            add_dots(q, dots, line)

        def bottom(q):
            dots, line = no_dots()

            @pl.when(has_down)
            def _():
                to_up(k, q).wait_recv()

            only_first(q, has_down, lambda: send_cs.wait_recv())
            dots = layer(q, 0, below_bottom(q), lambda at: v[q, 1, at, :], False, dots)
            line = both_rims(q, 0, line)
            start_down(lambda: [to_down(k + 1, q)])
            add_dots(q, dots, line)

        def inner_rims(q, low):
            line = lax.fori_loop(
                low, LA - 1, lambda a, carry: both_rims(q, a, carry), no_dots()[1])
            add_dots(q, no_dots()[0], line)

        def border(q, unused):
            wait_sides(k, q)
            only_first(q, has_left, lambda: send_cc.wait_recv())
            if last:
                inner_rims(q, 0)
                top(q)
                return unused

            @pl.when(core == 0)
            def _():
                bottom(q)
                top(q)

            @pl.when(core == 1)
            def _():
                top(q)
                bottom(q)

            inner_rims(q, 1)
            to_sides(k + 1, q)
            return unused

        return interior, border

    def step(index, group):
        for i, peer in enumerate(group):
            pltpu.make_async_remote_copy(
                src_ref=token, dst_ref=met.at[index, i], send_sem=meet_send.at[index],
                recv_sem=meet_recv.at[index], device_id=peer, device_id_type=MESH).start()

    step(0, along_z)
    interior, border = stages(0)
    lax.fori_loop(0, RHS, interior, 0)
    wait_for(met.at[0], meet_recv.at[0])
    step(1, along_y)
    for k in range(1, ITERS):
        next_interior, next_border = stages(k)

        def both(q, unused, border=border, interior=next_interior):
            border(q, unused)
            return interior(q, unused)

        lax.fori_loop(0, RHS, both, 0)
        border = next_border
        if k == 1:
            wait_for(met.at[1], meet_recv.at[1])
            step(2, along_x)
        else:
            wait_for(met.at[2], meet_recv.at[2])

    def sample_products(q, unused):
        def line(a, sums):
            for j in range(1, TILES - 1):
                at = pl.ds(8 * j, 8)
                t = [vector[q, a, at, :] for vector in vectors]
                sums = tuple(
                    total + fold(t[i] * t[l]) for total, (i, l) in zip(sums, PAIRS))
            return sums

        sums = lax.fori_loop(2, LA - 2, line, (jnp.zeros((8, 128), F32),) * len(PAIRS))
        for place, total in enumerate(sums):
            dots_ref[q, MOMENTS + place] = total
        return unused

    lax.fori_loop(0, RHS, sample_products, 0)

    rows = lax.broadcasted_iota(jnp.int32, (8, 128), 0)
    lanes = lax.broadcasted_iota(jnp.int32, (8, 128), 1)

    def lane_sums(tiles, target):
        stacked = jnp.concatenate(
            [jnp.sum(tile, axis=0, keepdims=True) for tile in tiles], axis=0)
        spread = jnp.broadcast_to(jnp.sum(stacked, axis=1, keepdims=True), (8, 128))
        return jnp.where(lanes == target, spread, 0.0)

    early = jnp.zeros((8, 128), F32)
    for q in range(RHS):
        tiles = [dots_ref[q, j] for j in range(LANES) if j != MOMENTS - 1]
        tiles.append(jnp.zeros((8, 128), F32))
        early = early + lane_sums(tiles[:8], LANES * q + rows + jnp.where(rows >= 5, 1, 0))
        early = early + lane_sums(tiles[8:], LANES * q + rows + 9)
    early_sum[...] = early

    lax.fori_loop(0, RHS, border, 0)

    late = [dots_ref[min(q, RHS - 1), MOMENTS - 1] for q in range(8)]
    packed = early_sum[...] + jnp.where(
        rows < RHS, lane_sums(late, LANES * rows + MOMENTS - 1), 0.0)
    own = jnp.sum(packed, axis=0, keepdims=True)

    chip = (row_y * 4 + col_z) * 4 + c
    sent[...] = own
    for dy, dz, dx in CHIP_OFFSETS:
        slab = lax.rem(row_y + dy, 4) * 8 + lax.rem(col_z + dz, 4) * 2 + core
        pltpu.make_async_remote_copy(
            src_ref=sent, dst_ref=got.at[chip], send_sem=sum_send.at[0],
            recv_sem=sum_recv.at[0], device_id=(slab, lax.rem(c + dx, 4)),
            device_id_type=MESH).start()
    got[chip] = own

    def complete(q, unused):
        @pl.when(has_down)
        def _():
            to_up(ITERS - 1, q).wait_recv()

        for j in range(TILES):
            at = pl.ds(8 * j, 8)
            v3[q, 0, at, :] = v3[q, 0, at, :] + cs_low[at, :] * (
                v2[q, 0, at, :] - halo_low[ITERS - 1, q, at, :])
        return unused

    lax.fori_loop(0, RHS, complete, 0)

    @pl.when(has_down)
    def _():
        wait_for(halo_up, halo_send.at[0])

    @pl.when(has_up)
    def _():
        wait_for(halo_low, halo_send.at[1])
        send_cs.wait_send()

    @pl.when(has_left)
    def _():
        wait_for(edge_low, halo_send.at[2])

    @pl.when(has_right)
    def _():
        wait_for(edge_up, halo_send.at[3])
        send_cc.wait_send()

    for index in range(3):
        wait_for(met.at[index], meet_send.at[index])

    others = got.at[pl.ds(0, len(CHIP_OFFSETS))]
    wait_for(others, sum_recv.at[0])
    terms = [got[i] for i in range(len(CHIP_OFFSETS) + 1)]
    while len(terms) > 1:
        terms = [terms[i] + terms[i + 1] for i in range(0, len(terms), 2)]
    pair_sent[...] = terms[0]
    pair = pltpu.make_async_remote_copy(
        src_ref=pair_sent, dst_ref=pair_got, send_sem=sum_send.at[1], recv_sem=sum_recv.at[1],
        device_id=(s + 1 - 2 * core, c), device_id_type=MESH)
    pair.start()
    wait_for(others, sum_send.at[0])
    pair.wait_recv()
    own = terms[0] + pair_got[...]

    summed = jnp.broadcast_to(own, (8, 128))
    used = (lanes % LANES == 0) & (lanes < LANES * RHS)
    stand_in = (1.0, 1.0, 2.0, 6.0, 24.0, 120.0) + (1.0,) * len(PAIRS)
    m = [
        jnp.where(used, pltpu.roll(summed, 128 - j, 1) if j else summed, stand_in[j])
        for j in range(LANES)
    ]
    coefs, sound = scalars_of(m[:MOMENTS], m[MOMENTS:])
    sound = sound | ~used
    for i, coef in enumerate(coefs):
        for q in range(RHS):
            mine = jnp.where(lanes == LANES * q, coef, 0.0)
            coef_ref[q, i] = jnp.broadcast_to(jnp.sum(mine, axis=1, keepdims=True), (8, 128))
    sound_ref[...] = jnp.min(jnp.where(sound, 1, 0), axis=1, keepdims=True)[0:1, :]

    pair.wait_send()


def combine_kernel(coef, v0, v1, v2, v3, x_hbm, r_hbm, x, r, sem):
    part = 2
    copies = []
    for q in range(RHS):
        x0, x1, x2, d1, d2, d3 = (
            jnp.concatenate([coef[q, i]] * (NC // 128), axis=1) for i in range(6))

        def layer(a, carry):
            for j in range(TILES):
                at = pl.ds(8 * j, 8)
                t0, t1, t2, t3 = (v[q, a, at, :] for v in (v0, v1, v2, v3))
                x[q, a, at, :] = x0 * t0 + x1 * t1 + x2 * t2
                r[q, a, at, :] = t0 + d1 * t1 + d2 * t2 + d3 * t3
            return carry

        for h in range(LA // part):
            lax.fori_loop(h * part, (h + 1) * part, layer, 0)
            layers = pl.ds(h * part, part)
            for index, (source, target) in enumerate(((x, x_hbm), (r, r_hbm))):
                copy = pltpu.make_async_copy(
                    source.at[q, layers], target.at[q, layers], sem.at[q, h, index])
                copy.start()
                copies.append(copy)
    for copy in copies:
        copy.wait()


def per_device(pressure_drive, throat_radius, wet_flag, cap_pressure, storage):
    field = (RHS, LA, LB, NC)
    vmem = functools.partial(pltpu.VMEM, dtype=F32)
    in_vmem = pl.BlockSpec(memory_space=pltpu.VMEM)
    anywhere = pl.BlockSpec(memory_space=pl.ANY)
    *vectors, coefs, sound = pl.pallas_call(
        powers_kernel,
        out_shape=[pltpu.VMEM(field, F32)] * 4
        + [
            pltpu.VMEM((RHS, 6, 8, 128), F32),
            jax.ShapeDtypeStruct((1, 1), jnp.int32),
        ],
        in_specs=[anywhere] * 5,
        out_specs=[in_vmem] * 6,
        scratch_shapes=[
            vmem(field),
            pltpu.VMEM(field, jnp.int32),
            vmem((LA, LB, NC)),
            vmem((LA, LB, NC)),
            vmem((LB, NC)),
            vmem((LA, 1, NC)),
            vmem((LA, 1, NC)),
            vmem((ITERS, RHS, LB, NC)),
            vmem((ITERS, RHS, LB, NC)),
            vmem((ITERS, RHS, LA, 1, NC)),
            vmem((ITERS, RHS, LA, 1, NC)),
            vmem((ITERS, RHS, 2, LA, 1, NC)),
            vmem((LB, NC)),
            vmem((RHS, LANES, 8, 128)),
            vmem((8, 128)),
            vmem((1, 128)),
            vmem((3, 3, 1, 128)),
            vmem((1, 128)),
            vmem((64, 1, 128)),
            vmem((1, 128)),
            vmem((1, 128)),
            pltpu.SemaphoreType.DMA((2,)),
            pltpu.SemaphoreType.DMA((CHUNKS, 3)),
            pltpu.SemaphoreType.DMA((4,)),
            pltpu.SemaphoreType.DMA((ITERS, RHS, 3)),
            pltpu.SemaphoreType.DMA((2,)),
            pltpu.SemaphoreType.DMA((2,)),
            pltpu.SemaphoreType.DMA((3,)),
            pltpu.SemaphoreType.DMA((3,)),
            pltpu.SemaphoreType.DMA((2,)),
            pltpu.SemaphoreType.DMA((2,)),
        ],
        compiler_params=pltpu.CompilerParams(
            collective_id=0, has_side_effects=True, vmem_limit_bytes=34 << 20
        ),
        name="powers",
    )(pressure_drive, throat_radius, wet_flag, cap_pressure, storage)
    fast = pl.pallas_call(
        combine_kernel,
        out_shape=[jax.ShapeDtypeStruct(field, F32)] * 2,
        in_specs=[in_vmem] * 5,
        out_specs=[anywhere] * 2,
        scratch_shapes=[vmem(field), vmem(field), pltpu.SemaphoreType.DMA((RHS, 4, 2))],
        compiler_params=pltpu.CompilerParams(vmem_limit_bytes=24 << 20),
        name="combine",
    )(coefs, *vectors)
    return lax.cond(
        sound[0, 0] == 1,
        lambda: tuple(fast),
        lambda: plain_iteration(pressure_drive, throat_radius, wet_flag, cap_pressure, storage),
    )


def solution(mesh):
    in_specs = (
        P(None, "slab", "cross", None),
        P(None, "slab", "cross", None),
        P(None, "slab", "cross", None),
        P("slab", "cross", None),
        P("slab", "cross", None),
    )
    out_specs = (P(None, "slab", "cross", None), P(None, "slab", "cross", None))
    return jax.shard_map(
        per_device, mesh=mesh, in_specs=in_specs, out_specs=out_specs, check_vma=False
    )
```

```python
import functools

import jax
import jax.numpy as jnp
from jax import lax
from jax.experimental import pallas as pl
from jax.experimental.pallas import tpu as pltpu
from jax.sharding import PartitionSpec as P

ITERS = 3
RHS = 3
F32 = jnp.float32
MESH = pl.DeviceIdType.MESH
SLABS, CROSSES = 32, 4
LA, LB, NC = 8, 64, 512
TILES = LB // 8
CHUNKS = LA // 2
CHIP_OFFSETS = sorted(
    [(y, z, x) for y in range(4) for z in range(4) for x in range(4) if x or y or z],
    key=lambda offset: -sum(min(step, 4 - step) for step in offset),
)
ERROR_GAIN_MAX = 3000.0
CANCEL_MAX = 150.0
MOMENTS = 6
PAIRS = [(i, j) for i in range(4) for j in range(i, 4)]
LANES = MOMENTS + len(PAIRS)


def shifted(value, axis, steps):
    count = lax.axis_size(axis)
    leading, last = (max(0, -steps), min(count, count - steps))
    return lax.ppermute(value, axis, [(source, source + steps) for source in range(leading, last)])


def with_halo(cells, sides, width):
    for axis, dim in sides:
        count = lax.axis_size(axis)
        ends = count - 1
        head = lax.slice_in_dim(cells, 0, width, axis=dim)
        tail = lax.slice_in_dim(cells, cells.shape[dim] - width, cells.shape[dim], axis=dim)
        cells = jnp.concatenate(
            [
                lax.ppermute(tail, axis, [(i, (i + 1) % count) for i in range(ends)]),
                cells,
                lax.ppermute(head, axis, [((i + 1) % count, i) for i in range(ends)]),
            ],
            axis=dim,
        )
    return cells


def totals(values):
    return jnp.sum(values, axis=(1, 2, 3))


def widen(scalars):
    return scalars[:, None, None, None]


def squares(residual):
    return lax.psum(totals(residual * residual), ("slab", "cross"))


def depth_terms(vector, along_depth, lower_depth):
    upper_values = jnp.pad(vector[..., 1:], ((0, 0), (0, 0), (0, 0), (0, 1)))
    lower_values = jnp.pad(vector[..., :-1], ((0, 0), (0, 0), (0, 0), (1, 0)))
    return along_depth * (vector - upper_values) + lower_depth * (vector - lower_values)


def plain_iteration(pressure_drive, throat_radius, wet_flag, cap_pressure, storage):
    squared = throat_radius * throat_radius
    film_term = 0.4 * squared / (cap_pressure * cap_pressure)[None]
    conduct = jnp.where(wet_flag == 1, squared * squared, film_term)
    extent = conduct.shape[1:]
    layer_slab = lax.broadcasted_iota(jnp.int32, extent, 0)
    layer_cross = lax.broadcasted_iota(jnp.int32, extent, 1)
    layer_depth = lax.broadcasted_iota(jnp.int32, extent, 2)
    edge_slab = (layer_slab == extent[0] - 1) & (
        lax.axis_index("slab") == lax.axis_size("slab") - 1
    )
    edge_cross = (layer_cross == extent[1] - 1) & (
        lax.axis_index("cross") == lax.axis_size("cross") - 1
    )
    along_slab = jnp.where(edge_slab, 0.0, conduct[0])
    along_cross = jnp.where(edge_cross, 0.0, conduct[1])
    along_depth = jnp.where(layer_depth == extent[2] - 1, 0.0, conduct[2])
    lower_depth = jnp.pad(along_depth[:, :, :-1], ((0, 0), (0, 0), (1, 0)))
    rim_slab = shifted(along_slab[-1:], "slab", 1)
    rim_cross = shifted(along_cross[:, -1:], "cross", 1)
    lower_slab = jnp.concatenate([rim_slab, along_slab[:-1]], 0)
    lower_cross = jnp.concatenate([rim_cross, along_cross[:, :-1]], 1)
    solution = jnp.zeros_like(pressure_drive)
    residual = pressure_drive
    direction = pressure_drive
    norm_now = squares(residual)
    for iteration in range(ITERS):
        padded = with_halo(direction, (("slab", 1), ("cross", 2)), 1)
        result = storage * direction
        result = result + along_slab * (direction - padded[:, 2:, 1:-1])
        result = result + lower_slab * (direction - padded[:, :-2, 1:-1])
        result = result + along_cross * (direction - padded[:, 1:-1, 2:])
        result = result + lower_cross * (direction - padded[:, 1:-1, :-2])
        applied = result + depth_terms(direction, along_depth, lower_depth)
        step_size = norm_now / lax.psum(totals(direction * applied), ("slab", "cross"))
        solution = solution + widen(step_size) * direction
        residual = residual - widen(step_size) * applied
        if iteration + 1 < ITERS:
            norm_next = squares(residual)
            direction = residual + widen(norm_next / norm_now) * direction
            norm_now = norm_next
    return (solution, residual)


def scalars_of(m, sample):
    def parts(c0, c1, c2, first):
        return (
            c0 * c0 * m[first],
            2.0 * c0 * c1 * m[first + 1],
            c1 * c1 * m[first + 2],
            2.0 * c0 * c2 * m[first + 2],
            2.0 * c1 * c2 * m[first + 3],
            c2 * c2 * m[first + 4],
        )

    def total(terms):
        return (terms[0] + terms[1]) + (terms[2] + terms[3]) + (terms[4] + terms[5])

    rr0 = m[0]
    step0 = m[0] / m[1]
    image0 = step0 * step0 * m[2]
    rr1 = image0 - rr0
    turn0 = rr1 / rr0
    p0, p1 = 1.0 + turn0, -step0

    def pair(first):
        return p0 * p0 * m[first], 2.0 * p0 * p1 * m[first + 1], p1 * p1 * m[first + 2]

    energy1 = pair(1)
    curve1 = energy1[0] + energy1[1] + energy1[2]
    step1 = rr1 / curve1
    image1 = pair(2)
    rr2 = step1 * step1 * (image1[0] + image1[1] + image1[2]) - rr1
    turn1 = rr2 / rr1
    r1, r2 = -step0 - step1 * p0, -step1 * p1
    q0, q1, q2 = 1.0 + turn1 * p0, r1 + turn1 * p1, r2
    energy2 = parts(q0, q1, q2, 1)
    curve2 = total(energy2)
    step2 = rr2 / curve2
    x0 = step0 + step1 * p0 + step2 * q0
    x1 = step1 * p1 + step2 * q1
    x2 = step2 * q2
    d1, d2, d3 = r1 - step2 * q0, r2 - step2 * q1, -step2 * q2

    d = (1.0, d1, d2, d3)
    rr3 = 0.0
    for products, (i, j) in zip(sample, PAIRS):
        rr3 = rr3 + (1.0 if i == j else 2.0) * d[i] * d[j] * products
    gain1 = (image0 + rr0) / rr1
    gain2 = (energy1[0] + jnp.abs(energy1[1]) + energy1[2]) / curve1
    gain3 = (step1 * step1 * (image1[0] + jnp.abs(image1[1]) + image1[2]) + rr1) / rr2
    gain4 = total([jnp.abs(term) for term in energy2]) / curve2
    gain = (
        (gain1 + gain2) * jnp.sqrt(rr0 / rr3)
        + gain3 * jnp.sqrt(rr1 / rr3)
        + gain4 * jnp.sqrt((rr2 + rr3) / rr3)
    )
    cancel = (
        jnp.sqrt(m[0]) + jnp.abs(d1) * jnp.sqrt(m[2]) + jnp.abs(d2) * jnp.sqrt(m[4])
    ) / jnp.sqrt(rr3)
    sound = (
        (rr1 > 0.0)
        & (curve1 > 0.0)
        & (rr2 > 0.0)
        & (curve2 > 0.0)
        & (rr3 > 0.0)
        & (gain < ERROR_GAIN_MAX)
        & (cancel < CANCEL_MAX)
    )
    return (x0, x1, x2, d1, d2, d3), sound


def fold(value):
    return (value[:, 0:128] + value[:, 128:256]) + (value[:, 256:384] + value[:, 384:512])


def powers_kernel(
    b_hbm, rad_hbm, wet_hbm, cap_hbm, sto_hbm,
    v0, v1, v2, v3, coef_ref, sound_ref,
    cond, wet, cap, sto, cs_low, cc_out, cc_low,
    halo_low, halo_up, edge_low, edge_up, rims,
    flux, dots_ref, early_sum, token, met, sent, got, pair_sent, pair_got,
    load_sem, chunk_sem, halo_send, halo_recv, cond_send, cond_recv, meet_send, meet_recv,
    sum_send, sum_recv,
):
    s, c = lax.axis_index("slab"), lax.axis_index("cross")
    has_up, has_down = s < SLABS - 1, s > 0
    has_right, has_left = c < CROSSES - 1, c > 0
    up, down = jnp.where(has_up, s + 1, s - 1), jnp.where(has_down, s - 1, s + 1)
    right, left = jnp.where(has_right, c + 1, c - 1), jnp.where(has_left, c - 1, c + 1)
    row_y = s // 8
    col_z, core = lax.rem(s // 2, 4), lax.rem(s, 2)
    along_z = [(row_y * 8 + lax.rem(col_z + i, 4) * 2 + core, c) for i in range(1, 4)]
    along_y = [(lax.rem(row_y + i, 4) * 8 + lax.rem(s, 8), c) for i in range(1, 4)]
    along_x = [(s, lax.rem(c + i, 4)) for i in range(1, 4)]
    barrier = pltpu.get_barrier_semaphore()
    greeted = along_x + along_z + along_y
    for peer in greeted:
        pl.semaphore_signal(barrier, inc=1, device_id=peer, device_id_type=MESH)
    for there, peer in ((has_up, up), (has_down, down)):
        @pl.when(there)
        def _(peer=peer):
            pl.semaphore_signal(barrier, inc=1, device_id=(peer, c), device_id_type=MESH)

    def chunk_copies(i):
        layers = pl.ds(LA - 2 - 2 * i, 2)
        return (
            pltpu.make_async_copy(rad_hbm.at[:, layers], cond.at[:, layers], chunk_sem.at[i, 0]),
            pltpu.make_async_copy(wet_hbm.at[:, layers], wet.at[:, layers], chunk_sem.at[i, 1]),
            pltpu.make_async_copy(cap_hbm.at[layers], cap.at[layers], chunk_sem.at[i, 2]),
        )

    load_b = pltpu.make_async_copy(b_hbm, v0, load_sem.at[0])
    load_sto = pltpu.make_async_copy(sto_hbm, sto, load_sem.at[1])
    for i in range(CHUNKS):
        for copy in chunk_copies(i):
            copy.start()
        if i == 0:
            load_b.start()
    load_sto.start()

    vectors = (v0, v1, v2, v3)

    def send(src, dst, direction, arrival, device):
        return pltpu.make_async_remote_copy(
            src_ref=src, dst_ref=dst, send_sem=halo_send.at[direction], recv_sem=arrival,
            device_id=device, device_id_type=MESH)

    def to_down(k, q):
        src = b_hbm if k == 0 else vectors[k]
        return send(src.at[q, 0], halo_up.at[k, q], 0, halo_recv.at[k, q, 0], (down, c))

    def to_up(k, q):
        src = b_hbm if k == 0 else vectors[k]
        return send(src.at[q, LA - 1], halo_low.at[k, q], 1, halo_recv.at[k, q, 1], (up, c))

    def to_sides(k, q):
        arrival = halo_recv.at[k, q, 2]

        @pl.when(has_left)
        def _():
            send(edge_low.at[k, q], rims.at[k, q, 1], 2, arrival, (s, left)).start()

        @pl.when(has_right)
        def _():
            send(edge_up.at[k, q], rims.at[k, q, 0], 3, arrival, (s, right)).start()

    def wait_sides(k, q):
        arrival = halo_recv.at[k, q, 2]

        @pl.when(has_left & has_right)
        def _():
            wait_for(rims.at[k, q], arrival)

        @pl.when(jnp.logical_not(has_left & has_right))
        def _():
            wait_for(rims.at[k, q, 0], arrival)

    def wait_for(whole, sem):
        pltpu.make_async_copy(whole, whole, sem).wait()

    send_cs = pltpu.make_async_remote_copy(
        src_ref=cond.at[0, LA - 1], dst_ref=cs_low, send_sem=cond_send.at[0],
        recv_sem=cond_recv.at[0], device_id=(up, c), device_id_type=MESH)
    send_cc = pltpu.make_async_remote_copy(
        src_ref=cc_out, dst_ref=cc_low, send_sem=cond_send.at[1],
        recv_sem=cond_recv.at[1], device_id=(s, right), device_id_type=MESH)

    pl.semaphore_wait(barrier, len(greeted) + jnp.where(has_up & has_down, 2, 1))

    def start_up(copies):
        @pl.when(has_up)
        def _():
            for copy in copies():
                copy.start()

    def start_down(copies):
        @pl.when(has_down)
        def _():
            for copy in copies():
                copy.start()

    start_up(lambda: [to_up(0, 0)])
    start_down(lambda: [to_down(0, q) for q in range(RHS)])

    @pl.when(s == 0)
    def _():
        halo_low[...] = jnp.zeros_like(halo_low)
        cs_low[...] = jnp.zeros_like(cs_low)

    @pl.when(s == SLABS - 1)
    def _():
        halo_up[...] = jnp.zeros_like(halo_up)

    @pl.when(c == 0)
    def _():
        rims[:, :, 0] = jnp.zeros((ITERS, RHS, LA, 1, NC), F32)
        cc_low[...] = jnp.zeros_like(cc_low)

    @pl.when(c == CROSSES - 1)
    def _():
        rims[:, :, 1] = jnp.zeros((ITERS, RHS, LA, 1, NC), F32)

    row = lax.broadcasted_iota(jnp.int32, (8, NC), 0)
    lane = lax.broadcasted_iota(jnp.int32, (8, NC), 1)
    first_row, last_row, last_lane = row == 0, row == 7, lane == NC - 1

    def conduct(a):
        ends_slab = (s == SLABS - 1) & (a == LA - 1)
        for j in range(TILES):
            at = pl.ds(8 * j, 8)
            pressure = cap[a, at, :]
            film = 0.4 / (pressure * pressure)
            for k in range(3):
                radius = cond[k, a, at, :]
                squared = radius * radius
                value = squared * jnp.where(wet[k, a, at, :] == 1, squared, film)
                if k == 0:
                    value = jnp.where(ends_slab, 0.0, value)
                if k == 1 and j == TILES - 1:
                    value = jnp.where(last_row & (c == CROSSES - 1), 0.0, value)
                    cc_out[a] = value[7:8, :]
                if k == 2:
                    value = jnp.where(last_lane, 0.0, value)
                cond[k, a, at, :] = value

    for copy in chunk_copies(0):
        copy.wait()
    conduct(LA - 1)
    start_up(lambda: [send_cs] + [to_up(0, q) for q in range(1, RHS)])
    token[...] = jnp.zeros_like(token)
    load_b.wait()

    def pack(a, carry):
        for q in range(RHS):
            edge_low[0, q, a] = v0[q, a, 0:1, :]
            edge_up[0, q, a] = v0[q, a, LB - 1 : LB, :]
        return carry

    lax.fori_loop(0, LA, pack, 0)
    for q in range(RHS):
        to_sides(0, q)
    conduct(LA - 2)

    def chunk(i, carry):
        for copy in chunk_copies(i):
            copy.wait()
        conduct(LA - 1 - 2 * i)
        conduct(LA - 2 - 2 * i)
        return carry

    lax.fori_loop(1, CHUNKS, chunk, 0)

    @pl.when(has_right)
    def _():
        send_cc.start()

    load_sto.wait()
    dots_ref[...] = jnp.zeros_like(dots_ref)

    def stages(k):
        v, w = vectors[k], vectors[k + 1]
        last = k + 1 == ITERS
        places = ((1, 2, 0), (3, 4), (5,))[k]

        def layer(q, a, below, above, dots):
            here = v[q, a, 0:8, :]
            here_up = pltpu.roll(here, 7, 0)
            passed = jnp.zeros((8, NC), F32)
            for j in range(TILES):
                at = pl.ds(8 * j, 8)
                if j + 1 < TILES:
                    after = v[q, a, 8 * j + 8 : 8 * j + 16, :]
                    after_up = pltpu.roll(after, 7, 0)
                else:
                    after = after_up = here
                flux_cross = cond[1, a, at, :] * (jnp.where(last_row, after_up, here_up) - here)
                arrived = pltpu.roll(flux_cross, 1, 0)
                flux_depth = cond[2, a, at, :] * (pltpu.roll(here, NC - 1, 1) - here)
                image = sto[a, at, :] * here
                if below:
                    image = image + flux[at, :]
                if above:
                    flux_slab = cond[0, a, at, :] * (v[q, a + 1, at, :] - here)
                    image = image - flux_slab
                    flux[at, :] = flux_slab
                image = image - flux_cross + jnp.where(first_row, passed, arrived)
                image = image - flux_depth + pltpu.roll(flux_depth, 1, 1)
                w[q, a, at, :] = image
                products = [here * image]
                if k + 1 < ITERS:
                    products.append(image * image)
                if k == 0:
                    products.append(here * here)
                dots = tuple(dot + fold(product) for dot, product in zip(dots, products))
                passed, here, here_up = arrived, after, after_up
            return dots

        def interior(q, unused):
            dots = (jnp.zeros((8, 128), F32),) * len(places)
            dots = layer(q, 0, False, True, dots)
            dots = lax.fori_loop(
                1, LA - 1, lambda a, carry: layer(q, a, True, True, carry), dots)
            dots = layer(q, LA - 1, True, False, dots)
            for place, dot in zip(places, dots):
                dots_ref[q, place] = dot
            return unused

        def rim_first(q, a, line):
            low = edge_low[k, q, a]
            enters = cc_low[a] * (low - rims[k, q, 0, a])
            old = w[q, a, 0:1, :]
            new = old + enters
            w[q, a, 0:1, :] = new
            if last:
                return (line[0] + fold(low * enters),)
            edge_low[k + 1, q, a] = new
            return line[0] + fold(low * enters), line[1] + fold(enters * (old + new))

        def rim_last(q, a, line):
            high = edge_up[k, q, a]
            leaves = cc_out[a] * (rims[k, q, 1, a] - high)
            old = w[q, a, LB - 1 : LB, :]
            new = old - leaves
            w[q, a, LB - 1 : LB, :] = new
            if last:
                return (line[0] - fold(high * leaves),)
            edge_up[k + 1, q, a] = new
            return line[0] - fold(high * leaves), line[1] - fold(leaves * (old + new))

        def only_first(q, there, wait):
            if k == 0:
                @pl.when((q == 0) & there)
                def _():
                    wait()

        def both_rims(q, a, line):
            return rim_last(q, a, rim_first(q, a, line))

        def no_dots():
            return (
                (jnp.zeros((8, 128), F32),) * len(places),
                (jnp.zeros((1, 128), F32),) * min(2, len(places)),
            )

        def add_dots(q, dots, line):
            for i, (place, dot) in enumerate(zip(places, dots)):
                dots_ref[q, place] = dots_ref[q, place] + dot
                if i < len(line):
                    dots_ref[q, place, 0:1, :] = dots_ref[q, place, 0:1, :] + line[i]

        def face(q, a, enters, energy):
            dots = (jnp.zeros((8, 128), F32),) * min(2, len(places))
            for j in range(TILES):
                at = pl.ds(8 * j, 8)
                flux_in = enters(at)
                old = w[q, a, at, :]
                new = old + flux_in
                w[q, a, at, :] = new
                dots = (dots[0] + fold(energy(at, flux_in)),) + (
                    () if last else (dots[1] + fold(flux_in * (old + new)),)
                )
                if not last and j == 0:
                    edge_low[k + 1, q, a] = new[0:1, :]
                if not last and j == TILES - 1:
                    edge_up[k + 1, q, a] = new[7:8, :]
            return dots

        def top(q):
            @pl.when(has_up)
            def _():
                to_down(k, q).wait_recv()

            a = LA - 1
            dots = face(
                q, a,
                lambda at: cond[0, a, at, :] * (v[q, a, at, :] - halo_up[k, q, at, :]),
                lambda at, flux_in: flux_in * (
                    v[q, a, at, :] - halo_up[k, q, at, :] if last else v[q, a, at, :]))
            if not last:
                start_up(lambda: [to_up(k + 1, q)])
            add_dots(q, dots, ())

        def bottom(q):
            @pl.when(has_down)
            def _():
                to_up(k, q).wait_recv()

            only_first(q, has_down, lambda: send_cs.wait_recv())
            dots = face(
                q, 0,
                lambda at: cs_low[at, :] * (v[q, 0, at, :] - halo_low[k, q, at, :]),
                lambda at, flux_in: flux_in * v[q, 0, at, :])
            start_down(lambda: [to_down(k + 1, q)])
            add_dots(q, dots, ())

        def border(q, unused):
            wait_sides(k, q)
            only_first(q, has_left, lambda: send_cc.wait_recv())
            line = lax.fori_loop(
                0, LA, lambda a, carry: both_rims(q, a, carry), no_dots()[1])
            add_dots(q, no_dots()[0], line)
            if last:
                top(q)
                return unused

            @pl.when(core == 0)
            def _():
                bottom(q)
                top(q)

            @pl.when(core == 1)
            def _():
                top(q)
                bottom(q)

            to_sides(k + 1, q)
            return unused

        return interior, border

    def step(index, group):
        for i, peer in enumerate(group):
            pltpu.make_async_remote_copy(
                src_ref=token, dst_ref=met.at[index, i], send_sem=meet_send.at[index],
                recv_sem=meet_recv.at[index], device_id=peer, device_id_type=MESH).start()

    step(0, along_z)
    interior, border = stages(0)
    lax.fori_loop(0, RHS, interior, 0)
    wait_for(met.at[0], meet_recv.at[0])
    step(1, along_y)
    for k in range(1, ITERS):
        next_interior, next_border = stages(k)

        def both(q, unused, border=border, interior=next_interior):
            border(q, unused)
            return interior(q, unused)

        lax.fori_loop(0, RHS, both, 0)
        border = next_border
        if k == 1:
            wait_for(met.at[1], meet_recv.at[1])
            step(2, along_x)
        else:
            wait_for(met.at[2], meet_recv.at[2])

    def sample_products(q, unused):
        def line(a, sums):
            for j in range(1, TILES - 1):
                at = pl.ds(8 * j, 8)
                t = [vector[q, a, at, :] for vector in vectors]
                sums = tuple(
                    total + fold(t[i] * t[l]) for total, (i, l) in zip(sums, PAIRS))
            return sums

        sums = lax.fori_loop(2, LA - 2, line, (jnp.zeros((8, 128), F32),) * len(PAIRS))
        for place, total in enumerate(sums):
            dots_ref[q, MOMENTS + place] = total
        return unused

    lax.fori_loop(0, RHS, sample_products, 0)

    rows = lax.broadcasted_iota(jnp.int32, (8, 128), 0)
    lanes = lax.broadcasted_iota(jnp.int32, (8, 128), 1)

    def lane_sums(tiles, target):
        stacked = jnp.concatenate(
            [jnp.sum(tile, axis=0, keepdims=True) for tile in tiles], axis=0)
        spread = jnp.broadcast_to(jnp.sum(stacked, axis=1, keepdims=True), (8, 128))
        return jnp.where(lanes == target, spread, 0.0)

    early = jnp.zeros((8, 128), F32)
    for q in range(RHS):
        tiles = [dots_ref[q, j] for j in range(LANES) if j != MOMENTS - 1]
        tiles.append(jnp.zeros((8, 128), F32))
        early = early + lane_sums(tiles[:8], LANES * q + rows + jnp.where(rows >= 5, 1, 0))
        early = early + lane_sums(tiles[8:], LANES * q + rows + 9)
    early_sum[...] = early

    lax.fori_loop(0, RHS, border, 0)

    late = [dots_ref[min(q, RHS - 1), MOMENTS - 1] for q in range(8)]
    packed = early_sum[...] + jnp.where(
        rows < RHS, lane_sums(late, LANES * rows + MOMENTS - 1), 0.0)
    own = jnp.sum(packed, axis=0, keepdims=True)

    chip = (row_y * 4 + col_z) * 4 + c
    sent[...] = own
    for dy, dz, dx in CHIP_OFFSETS:
        slab = lax.rem(row_y + dy, 4) * 8 + lax.rem(col_z + dz, 4) * 2 + core
        pltpu.make_async_remote_copy(
            src_ref=sent, dst_ref=got.at[chip], send_sem=sum_send.at[0],
            recv_sem=sum_recv.at[0], device_id=(slab, lax.rem(c + dx, 4)),
            device_id_type=MESH).start()
    got[chip] = own

    def complete(q, unused):
        @pl.when(has_down)
        def _():
            to_up(ITERS - 1, q).wait_recv()

        for j in range(TILES):
            at = pl.ds(8 * j, 8)
            v3[q, 0, at, :] = v3[q, 0, at, :] + cs_low[at, :] * (
                v2[q, 0, at, :] - halo_low[ITERS - 1, q, at, :])
        return unused

    lax.fori_loop(0, RHS, complete, 0)

    @pl.when(has_down)
    def _():
        wait_for(halo_up, halo_send.at[0])

    @pl.when(has_up)
    def _():
        wait_for(halo_low, halo_send.at[1])
        send_cs.wait_send()

    @pl.when(has_left)
    def _():
        wait_for(edge_low, halo_send.at[2])

    @pl.when(has_right)
    def _():
        wait_for(edge_up, halo_send.at[3])
        send_cc.wait_send()

    for index in range(3):
        wait_for(met.at[index], meet_send.at[index])

    others = got.at[pl.ds(0, len(CHIP_OFFSETS))]
    wait_for(others, sum_recv.at[0])
    terms = [got[i] for i in range(len(CHIP_OFFSETS) + 1)]
    while len(terms) > 1:
        terms = [terms[i] + terms[i + 1] for i in range(0, len(terms), 2)]
    pair_sent[...] = terms[0]
    pair = pltpu.make_async_remote_copy(
        src_ref=pair_sent, dst_ref=pair_got, send_sem=sum_send.at[1], recv_sem=sum_recv.at[1],
        device_id=(s + 1 - 2 * core, c), device_id_type=MESH)
    pair.start()
    wait_for(others, sum_send.at[0])
    pair.wait_recv()
    own = terms[0] + pair_got[...]

    summed = jnp.broadcast_to(own, (8, 128))
    used = (lanes % LANES == 0) & (lanes < LANES * RHS)
    stand_in = (1.0, 1.0, 2.0, 6.0, 24.0, 120.0) + (1.0,) * len(PAIRS)
    m = [
        jnp.where(used, pltpu.roll(summed, 128 - j, 1) if j else summed, stand_in[j])
        for j in range(LANES)
    ]
    coefs, sound = scalars_of(m[:MOMENTS], m[MOMENTS:])
    sound = sound | ~used
    for i, coef in enumerate(coefs):
        for q in range(RHS):
            mine = jnp.where(lanes == LANES * q, coef, 0.0)
            coef_ref[q, i] = jnp.broadcast_to(jnp.sum(mine, axis=1, keepdims=True), (8, 128))
    sound_ref[...] = jnp.min(jnp.where(sound, 1, 0), axis=1, keepdims=True)[0:1, :]

    pair.wait_send()


def combine_kernel(coef, v0, v1, v2, v3, x_hbm, r_hbm, x, r, sem):
    part = 2
    copies = []
    for q in range(RHS):
        x0, x1, x2, d1, d2, d3 = (
            jnp.concatenate([coef[q, i]] * (NC // 128), axis=1) for i in range(6))

        def layer(a, carry):
            for j in range(TILES):
                at = pl.ds(8 * j, 8)
                t0, t1, t2, t3 = (v[q, a, at, :] for v in (v0, v1, v2, v3))
                x[q, a, at, :] = x0 * t0 + x1 * t1 + x2 * t2
                r[q, a, at, :] = t0 + d1 * t1 + d2 * t2 + d3 * t3
            return carry

        for h in range(LA // part):
            lax.fori_loop(h * part, (h + 1) * part, layer, 0)
            layers = pl.ds(h * part, part)
            for index, (source, target) in enumerate(((x, x_hbm), (r, r_hbm))):
                copy = pltpu.make_async_copy(
                    source.at[q, layers], target.at[q, layers], sem.at[q, h, index])
                copy.start()
                copies.append(copy)
    for copy in copies:
        copy.wait()


def per_device(pressure_drive, throat_radius, wet_flag, cap_pressure, storage):
    field = (RHS, LA, LB, NC)
    vmem = functools.partial(pltpu.VMEM, dtype=F32)
    in_vmem = pl.BlockSpec(memory_space=pltpu.VMEM)
    anywhere = pl.BlockSpec(memory_space=pl.ANY)
    *vectors, coefs, sound = pl.pallas_call(
        powers_kernel,
        out_shape=[pltpu.VMEM(field, F32)] * 4
        + [
            pltpu.VMEM((RHS, 6, 8, 128), F32),
            jax.ShapeDtypeStruct((1, 1), jnp.int32),
        ],
        in_specs=[anywhere] * 5,
        out_specs=[in_vmem] * 6,
        scratch_shapes=[
            vmem(field),
            pltpu.VMEM(field, jnp.int32),
            vmem((LA, LB, NC)),
            vmem((LA, LB, NC)),
            vmem((LB, NC)),
            vmem((LA, 1, NC)),
            vmem((LA, 1, NC)),
            vmem((ITERS, RHS, LB, NC)),
            vmem((ITERS, RHS, LB, NC)),
            vmem((ITERS, RHS, LA, 1, NC)),
            vmem((ITERS, RHS, LA, 1, NC)),
            vmem((ITERS, RHS, 2, LA, 1, NC)),
            vmem((LB, NC)),
            vmem((RHS, LANES, 8, 128)),
            vmem((8, 128)),
            vmem((1, 128)),
            vmem((3, 3, 1, 128)),
            vmem((1, 128)),
            vmem((64, 1, 128)),
            vmem((1, 128)),
            vmem((1, 128)),
            pltpu.SemaphoreType.DMA((2,)),
            pltpu.SemaphoreType.DMA((CHUNKS, 3)),
            pltpu.SemaphoreType.DMA((4,)),
            pltpu.SemaphoreType.DMA((ITERS, RHS, 3)),
            pltpu.SemaphoreType.DMA((2,)),
            pltpu.SemaphoreType.DMA((2,)),
            pltpu.SemaphoreType.DMA((3,)),
            pltpu.SemaphoreType.DMA((3,)),
            pltpu.SemaphoreType.DMA((2,)),
            pltpu.SemaphoreType.DMA((2,)),
        ],
        compiler_params=pltpu.CompilerParams(
            collective_id=0, has_side_effects=True, vmem_limit_bytes=34 << 20
        ),
        name="powers",
    )(pressure_drive, throat_radius, wet_flag, cap_pressure, storage)
    fast = pl.pallas_call(
        combine_kernel,
        out_shape=[jax.ShapeDtypeStruct(field, F32)] * 2,
        in_specs=[in_vmem] * 5,
        out_specs=[anywhere] * 2,
        scratch_shapes=[vmem(field), vmem(field), pltpu.SemaphoreType.DMA((RHS, 4, 2))],
        compiler_params=pltpu.CompilerParams(vmem_limit_bytes=24 << 20),
        name="combine",
    )(coefs, *vectors)
    return lax.cond(
        sound[0, 0] == 1,
        lambda: tuple(fast),
        lambda: plain_iteration(pressure_drive, throat_radius, wet_flag, cap_pressure, storage),
    )


def solution(mesh):
    in_specs = (
        P(None, "slab", "cross", None),
        P(None, "slab", "cross", None),
        P(None, "slab", "cross", None),
        P("slab", "cross", None),
        P("slab", "cross", None),
    )
    out_specs = (P(None, "slab", "cross", None), P(None, "slab", "cross", None))
    return jax.shard_map(
        per_device, mesh=mesh, in_specs=in_specs, out_specs=out_specs, check_vma=False
    )
```

```python
import functools

import jax
import jax.numpy as jnp
from jax import lax
from jax.experimental import pallas as pl
from jax.experimental.pallas import tpu as pltpu
from jax.sharding import PartitionSpec as P

ITERS = 3
RHS = 3
F32 = jnp.float32
MESH = pl.DeviceIdType.MESH
SLABS, CROSSES = 32, 4
LA, LB, NC = 8, 64, 512
TILES = LB // 8
CHUNKS = LA // 2
OFFSETS = sorted(
    [
        (y, z, x, core)
        for y in range(4) for z in range(4) for x in range(4) for core in range(2)
        if x or y or z or core
    ],
    key=lambda offset: -sum(min(step, 4 - step) for step in offset[:3]),
)
ERROR_GAIN_MAX = 3000.0
CANCEL_MAX = 150.0
MOMENTS = 6
PAIRS = [(i, j) for i in range(4) for j in range(i, 4)]
LANES = MOMENTS + len(PAIRS)


def shifted(value, axis, steps):
    count = lax.axis_size(axis)
    leading, last = (max(0, -steps), min(count, count - steps))
    return lax.ppermute(value, axis, [(source, source + steps) for source in range(leading, last)])


def with_halo(cells, sides, width):
    for axis, dim in sides:
        count = lax.axis_size(axis)
        ends = count - 1
        head = lax.slice_in_dim(cells, 0, width, axis=dim)
        tail = lax.slice_in_dim(cells, cells.shape[dim] - width, cells.shape[dim], axis=dim)
        cells = jnp.concatenate(
            [
                lax.ppermute(tail, axis, [(i, (i + 1) % count) for i in range(ends)]),
                cells,
                lax.ppermute(head, axis, [((i + 1) % count, i) for i in range(ends)]),
            ],
            axis=dim,
        )
    return cells


def totals(values):
    return jnp.sum(values, axis=(1, 2, 3))


def widen(scalars):
    return scalars[:, None, None, None]


def squares(residual):
    return lax.psum(totals(residual * residual), ("slab", "cross"))


def depth_terms(vector, along_depth, lower_depth):
    upper_values = jnp.pad(vector[..., 1:], ((0, 0), (0, 0), (0, 0), (0, 1)))
    lower_values = jnp.pad(vector[..., :-1], ((0, 0), (0, 0), (0, 0), (1, 0)))
    return along_depth * (vector - upper_values) + lower_depth * (vector - lower_values)


def plain_iteration(pressure_drive, throat_radius, wet_flag, cap_pressure, storage):
    squared = throat_radius * throat_radius
    film_term = 0.4 * squared / (cap_pressure * cap_pressure)[None]
    conduct = jnp.where(wet_flag == 1, squared * squared, film_term)
    extent = conduct.shape[1:]
    layer_slab = lax.broadcasted_iota(jnp.int32, extent, 0)
    layer_cross = lax.broadcasted_iota(jnp.int32, extent, 1)
    layer_depth = lax.broadcasted_iota(jnp.int32, extent, 2)
    edge_slab = (layer_slab == extent[0] - 1) & (
        lax.axis_index("slab") == lax.axis_size("slab") - 1
    )
    edge_cross = (layer_cross == extent[1] - 1) & (
        lax.axis_index("cross") == lax.axis_size("cross") - 1
    )
    along_slab = jnp.where(edge_slab, 0.0, conduct[0])
    along_cross = jnp.where(edge_cross, 0.0, conduct[1])
    along_depth = jnp.where(layer_depth == extent[2] - 1, 0.0, conduct[2])
    lower_depth = jnp.pad(along_depth[:, :, :-1], ((0, 0), (0, 0), (1, 0)))
    rim_slab = shifted(along_slab[-1:], "slab", 1)
    rim_cross = shifted(along_cross[:, -1:], "cross", 1)
    lower_slab = jnp.concatenate([rim_slab, along_slab[:-1]], 0)
    lower_cross = jnp.concatenate([rim_cross, along_cross[:, :-1]], 1)
    solution = jnp.zeros_like(pressure_drive)
    residual = pressure_drive
    direction = pressure_drive
    norm_now = squares(residual)
    for iteration in range(ITERS):
        padded = with_halo(direction, (("slab", 1), ("cross", 2)), 1)
        result = storage * direction
        result = result + along_slab * (direction - padded[:, 2:, 1:-1])
        result = result + lower_slab * (direction - padded[:, :-2, 1:-1])
        result = result + along_cross * (direction - padded[:, 1:-1, 2:])
        result = result + lower_cross * (direction - padded[:, 1:-1, :-2])
        applied = result + depth_terms(direction, along_depth, lower_depth)
        step_size = norm_now / lax.psum(totals(direction * applied), ("slab", "cross"))
        solution = solution + widen(step_size) * direction
        residual = residual - widen(step_size) * applied
        if iteration + 1 < ITERS:
            norm_next = squares(residual)
            direction = residual + widen(norm_next / norm_now) * direction
            norm_now = norm_next
    return (solution, residual)


def scalars_of(m, sample):
    def parts(c0, c1, c2, first):
        return (
            c0 * c0 * m[first],
            2.0 * c0 * c1 * m[first + 1],
            c1 * c1 * m[first + 2],
            2.0 * c0 * c2 * m[first + 2],
            2.0 * c1 * c2 * m[first + 3],
            c2 * c2 * m[first + 4],
        )

    def total(terms):
        return (terms[0] + terms[1]) + (terms[2] + terms[3]) + (terms[4] + terms[5])

    rr0 = m[0]
    step0 = m[0] / m[1]
    image0 = step0 * step0 * m[2]
    rr1 = image0 - rr0
    turn0 = rr1 / rr0
    p0, p1 = 1.0 + turn0, -step0

    def pair(first):
        return p0 * p0 * m[first], 2.0 * p0 * p1 * m[first + 1], p1 * p1 * m[first + 2]

    energy1 = pair(1)
    curve1 = energy1[0] + energy1[1] + energy1[2]
    step1 = rr1 / curve1
    image1 = pair(2)
    rr2 = step1 * step1 * (image1[0] + image1[1] + image1[2]) - rr1
    turn1 = rr2 / rr1
    r1, r2 = -step0 - step1 * p0, -step1 * p1
    q0, q1, q2 = 1.0 + turn1 * p0, r1 + turn1 * p1, r2
    energy2 = parts(q0, q1, q2, 1)
    curve2 = total(energy2)
    step2 = rr2 / curve2
    x0 = step0 + step1 * p0 + step2 * q0
    x1 = step1 * p1 + step2 * q1
    x2 = step2 * q2
    d1, d2, d3 = r1 - step2 * q0, r2 - step2 * q1, -step2 * q2

    d = (1.0, d1, d2, d3)
    rr3 = 0.0
    for products, (i, j) in zip(sample, PAIRS):
        rr3 = rr3 + (1.0 if i == j else 2.0) * d[i] * d[j] * products
    gain1 = (image0 + rr0) / rr1
    gain2 = (energy1[0] + jnp.abs(energy1[1]) + energy1[2]) / curve1
    gain3 = (step1 * step1 * (image1[0] + jnp.abs(image1[1]) + image1[2]) + rr1) / rr2
    gain4 = total([jnp.abs(term) for term in energy2]) / curve2
    gain = (
        (gain1 + gain2) * jnp.sqrt(rr0 / rr3)
        + gain3 * jnp.sqrt(rr1 / rr3)
        + gain4 * jnp.sqrt((rr2 + rr3) / rr3)
    )
    cancel = (
        jnp.sqrt(m[0]) + jnp.abs(d1) * jnp.sqrt(m[2]) + jnp.abs(d2) * jnp.sqrt(m[4])
    ) / jnp.sqrt(rr3)
    sound = (
        (rr1 > 0.0)
        & (curve1 > 0.0)
        & (rr2 > 0.0)
        & (curve2 > 0.0)
        & (rr3 > 0.0)
        & (gain < ERROR_GAIN_MAX)
        & (cancel < CANCEL_MAX)
    )
    return (x0, x1, x2, d1, d2, d3), sound


def fold(value):
    return (value[:, 0:128] + value[:, 128:256]) + (value[:, 256:384] + value[:, 384:512])


def powers_kernel(
    b_hbm, rad_hbm, wet_hbm, cap_hbm, sto_hbm,
    v0, v1, v2, v3, coef_ref, sound_ref,
    cond, wet, cap, sto, cs_low, cc_out, cc_low,
    halo_low, halo_up, edge_low, edge_up, rims,
    flux, dots_ref, early_sum, token, met, sent, got,
    load_sem, chunk_sem, halo_send, halo_recv, cond_send, cond_recv, meet_send, meet_recv,
    sum_send, sum_recv,
):
    s, c = lax.axis_index("slab"), lax.axis_index("cross")
    has_up, has_down = s < SLABS - 1, s > 0
    has_right, has_left = c < CROSSES - 1, c > 0
    up, down = jnp.where(has_up, s + 1, s - 1), jnp.where(has_down, s - 1, s + 1)
    right, left = jnp.where(has_right, c + 1, c - 1), jnp.where(has_left, c - 1, c + 1)
    row_y = s // 8
    col_z, core = lax.rem(s // 2, 4), lax.rem(s, 2)
    along_z = [(row_y * 8 + lax.rem(col_z + i, 4) * 2 + core, c) for i in range(1, 4)]
    along_y = [(lax.rem(row_y + i, 4) * 8 + lax.rem(s, 8), c) for i in range(1, 4)]
    along_x = [(s, lax.rem(c + i, 4)) for i in range(1, 4)]
    barrier = pltpu.get_barrier_semaphore()
    greeted = along_x + along_z + along_y
    for peer in greeted:
        pl.semaphore_signal(barrier, inc=1, device_id=peer, device_id_type=MESH)
    for there, peer in ((has_up, up), (has_down, down)):
        @pl.when(there)
        def _(peer=peer):
            pl.semaphore_signal(barrier, inc=1, device_id=(peer, c), device_id_type=MESH)

    def chunk_copies(i):
        layers = pl.ds(LA - 2 - 2 * i, 2)
        return (
            pltpu.make_async_copy(rad_hbm.at[:, layers], cond.at[:, layers], chunk_sem.at[i, 0]),
            pltpu.make_async_copy(wet_hbm.at[:, layers], wet.at[:, layers], chunk_sem.at[i, 1]),
            pltpu.make_async_copy(cap_hbm.at[layers], cap.at[layers], chunk_sem.at[i, 2]),
        )

    load_b = pltpu.make_async_copy(b_hbm, v0, load_sem.at[0])
    load_sto = pltpu.make_async_copy(sto_hbm, sto, load_sem.at[1])
    for i in range(CHUNKS):
        for copy in chunk_copies(i):
            copy.start()
        if i == 0:
            load_b.start()
    load_sto.start()

    vectors = (v0, v1, v2, v3)

    def send(src, dst, direction, arrival, device):
        return pltpu.make_async_remote_copy(
            src_ref=src, dst_ref=dst, send_sem=halo_send.at[direction], recv_sem=arrival,
            device_id=device, device_id_type=MESH)

    def to_down(k, q):
        src = b_hbm if k == 0 else vectors[k]
        return send(src.at[q, 0], halo_up.at[k, q], 0, halo_recv.at[k, q, 0], (down, c))

    def to_up(k, q):
        src = b_hbm if k == 0 else vectors[k]
        return send(src.at[q, LA - 1], halo_low.at[k, q], 1, halo_recv.at[k, q, 1], (up, c))

    def to_sides(k, q):
        arrival = halo_recv.at[k, q, 2]

        @pl.when(has_left)
        def _():
            send(edge_low.at[k, q], rims.at[k, q, 1], 2, arrival, (s, left)).start()

        @pl.when(has_right)
        def _():
            send(edge_up.at[k, q], rims.at[k, q, 0], 3, arrival, (s, right)).start()

    def wait_sides(k, q):
        arrival = halo_recv.at[k, q, 2]

        @pl.when(has_left & has_right)
        def _():
            wait_for(rims.at[k, q], arrival)

        @pl.when(jnp.logical_not(has_left & has_right))
        def _():
            wait_for(rims.at[k, q, 0], arrival)

    def wait_for(whole, sem):
        pltpu.make_async_copy(whole, whole, sem).wait()

    send_cs = pltpu.make_async_remote_copy(
        src_ref=cond.at[0, LA - 1], dst_ref=cs_low, send_sem=cond_send.at[0],
        recv_sem=cond_recv.at[0], device_id=(up, c), device_id_type=MESH)
    send_cc = pltpu.make_async_remote_copy(
        src_ref=cc_out, dst_ref=cc_low, send_sem=cond_send.at[1],
        recv_sem=cond_recv.at[1], device_id=(s, right), device_id_type=MESH)

    pl.semaphore_wait(barrier, len(greeted) + jnp.where(has_up & has_down, 2, 1))

    def start_up(copies):
        @pl.when(has_up)
        def _():
            for copy in copies():
                copy.start()

    def start_down(copies):
        @pl.when(has_down)
        def _():
            for copy in copies():
                copy.start()

    start_up(lambda: [to_up(0, 0)])
    start_down(lambda: [to_down(0, q) for q in range(RHS)])

    @pl.when(s == 0)
    def _():
        halo_low[...] = jnp.zeros_like(halo_low)
        cs_low[...] = jnp.zeros_like(cs_low)

    @pl.when(s == SLABS - 1)
    def _():
        halo_up[...] = jnp.zeros_like(halo_up)

    @pl.when(c == 0)
    def _():
        rims[:, :, 0] = jnp.zeros((ITERS, RHS, LA, 1, NC), F32)
        cc_low[...] = jnp.zeros_like(cc_low)

    @pl.when(c == CROSSES - 1)
    def _():
        rims[:, :, 1] = jnp.zeros((ITERS, RHS, LA, 1, NC), F32)

    row = lax.broadcasted_iota(jnp.int32, (8, NC), 0)
    lane = lax.broadcasted_iota(jnp.int32, (8, NC), 1)
    first_row, last_row, last_lane = row == 0, row == 7, lane == NC - 1

    def conduct(a):
        ends_slab = (s == SLABS - 1) & (a == LA - 1)
        for j in range(TILES):
            at = pl.ds(8 * j, 8)
            pressure = cap[a, at, :]
            film = 0.4 / (pressure * pressure)
            for k in range(3):
                radius = cond[k, a, at, :]
                squared = radius * radius
                value = squared * jnp.where(wet[k, a, at, :] == 1, squared, film)
                if k == 0:
                    value = jnp.where(ends_slab, 0.0, value)
                if k == 1 and j == TILES - 1:
                    value = jnp.where(last_row & (c == CROSSES - 1), 0.0, value)
                    cc_out[a] = value[7:8, :]
                if k == 2:
                    value = jnp.where(last_lane, 0.0, value)
                cond[k, a, at, :] = value

    for copy in chunk_copies(0):
        copy.wait()
    conduct(LA - 1)
    start_up(lambda: [send_cs] + [to_up(0, q) for q in range(1, RHS)])
    token[...] = jnp.zeros_like(token)
    load_b.wait()

    def pack(a, carry):
        for q in range(RHS):
            edge_low[0, q, a] = v0[q, a, 0:1, :]
            edge_up[0, q, a] = v0[q, a, LB - 1 : LB, :]
        return carry

    lax.fori_loop(0, LA, pack, 0)
    for q in range(RHS):
        to_sides(0, q)
    conduct(LA - 2)

    def chunk(i, carry):
        for copy in chunk_copies(i):
            copy.wait()
        conduct(LA - 1 - 2 * i)
        conduct(LA - 2 - 2 * i)
        return carry

    lax.fori_loop(1, CHUNKS, chunk, 0)

    @pl.when(has_right)
    def _():
        send_cc.start()

    load_sto.wait()
    dots_ref[...] = jnp.zeros_like(dots_ref)

    def stages(k):
        v, w = vectors[k], vectors[k + 1]
        last = k + 1 == ITERS
        places = ((1, 2, 0), (3, 4), (5,))[k]

        def layer(q, a, below, above, dots):
            here = v[q, a, 0:8, :]
            here_up = pltpu.roll(here, 7, 0)
            passed = jnp.zeros((8, NC), F32)
            for j in range(TILES):
                at = pl.ds(8 * j, 8)
                if j + 1 < TILES:
                    after = v[q, a, 8 * j + 8 : 8 * j + 16, :]
                    after_up = pltpu.roll(after, 7, 0)
                else:
                    after = after_up = here
                flux_cross = cond[1, a, at, :] * (jnp.where(last_row, after_up, here_up) - here)
                arrived = pltpu.roll(flux_cross, 1, 0)
                flux_depth = cond[2, a, at, :] * (pltpu.roll(here, NC - 1, 1) - here)
                image = sto[a, at, :] * here
                if below:
                    image = image + flux[at, :]
                if above:
                    flux_slab = cond[0, a, at, :] * (v[q, a + 1, at, :] - here)
                    image = image - flux_slab
                    flux[at, :] = flux_slab
                image = image - flux_cross + jnp.where(first_row, passed, arrived)
                image = image - flux_depth + pltpu.roll(flux_depth, 1, 1)
                w[q, a, at, :] = image
                products = [here * image]
                if k + 1 < ITERS:
                    products.append(image * image)
                if k == 0:
                    products.append(here * here)
                dots = tuple(dot + fold(product) for dot, product in zip(dots, products))
                passed, here, here_up = arrived, after, after_up
            return dots

        def interior(q, unused):
            dots = (jnp.zeros((8, 128), F32),) * len(places)
            dots = layer(q, 0, False, True, dots)
            dots = lax.fori_loop(
                1, LA - 1, lambda a, carry: layer(q, a, True, True, carry), dots)
            dots = layer(q, LA - 1, True, False, dots)
            for place, dot in zip(places, dots):
                dots_ref[q, place] = dot
            return unused

        def rim_first(q, a, line):
            low = edge_low[k, q, a]
            enters = cc_low[a] * (low - rims[k, q, 0, a])
            old = w[q, a, 0:1, :]
            new = old + enters
            w[q, a, 0:1, :] = new
            if last:
                return (line[0] + fold(low * enters),)
            edge_low[k + 1, q, a] = new
            return line[0] + fold(low * enters), line[1] + fold(enters * (old + new))

        def rim_last(q, a, line):
            high = edge_up[k, q, a]
            leaves = cc_out[a] * (rims[k, q, 1, a] - high)
            old = w[q, a, LB - 1 : LB, :]
            new = old - leaves
            w[q, a, LB - 1 : LB, :] = new
            if last:
                return (line[0] - fold(high * leaves),)
            edge_up[k + 1, q, a] = new
            return line[0] - fold(high * leaves), line[1] - fold(leaves * (old + new))

        def only_first(q, there, wait):
            if k == 0:
                @pl.when((q == 0) & there)
                def _():
                    wait()

        def both_rims(q, a, line):
            return rim_last(q, a, rim_first(q, a, line))

        def no_dots():
            return (
                (jnp.zeros((8, 128), F32),) * len(places),
                (jnp.zeros((1, 128), F32),) * min(2, len(places)),
            )

        def add_dots(q, dots, line):
            for i, (place, dot) in enumerate(zip(places, dots)):
                dots_ref[q, place] = dots_ref[q, place] + dot
                if i < len(line):
                    dots_ref[q, place, 0:1, :] = dots_ref[q, place, 0:1, :] + line[i]

        def face(q, a, enters, energy):
            dots = (jnp.zeros((8, 128), F32),) * min(2, len(places))
            for j in range(TILES):
                at = pl.ds(8 * j, 8)
                flux_in = enters(at)
                old = w[q, a, at, :]
                new = old + flux_in
                w[q, a, at, :] = new
                dots = (dots[0] + fold(energy(at, flux_in)),) + (
                    () if last else (dots[1] + fold(flux_in * (old + new)),)
                )
                if not last and j == 0:
                    edge_low[k + 1, q, a] = new[0:1, :]
                if not last and j == TILES - 1:
                    edge_up[k + 1, q, a] = new[7:8, :]
            return dots

        def top(q):
            @pl.when(has_up)
            def _():
                to_down(k, q).wait_recv()

            a = LA - 1
            dots = face(
                q, a,
                lambda at: cond[0, a, at, :] * (v[q, a, at, :] - halo_up[k, q, at, :]),
                lambda at, flux_in: flux_in * (
                    v[q, a, at, :] - halo_up[k, q, at, :] if last else v[q, a, at, :]))
            if not last:
                start_up(lambda: [to_up(k + 1, q)])
            add_dots(q, dots, ())

        def bottom(q):
            @pl.when(has_down)
            def _():
                to_up(k, q).wait_recv()

            only_first(q, has_down, lambda: send_cs.wait_recv())
            dots = face(
                q, 0,
                lambda at: cs_low[at, :] * (v[q, 0, at, :] - halo_low[k, q, at, :]),
                lambda at, flux_in: flux_in * v[q, 0, at, :])
            start_down(lambda: [to_down(k + 1, q)])
            add_dots(q, dots, ())

        def border(q, unused):
            wait_sides(k, q)
            only_first(q, has_left, lambda: send_cc.wait_recv())
            line = lax.fori_loop(
                0, LA, lambda a, carry: both_rims(q, a, carry), no_dots()[1])
            add_dots(q, no_dots()[0], line)
            if last:
                top(q)
                return unused

            @pl.when(core == 0)
            def _():
                bottom(q)
                top(q)

            @pl.when(core == 1)
            def _():
                top(q)
                bottom(q)

            to_sides(k + 1, q)
            return unused

        return interior, border

    def step(index, group):
        for i, peer in enumerate(group):
            pltpu.make_async_remote_copy(
                src_ref=token, dst_ref=met.at[index, i], send_sem=meet_send.at[index],
                recv_sem=meet_recv.at[index], device_id=peer, device_id_type=MESH).start()

    step(0, along_z)
    interior, border = stages(0)
    lax.fori_loop(0, RHS, interior, 0)
    wait_for(met.at[0], meet_recv.at[0])
    step(1, along_y)
    for k in range(1, ITERS):
        next_interior, next_border = stages(k)

        def both(q, unused, border=border, interior=next_interior):
            border(q, unused)
            return interior(q, unused)

        lax.fori_loop(0, RHS, both, 0)
        border = next_border
        if k == 1:
            wait_for(met.at[1], meet_recv.at[1])
            step(2, along_x)
        else:
            wait_for(met.at[2], meet_recv.at[2])

    def sample_products(q, unused):
        def line(a, sums):
            for j in range(1, TILES - 1):
                at = pl.ds(8 * j, 8)
                t = [vector[q, a, at, :] for vector in vectors]
                sums = tuple(
                    total + fold(t[i] * t[l]) for total, (i, l) in zip(sums, PAIRS))
            return sums

        sums = lax.fori_loop(2, LA - 2, line, (jnp.zeros((8, 128), F32),) * len(PAIRS))
        for place, total in enumerate(sums):
            dots_ref[q, MOMENTS + place] = total
        return unused

    lax.fori_loop(0, RHS, sample_products, 0)

    rows = lax.broadcasted_iota(jnp.int32, (8, 128), 0)
    lanes = lax.broadcasted_iota(jnp.int32, (8, 128), 1)

    def lane_sums(tiles, target):
        stacked = jnp.concatenate(
            [jnp.sum(tile, axis=0, keepdims=True) for tile in tiles], axis=0)
        spread = jnp.broadcast_to(jnp.sum(stacked, axis=1, keepdims=True), (8, 128))
        return jnp.where(lanes == target, spread, 0.0)

    early = jnp.zeros((8, 128), F32)
    for q in range(RHS):
        tiles = [dots_ref[q, j] for j in range(LANES) if j != MOMENTS - 1]
        tiles.append(jnp.zeros((8, 128), F32))
        early = early + lane_sums(tiles[:8], LANES * q + rows + jnp.where(rows >= 5, 1, 0))
        early = early + lane_sums(tiles[8:], LANES * q + rows + 9)
    early_sum[...] = early

    lax.fori_loop(0, RHS, border, 0)

    late = [dots_ref[min(q, RHS - 1), MOMENTS - 1] for q in range(8)]
    packed = early_sum[...] + jnp.where(
        rows < RHS, lane_sums(late, LANES * rows + MOMENTS - 1), 0.0)
    own = jnp.sum(packed, axis=0, keepdims=True)

    own_place = s * CROSSES + c
    sent[...] = own
    for dy, dz, dx, other in OFFSETS:
        at_core = 1 - core if other else core
        slab = lax.rem(row_y + dy, 4) * 8 + lax.rem(col_z + dz, 4) * 2 + at_core
        pltpu.make_async_remote_copy(
            src_ref=sent, dst_ref=got.at[own_place], send_sem=sum_send.at[0],
            recv_sem=sum_recv.at[0], device_id=(slab, lax.rem(c + dx, 4)),
            device_id_type=MESH).start()
    got[own_place] = own

    def complete(q, unused):
        @pl.when(has_down)
        def _():
            to_up(ITERS - 1, q).wait_recv()

        for j in range(TILES):
            at = pl.ds(8 * j, 8)
            v3[q, 0, at, :] = v3[q, 0, at, :] + cs_low[at, :] * (
                v2[q, 0, at, :] - halo_low[ITERS - 1, q, at, :])
        return unused

    lax.fori_loop(0, RHS, complete, 0)

    @pl.when(has_down)
    def _():
        wait_for(halo_up, halo_send.at[0])

    @pl.when(has_up)
    def _():
        wait_for(halo_low, halo_send.at[1])
        send_cs.wait_send()

    @pl.when(has_left)
    def _():
        wait_for(edge_low, halo_send.at[2])

    @pl.when(has_right)
    def _():
        wait_for(edge_up, halo_send.at[3])
        send_cc.wait_send()

    for index in range(3):
        wait_for(met.at[index], meet_send.at[index])

    others = got.at[pl.ds(0, len(OFFSETS))]
    wait_for(others, sum_recv.at[0])
    terms = [got[i] for i in range(len(OFFSETS) + 1)]
    while len(terms) > 1:
        terms = [terms[i] + terms[i + 1] for i in range(0, len(terms), 2)]
    own = terms[0]
    wait_for(others, sum_send.at[0])

    summed = jnp.broadcast_to(own, (8, 128))
    used = (lanes % LANES == 0) & (lanes < LANES * RHS)
    stand_in = (1.0, 1.0, 2.0, 6.0, 24.0, 120.0) + (1.0,) * len(PAIRS)
    m = [
        jnp.where(used, pltpu.roll(summed, 128 - j, 1) if j else summed, stand_in[j])
        for j in range(LANES)
    ]
    coefs, sound = scalars_of(m[:MOMENTS], m[MOMENTS:])
    sound = sound | ~used
    for i, coef in enumerate(coefs):
        for q in range(RHS):
            mine = jnp.where(lanes == LANES * q, coef, 0.0)
            coef_ref[q, i] = jnp.broadcast_to(jnp.sum(mine, axis=1, keepdims=True), (8, 128))
    sound_ref[...] = jnp.min(jnp.where(sound, 1, 0), axis=1, keepdims=True)[0:1, :]


def combine_kernel(coef, v0, v1, v2, v3, x_hbm, r_hbm, x, r, sem):
    part = 2
    copies = []
    for q in range(RHS):
        x0, x1, x2, d1, d2, d3 = (
            jnp.concatenate([coef[q, i]] * (NC // 128), axis=1) for i in range(6))

        def layer(a, carry):
            for j in range(TILES):
                at = pl.ds(8 * j, 8)
                t0, t1, t2, t3 = (v[q, a, at, :] for v in (v0, v1, v2, v3))
                x[q, a, at, :] = x0 * t0 + x1 * t1 + x2 * t2
                r[q, a, at, :] = t0 + d1 * t1 + d2 * t2 + d3 * t3
            return carry

        for h in range(LA // part):
            lax.fori_loop(h * part, (h + 1) * part, layer, 0)
            layers = pl.ds(h * part, part)
            for index, (source, target) in enumerate(((x, x_hbm), (r, r_hbm))):
                copy = pltpu.make_async_copy(
                    source.at[q, layers], target.at[q, layers], sem.at[q, h, index])
                copy.start()
                copies.append(copy)
    for copy in copies:
        copy.wait()


def per_device(pressure_drive, throat_radius, wet_flag, cap_pressure, storage):
    field = (RHS, LA, LB, NC)
    vmem = functools.partial(pltpu.VMEM, dtype=F32)
    in_vmem = pl.BlockSpec(memory_space=pltpu.VMEM)
    anywhere = pl.BlockSpec(memory_space=pl.ANY)
    *vectors, coefs, sound = pl.pallas_call(
        powers_kernel,
        out_shape=[pltpu.VMEM(field, F32)] * 4
        + [
            pltpu.VMEM((RHS, 6, 8, 128), F32),
            jax.ShapeDtypeStruct((1, 1), jnp.int32),
        ],
        in_specs=[anywhere] * 5,
        out_specs=[in_vmem] * 6,
        scratch_shapes=[
            vmem(field),
            pltpu.VMEM(field, jnp.int32),
            vmem((LA, LB, NC)),
            vmem((LA, LB, NC)),
            vmem((LB, NC)),
            vmem((LA, 1, NC)),
            vmem((LA, 1, NC)),
            vmem((ITERS, RHS, LB, NC)),
            vmem((ITERS, RHS, LB, NC)),
            vmem((ITERS, RHS, LA, 1, NC)),
            vmem((ITERS, RHS, LA, 1, NC)),
            vmem((ITERS, RHS, 2, LA, 1, NC)),
            vmem((LB, NC)),
            vmem((RHS, LANES, 8, 128)),
            vmem((8, 128)),
            vmem((1, 128)),
            vmem((3, 3, 1, 128)),
            vmem((1, 128)),
            vmem((128, 1, 128)),
            pltpu.SemaphoreType.DMA((2,)),
            pltpu.SemaphoreType.DMA((CHUNKS, 3)),
            pltpu.SemaphoreType.DMA((4,)),
            pltpu.SemaphoreType.DMA((ITERS, RHS, 3)),
            pltpu.SemaphoreType.DMA((2,)),
            pltpu.SemaphoreType.DMA((2,)),
            pltpu.SemaphoreType.DMA((3,)),
            pltpu.SemaphoreType.DMA((3,)),
            pltpu.SemaphoreType.DMA((1,)),
            pltpu.SemaphoreType.DMA((1,)),
        ],
        compiler_params=pltpu.CompilerParams(
            collective_id=0, has_side_effects=True, vmem_limit_bytes=34 << 20
        ),
        name="powers",
    )(pressure_drive, throat_radius, wet_flag, cap_pressure, storage)
    fast = pl.pallas_call(
        combine_kernel,
        out_shape=[jax.ShapeDtypeStruct(field, F32)] * 2,
        in_specs=[in_vmem] * 5,
        out_specs=[anywhere] * 2,
        scratch_shapes=[vmem(field), vmem(field), pltpu.SemaphoreType.DMA((RHS, 4, 2))],
        compiler_params=pltpu.CompilerParams(vmem_limit_bytes=24 << 20),
        name="combine",
    )(coefs, *vectors)
    return lax.cond(
        sound[0, 0] == 1,
        lambda: tuple(fast),
        lambda: plain_iteration(pressure_drive, throat_radius, wet_flag, cap_pressure, storage),
    )


def solution(mesh):
    in_specs = (
        P(None, "slab", "cross", None),
        P(None, "slab", "cross", None),
        P(None, "slab", "cross", None),
        P("slab", "cross", None),
        P("slab", "cross", None),
    )
    out_specs = (P(None, "slab", "cross", None), P(None, "slab", "cross", None))
    return jax.shard_map(
        per_device, mesh=mesh, in_specs=in_specs, out_specs=out_specs, check_vma=False
    )
```

```python
import functools

import jax
import jax.numpy as jnp
from jax import lax
from jax.experimental import pallas as pl
from jax.experimental.pallas import tpu as pltpu
from jax.sharding import PartitionSpec as P

ITERS = 3
RHS = 3
F32 = jnp.float32
MESH = pl.DeviceIdType.MESH
SLABS, CROSSES = 32, 4
LA, LB, NC = 8, 64, 512
TILES = LB // 8
CHUNKS = LA // 2
OFFSETS = sorted(
    [
        (y, z, x, core)
        for y in range(4) for z in range(4) for x in range(4) for core in range(2)
        if x or y or z or core
    ],
    key=lambda offset: -sum(min(step, 4 - step) for step in offset[:3]),
)
ERROR_GAIN_MAX = 3000.0
CANCEL_MAX = 150.0
MOMENTS = 6
PAIRS = [(i, j) for i in range(4) for j in range(i, 4)]
LANES = MOMENTS + len(PAIRS)


def shifted(value, axis, steps):
    count = lax.axis_size(axis)
    leading, last = (max(0, -steps), min(count, count - steps))
    return lax.ppermute(value, axis, [(source, source + steps) for source in range(leading, last)])


def with_halo(cells, sides, width):
    for axis, dim in sides:
        count = lax.axis_size(axis)
        ends = count - 1
        head = lax.slice_in_dim(cells, 0, width, axis=dim)
        tail = lax.slice_in_dim(cells, cells.shape[dim] - width, cells.shape[dim], axis=dim)
        cells = jnp.concatenate(
            [
                lax.ppermute(tail, axis, [(i, (i + 1) % count) for i in range(ends)]),
                cells,
                lax.ppermute(head, axis, [((i + 1) % count, i) for i in range(ends)]),
            ],
            axis=dim,
        )
    return cells


def totals(values):
    return jnp.sum(values, axis=(1, 2, 3))


def widen(scalars):
    return scalars[:, None, None, None]


def squares(residual):
    return lax.psum(totals(residual * residual), ("slab", "cross"))


def depth_terms(vector, along_depth, lower_depth):
    upper_values = jnp.pad(vector[..., 1:], ((0, 0), (0, 0), (0, 0), (0, 1)))
    lower_values = jnp.pad(vector[..., :-1], ((0, 0), (0, 0), (0, 0), (1, 0)))
    return along_depth * (vector - upper_values) + lower_depth * (vector - lower_values)


def plain_iteration(pressure_drive, throat_radius, wet_flag, cap_pressure, storage):
    squared = throat_radius * throat_radius
    film_term = 0.4 * squared / (cap_pressure * cap_pressure)[None]
    conduct = jnp.where(wet_flag == 1, squared * squared, film_term)
    extent = conduct.shape[1:]
    layer_slab = lax.broadcasted_iota(jnp.int32, extent, 0)
    layer_cross = lax.broadcasted_iota(jnp.int32, extent, 1)
    layer_depth = lax.broadcasted_iota(jnp.int32, extent, 2)
    edge_slab = (layer_slab == extent[0] - 1) & (
        lax.axis_index("slab") == lax.axis_size("slab") - 1
    )
    edge_cross = (layer_cross == extent[1] - 1) & (
        lax.axis_index("cross") == lax.axis_size("cross") - 1
    )
    along_slab = jnp.where(edge_slab, 0.0, conduct[0])
    along_cross = jnp.where(edge_cross, 0.0, conduct[1])
    along_depth = jnp.where(layer_depth == extent[2] - 1, 0.0, conduct[2])
    lower_depth = jnp.pad(along_depth[:, :, :-1], ((0, 0), (0, 0), (1, 0)))
    rim_slab = shifted(along_slab[-1:], "slab", 1)
    rim_cross = shifted(along_cross[:, -1:], "cross", 1)
    lower_slab = jnp.concatenate([rim_slab, along_slab[:-1]], 0)
    lower_cross = jnp.concatenate([rim_cross, along_cross[:, :-1]], 1)
    solution = jnp.zeros_like(pressure_drive)
    residual = pressure_drive
    direction = pressure_drive
    norm_now = squares(residual)
    for iteration in range(ITERS):
        padded = with_halo(direction, (("slab", 1), ("cross", 2)), 1)
        result = storage * direction
        result = result + along_slab * (direction - padded[:, 2:, 1:-1])
        result = result + lower_slab * (direction - padded[:, :-2, 1:-1])
        result = result + along_cross * (direction - padded[:, 1:-1, 2:])
        result = result + lower_cross * (direction - padded[:, 1:-1, :-2])
        applied = result + depth_terms(direction, along_depth, lower_depth)
        step_size = norm_now / lax.psum(totals(direction * applied), ("slab", "cross"))
        solution = solution + widen(step_size) * direction
        residual = residual - widen(step_size) * applied
        if iteration + 1 < ITERS:
            norm_next = squares(residual)
            direction = residual + widen(norm_next / norm_now) * direction
            norm_now = norm_next
    return (solution, residual)


def scalars_of(m, sample):
    def parts(c0, c1, c2, first):
        return (
            c0 * c0 * m[first],
            2.0 * c0 * c1 * m[first + 1],
            c1 * c1 * m[first + 2],
            2.0 * c0 * c2 * m[first + 2],
            2.0 * c1 * c2 * m[first + 3],
            c2 * c2 * m[first + 4],
        )

    def total(terms):
        return (terms[0] + terms[1]) + (terms[2] + terms[3]) + (terms[4] + terms[5])

    rr0 = m[0]
    step0 = m[0] / m[1]
    image0 = step0 * step0 * m[2]
    rr1 = image0 - rr0
    turn0 = rr1 / rr0
    p0, p1 = 1.0 + turn0, -step0

    def pair(first):
        return p0 * p0 * m[first], 2.0 * p0 * p1 * m[first + 1], p1 * p1 * m[first + 2]

    energy1 = pair(1)
    curve1 = energy1[0] + energy1[1] + energy1[2]
    step1 = rr1 / curve1
    image1 = pair(2)
    rr2 = step1 * step1 * (image1[0] + image1[1] + image1[2]) - rr1
    turn1 = rr2 / rr1
    r1, r2 = -step0 - step1 * p0, -step1 * p1
    q0, q1, q2 = 1.0 + turn1 * p0, r1 + turn1 * p1, r2
    energy2 = parts(q0, q1, q2, 1)
    curve2 = total(energy2)
    step2 = rr2 / curve2
    x0 = step0 + step1 * p0 + step2 * q0
    x1 = step1 * p1 + step2 * q1
    x2 = step2 * q2
    d1, d2, d3 = r1 - step2 * q0, r2 - step2 * q1, -step2 * q2

    d = (1.0, d1, d2, d3)
    rr3 = 0.0
    for products, (i, j) in zip(sample, PAIRS):
        rr3 = rr3 + (1.0 if i == j else 2.0) * d[i] * d[j] * products
    gain1 = (image0 + rr0) / rr1
    gain2 = (energy1[0] + jnp.abs(energy1[1]) + energy1[2]) / curve1
    gain3 = (step1 * step1 * (image1[0] + jnp.abs(image1[1]) + image1[2]) + rr1) / rr2
    gain4 = total([jnp.abs(term) for term in energy2]) / curve2
    gain = (
        (gain1 + gain2) * jnp.sqrt(rr0 / rr3)
        + gain3 * jnp.sqrt(rr1 / rr3)
        + gain4 * jnp.sqrt((rr2 + rr3) / rr3)
    )
    cancel = (
        jnp.sqrt(m[0]) + jnp.abs(d1) * jnp.sqrt(m[2]) + jnp.abs(d2) * jnp.sqrt(m[4])
    ) / jnp.sqrt(rr3)
    sound = (
        (rr1 > 0.0)
        & (curve1 > 0.0)
        & (rr2 > 0.0)
        & (curve2 > 0.0)
        & (rr3 > 0.0)
        & (gain < ERROR_GAIN_MAX)
        & (cancel < CANCEL_MAX)
    )
    return (x0, x1, x2, d1, d2, d3), sound


def fold(value):
    return (value[:, 0:128] + value[:, 128:256]) + (value[:, 256:384] + value[:, 384:512])


def powers_kernel(
    b_hbm, rad_hbm, wet_hbm, cap_hbm, sto_hbm,
    v0, v1, v2, v3, coef_ref, sound_ref,
    cond, wet, cap, sto, cs_low, cc_out, cc_low,
    halo_low, halo_up, edge_low, edge_up, rims,
    flux, dots_ref, early_sum, token, met, sent, got,
    load_sem, chunk_sem, halo_send, halo_recv, cond_send, cond_recv, meet_send, meet_recv,
    sum_send, sum_recv,
):
    s, c = lax.axis_index("slab"), lax.axis_index("cross")
    has_up, has_down = s < SLABS - 1, s > 0
    has_right, has_left = c < CROSSES - 1, c > 0
    up, down = jnp.where(has_up, s + 1, s - 1), jnp.where(has_down, s - 1, s + 1)
    right, left = jnp.where(has_right, c + 1, c - 1), jnp.where(has_left, c - 1, c + 1)
    row_y = s // 8
    col_z, core = lax.rem(s // 2, 4), lax.rem(s, 2)
    along_z = [(row_y * 8 + lax.rem(col_z + i, 4) * 2 + core, c) for i in range(1, 4)]
    along_y = [(lax.rem(row_y + i, 4) * 8 + lax.rem(s, 8), c) for i in range(1, 4)]
    along_x = [(s, lax.rem(c + i, 4)) for i in range(1, 4)]
    barrier = pltpu.get_barrier_semaphore()
    greeted = along_x + along_z + along_y
    for peer in greeted:
        pl.semaphore_signal(barrier, inc=1, device_id=peer, device_id_type=MESH)
    for there, peer in ((has_up, up), (has_down, down)):
        @pl.when(there)
        def _(peer=peer):
            pl.semaphore_signal(barrier, inc=1, device_id=(peer, c), device_id_type=MESH)

    def chunk_copies(i):
        layers = pl.ds(LA - 2 - 2 * i, 2)
        return (
            pltpu.make_async_copy(rad_hbm.at[:, layers], cond.at[:, layers], chunk_sem.at[i, 0]),
            pltpu.make_async_copy(wet_hbm.at[:, layers], wet.at[:, layers], chunk_sem.at[i, 1]),
            pltpu.make_async_copy(cap_hbm.at[layers], cap.at[layers], chunk_sem.at[i, 2]),
        )

    load_b = pltpu.make_async_copy(b_hbm, v0, load_sem.at[0])
    load_sto = pltpu.make_async_copy(sto_hbm, sto, load_sem.at[1])
    for i in range(CHUNKS):
        for copy in chunk_copies(i):
            copy.start()
        if i == 0:
            load_b.start()
    load_sto.start()

    vectors = (v0, v1, v2, v3)

    def send(src, dst, direction, arrival, device):
        return pltpu.make_async_remote_copy(
            src_ref=src, dst_ref=dst, send_sem=halo_send.at[direction], recv_sem=arrival,
            device_id=device, device_id_type=MESH)

    def to_down(k, q):
        src = b_hbm if k == 0 else vectors[k]
        return send(src.at[q, 0], halo_up.at[k, q], 0, halo_recv.at[k, q, 0], (down, c))

    def to_up(k, q):
        src = b_hbm if k == 0 else vectors[k]
        return send(src.at[q, LA - 1], halo_low.at[k, q], 1, halo_recv.at[k, q, 1], (up, c))

    def to_sides(k, q):
        arrival = halo_recv.at[k, q, 2]

        @pl.when(has_left)
        def _():
            send(edge_low.at[k, q], rims.at[k, q, 1], 2, arrival, (s, left)).start()

        @pl.when(has_right)
        def _():
            send(edge_up.at[k, q], rims.at[k, q, 0], 3, arrival, (s, right)).start()

    def wait_sides(k, q):
        arrival = halo_recv.at[k, q, 2]

        @pl.when(has_left & has_right)
        def _():
            wait_for(rims.at[k, q], arrival)

        @pl.when(jnp.logical_not(has_left & has_right))
        def _():
            wait_for(rims.at[k, q, 0], arrival)

    def wait_for(whole, sem):
        pltpu.make_async_copy(whole, whole, sem).wait()

    send_cs = pltpu.make_async_remote_copy(
        src_ref=cond.at[0, LA - 1], dst_ref=cs_low, send_sem=cond_send.at[0],
        recv_sem=cond_recv.at[0], device_id=(up, c), device_id_type=MESH)
    send_cc = pltpu.make_async_remote_copy(
        src_ref=cc_out, dst_ref=cc_low, send_sem=cond_send.at[1],
        recv_sem=cond_recv.at[1], device_id=(s, right), device_id_type=MESH)

    pl.semaphore_wait(barrier, len(greeted) + jnp.where(has_up & has_down, 2, 1))

    def start_up(copies):
        @pl.when(has_up)
        def _():
            for copy in copies():
                copy.start()

    def start_down(copies):
        @pl.when(has_down)
        def _():
            for copy in copies():
                copy.start()

    start_up(lambda: [to_up(0, 0)])
    start_down(lambda: [to_down(0, q) for q in range(RHS)])

    @pl.when(s == 0)
    def _():
        halo_low[...] = jnp.zeros_like(halo_low)
        cs_low[...] = jnp.zeros_like(cs_low)

    @pl.when(s == SLABS - 1)
    def _():
        halo_up[...] = jnp.zeros_like(halo_up)

    @pl.when(c == 0)
    def _():
        rims[:, :, 0] = jnp.zeros((ITERS, RHS, LA, 1, NC), F32)
        cc_low[...] = jnp.zeros_like(cc_low)

    @pl.when(c == CROSSES - 1)
    def _():
        rims[:, :, 1] = jnp.zeros((ITERS, RHS, LA, 1, NC), F32)

    row = lax.broadcasted_iota(jnp.int32, (8, NC), 0)
    lane = lax.broadcasted_iota(jnp.int32, (8, NC), 1)
    first_row, last_row, last_lane = row == 0, row == 7, lane == NC - 1

    def conduct(a):
        ends_slab = (s == SLABS - 1) & (a == LA - 1)
        for j in range(TILES):
            at = pl.ds(8 * j, 8)
            pressure = cap[a, at, :]
            film = 0.4 / (pressure * pressure)
            for k in range(3):
                radius = cond[k, a, at, :]
                squared = radius * radius
                value = squared * jnp.where(wet[k, a, at, :] == 1, squared, film)
                if k == 0:
                    value = jnp.where(ends_slab, 0.0, value)
                if k == 1 and j == TILES - 1:
                    value = jnp.where(last_row & (c == CROSSES - 1), 0.0, value)
                    cc_out[a] = value[7:8, :]
                if k == 2:
                    value = jnp.where(last_lane, 0.0, value)
                cond[k, a, at, :] = value

    for copy in chunk_copies(0):
        copy.wait()
    conduct(LA - 1)
    start_up(lambda: [send_cs] + [to_up(0, q) for q in range(1, RHS)])
    token[...] = jnp.zeros_like(token)
    load_b.wait()

    def pack(a, carry):
        for q in range(RHS):
            edge_low[0, q, a] = v0[q, a, 0:1, :]
            edge_up[0, q, a] = v0[q, a, LB - 1 : LB, :]
        return carry

    lax.fori_loop(0, LA, pack, 0)
    for q in range(RHS):
        to_sides(0, q)
    conduct(LA - 2)

    def chunk(i, carry):
        for copy in chunk_copies(i):
            copy.wait()
        conduct(LA - 1 - 2 * i)
        conduct(LA - 2 - 2 * i)
        return carry

    lax.fori_loop(1, CHUNKS, chunk, 0)

    @pl.when(has_right)
    def _():
        send_cc.start()

    load_sto.wait()
    dots_ref[...] = jnp.zeros_like(dots_ref)

    def stages(k):
        v, w = vectors[k], vectors[k + 1]
        last = k + 1 == ITERS
        places = ((1, 2, 0), (3, 4), (5,))[k]

        def layer(q, a, below, above, dots):
            here = v[q, a, 0:8, :]
            here_up = pltpu.roll(here, 7, 0)
            passed = jnp.zeros((8, NC), F32)
            for j in range(TILES):
                at = pl.ds(8 * j, 8)
                if j + 1 < TILES:
                    after = v[q, a, 8 * j + 8 : 8 * j + 16, :]
                    after_up = pltpu.roll(after, 7, 0)
                else:
                    after = after_up = here
                flux_cross = cond[1, a, at, :] * (jnp.where(last_row, after_up, here_up) - here)
                arrived = pltpu.roll(flux_cross, 1, 0)
                flux_depth = cond[2, a, at, :] * (pltpu.roll(here, NC - 1, 1) - here)
                image = sto[a, at, :] * here
                if below:
                    image = image + flux[at, :]
                if above:
                    flux_slab = cond[0, a, at, :] * (v[q, a + 1, at, :] - here)
                    image = image - flux_slab
                    flux[at, :] = flux_slab
                image = image - flux_cross + jnp.where(first_row, passed, arrived)
                image = image - flux_depth + pltpu.roll(flux_depth, 1, 1)
                w[q, a, at, :] = image
                products = [here * image]
                if k + 1 < ITERS:
                    products.append(image * image)
                if k == 0:
                    products.append(here * here)
                dots = tuple(dot + fold(product) for dot, product in zip(dots, products))
                passed, here, here_up = arrived, after, after_up
            return dots

        def interior(q, unused):
            dots = (jnp.zeros((8, 128), F32),) * len(places)
            dots = layer(q, 0, False, True, dots)
            dots = lax.fori_loop(
                1, LA - 1, lambda a, carry: layer(q, a, True, True, carry), dots)
            dots = layer(q, LA - 1, True, False, dots)
            for place, dot in zip(places, dots):
                dots_ref[q, place] = dot
            return unused

        def rim_first(q, a, line):
            low = edge_low[k, q, a]
            enters = cc_low[a] * (low - rims[k, q, 0, a])
            old = w[q, a, 0:1, :]
            new = old + enters
            w[q, a, 0:1, :] = new
            if last:
                return (line[0] + fold(low * enters),)
            edge_low[k + 1, q, a] = new
            return line[0] + fold(low * enters), line[1] + fold(enters * (old + new))

        def rim_last(q, a, line):
            high = edge_up[k, q, a]
            leaves = cc_out[a] * (rims[k, q, 1, a] - high)
            old = w[q, a, LB - 1 : LB, :]
            new = old - leaves
            w[q, a, LB - 1 : LB, :] = new
            if last:
                return (line[0] - fold(high * leaves),)
            edge_up[k + 1, q, a] = new
            return line[0] - fold(high * leaves), line[1] - fold(leaves * (old + new))

        def only_first(q, there, wait):
            if k == 0:
                @pl.when((q == 0) & there)
                def _():
                    wait()

        def both_rims(q, a, line):
            return rim_last(q, a, rim_first(q, a, line))

        def no_dots():
            return (
                (jnp.zeros((8, 128), F32),) * len(places),
                (jnp.zeros((1, 128), F32),) * min(2, len(places)),
            )

        def add_dots(q, dots, line):
            for i, (place, dot) in enumerate(zip(places, dots)):
                dots_ref[q, place] = dots_ref[q, place] + dot
                if i < len(line):
                    dots_ref[q, place, 0:1, :] = dots_ref[q, place, 0:1, :] + line[i]

        def face(q, a, enters, energy):
            dots = (jnp.zeros((8, 128), F32),) * min(2, len(places))
            for j in range(TILES):
                at = pl.ds(8 * j, 8)
                flux_in = enters(at)
                old = w[q, a, at, :]
                new = old + flux_in
                w[q, a, at, :] = new
                dots = (dots[0] + fold(energy(at, flux_in)),) + (
                    () if last else (dots[1] + fold(flux_in * (old + new)),)
                )
                if not last and j == 0:
                    edge_low[k + 1, q, a] = new[0:1, :]
                if not last and j == TILES - 1:
                    edge_up[k + 1, q, a] = new[7:8, :]
            return dots

        def top(q):
            @pl.when(has_up)
            def _():
                to_down(k, q).wait_recv()

            a = LA - 1
            dots = face(
                q, a,
                lambda at: cond[0, a, at, :] * (v[q, a, at, :] - halo_up[k, q, at, :]),
                lambda at, flux_in: flux_in * (
                    v[q, a, at, :] - halo_up[k, q, at, :] if last else v[q, a, at, :]))
            if not last:
                start_up(lambda: [to_up(k + 1, q)])
            add_dots(q, dots, ())

        def bottom(q):
            @pl.when(has_down)
            def _():
                to_up(k, q).wait_recv()

            only_first(q, has_down, lambda: send_cs.wait_recv())
            dots = face(
                q, 0,
                lambda at: cs_low[at, :] * (v[q, 0, at, :] - halo_low[k, q, at, :]),
                lambda at, flux_in: flux_in * v[q, 0, at, :])
            start_down(lambda: [to_down(k + 1, q)])
            add_dots(q, dots, ())

        def border(q, unused):
            wait_sides(k, q)
            only_first(q, has_left, lambda: send_cc.wait_recv())
            line = lax.fori_loop(
                0, LA, lambda a, carry: both_rims(q, a, carry), no_dots()[1])
            add_dots(q, no_dots()[0], line)
            if last:
                top(q)
                return unused

            @pl.when(core == 0)
            def _():
                bottom(q)
                top(q)

            @pl.when(core == 1)
            def _():
                top(q)
                bottom(q)

            to_sides(k + 1, q)
            return unused

        return interior, border

    def step(index, group):
        for i, peer in enumerate(group):
            pltpu.make_async_remote_copy(
                src_ref=token, dst_ref=met.at[index, i], send_sem=meet_send.at[index],
                recv_sem=meet_recv.at[index], device_id=peer, device_id_type=MESH).start()

    step(0, along_z)
    interior, border = stages(0)
    lax.fori_loop(0, RHS, interior, 0)
    wait_for(met.at[0], meet_recv.at[0])
    step(1, along_y)
    for k in range(1, ITERS):
        next_interior, next_border = stages(k)

        def both(q, unused, border=border, interior=next_interior):
            border(q, unused)
            return interior(q, unused)

        lax.fori_loop(0, RHS, both, 0)
        border = next_border
        if k == 1:
            wait_for(met.at[1], meet_recv.at[1])
            step(2, along_x)
        else:
            wait_for(met.at[2], meet_recv.at[2])

    def sample_products(q, unused):
        def line(a, sums):
            for j in range(1, TILES - 1):
                at = pl.ds(8 * j, 8)
                t = [vector[q, a, at, :] for vector in vectors]
                sums = tuple(
                    total + fold(t[i] * t[l]) for total, (i, l) in zip(sums, PAIRS))
            return sums

        sums = lax.fori_loop(2, LA - 2, line, (jnp.zeros((8, 128), F32),) * len(PAIRS))
        for place, total in enumerate(sums):
            dots_ref[q, MOMENTS + place] = total
        return unused

    lax.fori_loop(0, RHS, sample_products, 0)

    rows = lax.broadcasted_iota(jnp.int32, (8, 128), 0)
    lanes = lax.broadcasted_iota(jnp.int32, (8, 128), 1)

    def lane_sums(tiles, target):
        stacked = jnp.concatenate(
            [jnp.sum(tile, axis=0, keepdims=True) for tile in tiles], axis=0)
        spread = jnp.broadcast_to(jnp.sum(stacked, axis=1, keepdims=True), (8, 128))
        return jnp.where(lanes == target, spread, 0.0)

    early = jnp.zeros((8, 128), F32)
    for q in range(RHS):
        tiles = [dots_ref[q, j] for j in range(LANES) if j != MOMENTS - 1]
        tiles.append(jnp.zeros((8, 128), F32))
        early = early + lane_sums(tiles[:8], LANES * q + rows + jnp.where(rows >= 5, 1, 0))
        early = early + lane_sums(tiles[8:], LANES * q + rows + 9)
    early_sum[...] = early

    lax.fori_loop(0, RHS, border, 0)

    late = [dots_ref[min(q, RHS - 1), MOMENTS - 1] for q in range(8)]
    packed = early_sum[...] + jnp.where(
        rows < RHS, lane_sums(late, LANES * rows + MOMENTS - 1), 0.0)
    own = jnp.sum(packed, axis=0, keepdims=True)

    own_place = s * CROSSES + c
    sent[...] = own
    for dy, dz, dx, other in OFFSETS:
        at_core = 1 - core if other else core
        slab = lax.rem(row_y + dy, 4) * 8 + lax.rem(col_z + dz, 4) * 2 + at_core
        pltpu.make_async_remote_copy(
            src_ref=sent, dst_ref=got.at[own_place], send_sem=sum_send.at[0],
            recv_sem=sum_recv.at[0], device_id=(slab, lax.rem(c + dx, 4)),
            device_id_type=MESH).start()
    got[own_place] = own

    def complete(q, unused):
        @pl.when(has_down)
        def _():
            to_up(ITERS - 1, q).wait_recv()

        for j in range(TILES):
            at = pl.ds(8 * j, 8)
            v3[q, 0, at, :] = v3[q, 0, at, :] + cs_low[at, :] * (
                v2[q, 0, at, :] - halo_low[ITERS - 1, q, at, :])
        return unused

    lax.fori_loop(0, RHS, complete, 0)

    @pl.when(has_down)
    def _():
        wait_for(halo_up, halo_send.at[0])

    @pl.when(has_up)
    def _():
        wait_for(halo_low, halo_send.at[1])
        send_cs.wait_send()

    @pl.when(has_left)
    def _():
        wait_for(edge_low, halo_send.at[2])

    @pl.when(has_right)
    def _():
        wait_for(edge_up, halo_send.at[3])
        send_cc.wait_send()

    for index in range(3):
        wait_for(met.at[index], meet_send.at[index])

    others = got.at[pl.ds(0, len(OFFSETS))]
    wait_for(others, sum_recv.at[0])
    terms = [got[pl.ds(8 * i, 8), 0, :] for i in range((len(OFFSETS) + 1) // 8)]
    while len(terms) > 1:
        terms = [terms[i] + terms[i + 1] for i in range(0, len(terms), 2)]
    terms = [jnp.sum(terms[0], axis=0, keepdims=True)]
    own = terms[0]
    wait_for(others, sum_send.at[0])

    summed = jnp.broadcast_to(own, (8, 128))
    used = (lanes % LANES == 0) & (lanes < LANES * RHS)
    stand_in = (1.0, 1.0, 2.0, 6.0, 24.0, 120.0) + (1.0,) * len(PAIRS)
    m = [
        jnp.where(used, pltpu.roll(summed, 128 - j, 1) if j else summed, stand_in[j])
        for j in range(LANES)
    ]
    coefs, sound = scalars_of(m[:MOMENTS], m[MOMENTS:])
    sound = sound | ~used
    for i, coef in enumerate(coefs):
        for q in range(RHS):
            mine = jnp.where(lanes == LANES * q, coef, 0.0)
            coef_ref[q, i] = jnp.broadcast_to(jnp.sum(mine, axis=1, keepdims=True), (8, 128))
    sound_ref[...] = jnp.min(jnp.where(sound, 1, 0), axis=1, keepdims=True)[0:1, :]


def combine_kernel(coef, v0, v1, v2, v3, x_hbm, r_hbm, x, r, sem):
    part = 2
    copies = []
    for q in range(RHS):
        x0, x1, x2, d1, d2, d3 = (
            jnp.concatenate([coef[q, i]] * (NC // 128), axis=1) for i in range(6))

        def layer(a, carry):
            for j in range(TILES):
                at = pl.ds(8 * j, 8)
                t0, t1, t2, t3 = (v[q, a, at, :] for v in (v0, v1, v2, v3))
                x[q, a, at, :] = x0 * t0 + x1 * t1 + x2 * t2
                r[q, a, at, :] = t0 + d1 * t1 + d2 * t2 + d3 * t3
            return carry

        for h in range(LA // part):
            lax.fori_loop(h * part, (h + 1) * part, layer, 0)
            layers = pl.ds(h * part, part)
            for index, (source, target) in enumerate(((x, x_hbm), (r, r_hbm))):
                copy = pltpu.make_async_copy(
                    source.at[q, layers], target.at[q, layers], sem.at[q, h, index])
                copy.start()
                copies.append(copy)
    for copy in copies:
        copy.wait()


def per_device(pressure_drive, throat_radius, wet_flag, cap_pressure, storage):
    field = (RHS, LA, LB, NC)
    vmem = functools.partial(pltpu.VMEM, dtype=F32)
    in_vmem = pl.BlockSpec(memory_space=pltpu.VMEM)
    anywhere = pl.BlockSpec(memory_space=pl.ANY)
    *vectors, coefs, sound = pl.pallas_call(
        powers_kernel,
        out_shape=[pltpu.VMEM(field, F32)] * 4
        + [
            pltpu.VMEM((RHS, 6, 8, 128), F32),
            jax.ShapeDtypeStruct((1, 1), jnp.int32),
        ],
        in_specs=[anywhere] * 5,
        out_specs=[in_vmem] * 6,
        scratch_shapes=[
            vmem(field),
            pltpu.VMEM(field, jnp.int32),
            vmem((LA, LB, NC)),
            vmem((LA, LB, NC)),
            vmem((LB, NC)),
            vmem((LA, 1, NC)),
            vmem((LA, 1, NC)),
            vmem((ITERS, RHS, LB, NC)),
            vmem((ITERS, RHS, LB, NC)),
            vmem((ITERS, RHS, LA, 1, NC)),
            vmem((ITERS, RHS, LA, 1, NC)),
            vmem((ITERS, RHS, 2, LA, 1, NC)),
            vmem((LB, NC)),
            vmem((RHS, LANES, 8, 128)),
            vmem((8, 128)),
            vmem((1, 128)),
            vmem((3, 3, 1, 128)),
            vmem((1, 128)),
            vmem((128, 1, 128)),
            pltpu.SemaphoreType.DMA((2,)),
            pltpu.SemaphoreType.DMA((CHUNKS, 3)),
            pltpu.SemaphoreType.DMA((4,)),
            pltpu.SemaphoreType.DMA((ITERS, RHS, 3)),
            pltpu.SemaphoreType.DMA((2,)),
            pltpu.SemaphoreType.DMA((2,)),
            pltpu.SemaphoreType.DMA((3,)),
            pltpu.SemaphoreType.DMA((3,)),
            pltpu.SemaphoreType.DMA((1,)),
            pltpu.SemaphoreType.DMA((1,)),
        ],
        compiler_params=pltpu.CompilerParams(
            collective_id=0, has_side_effects=True, vmem_limit_bytes=34 << 20
        ),
        name="powers",
    )(pressure_drive, throat_radius, wet_flag, cap_pressure, storage)
    fast = pl.pallas_call(
        combine_kernel,
        out_shape=[jax.ShapeDtypeStruct(field, F32)] * 2,
        in_specs=[in_vmem] * 5,
        out_specs=[anywhere] * 2,
        scratch_shapes=[vmem(field), vmem(field), pltpu.SemaphoreType.DMA((RHS, 4, 2))],
        compiler_params=pltpu.CompilerParams(vmem_limit_bytes=24 << 20),
        name="combine",
    )(coefs, *vectors)
    return lax.cond(
        sound[0, 0] == 1,
        lambda: tuple(fast),
        lambda: plain_iteration(pressure_drive, throat_radius, wet_flag, cap_pressure, storage),
    )


def solution(mesh):
    in_specs = (
        P(None, "slab", "cross", None),
        P(None, "slab", "cross", None),
        P(None, "slab", "cross", None),
        P("slab", "cross", None),
        P("slab", "cross", None),
    )
    out_specs = (P(None, "slab", "cross", None), P(None, "slab", "cross", None))
    return jax.shard_map(
        per_device, mesh=mesh, in_specs=in_specs, out_specs=out_specs, check_vma=False
    )
```
